32 devices in a mesh: dp: 4 (over y, x), seq: 8 (over z, core).
Axes of the slice: x: 2, y: 2, z: 4, core: 2. Of those that a mesh axis runs over, the one named last changes fastest.
Arguments:
- tokens: bfloat16 [32768, 768], P(('dp', 'seq')), may hold values from -6 to 6
- w_qkv: bfloat16 [768, 2304], P(('dp', 'seq')), may hold values from -0.21875 to 0.21875
- w_out: bfloat16 [768, 768], P(('dp', 'seq')), may hold values from -0.625 to 0.625
- w_up: bfloat16 [768, 3072], P(('dp', 'seq')), may hold values from -0.21875 to 0.21875
- w_down: bfloat16 [3072, 768], P(('dp', 'seq')), may hold values from -0.109375 to 0.109375
- vectors: bfloat16 [8, 768], P(None, ('dp', 'seq'))
- up_bias: bfloat16 [3072], P(('dp', 'seq')), may hold values from -3 to 3
- cluster_route: int32 [4, 12, 8192], P('dp'), may hold values from 0 to 1023, as said below
- upstream: bfloat16 [32768, 768], P(('dp', 'seq')), may hold values from -6 to 6
Outputs:
- layer_out: bfloat16 [32768, 768], P(('dp', 'seq'))
- grad_tokens: bfloat16 [32768, 768], P(('dp', 'seq'))
- grad_qkv: float32 [768, 2304], P(('dp', 'seq'))
- grad_out: float32 [768, 768], P(('dp', 'seq'))
- grad_up: float32 [768, 3072], P(('dp', 'seq'))
- grad_down: float32 [3072, 768], P(('dp', 'seq'))
- grad_vectors: float32 [8, 768], P(None, ('dp', 'seq'))
- grad_up_bias: float32 [3072], P(('dp', 'seq'))
The draws below stay inside these ranges and needn't reach their ends.
Inputs may be any that keep to these rules, and one draw needn't show every extreme that they name: Each block of 1024 rows holds, in order, 6 sequences of 128 rows and then 16 sequences of 16 rows; sequence number s is made of its rows in all 8 blocks of the group. For each group g, head h and block k, the entries cluster_route[g, h, k * 1024 : (k + 1) * 1024] are a permutation of 0 to 1023; entry k * 1024 + j * 128 + i names the row, within block k, of the token in slot j * 1024 + i * 8 + k. All tokens of one cluster belong to one sequence.
All inputs are finite; a program needn't handle non-finite values.
Results may differ from the reference program's by a relative error of at most 0.014.
Values may be sent and summed in bfloat16 or wider, within the bound.
A program may use at most 192 MiB of HBM per device.

```python
import jax
import jax.numpy as jnp
from jax import lax

D = 768
H = 12
FF = 3072
DH = 64
CL = 128
LONG_ROWS = 128
SHORT_ROWS = 16
NLONG = 6
TOK_DEV = 1024
SHARE = 16
GROUP = 8192
TOKENS = 32768
N_DP = 4


def draw_vectors(key, part):
    key = jax.random.fold_in(key, 11)
    gaussian = jax.random.normal(key, (8, D), jnp.float32)
    row_index = jnp.arange(8)[:, None]
    is_gain = (row_index == 4) | (row_index == 6)
    return jnp.where(is_gain, 1.0 + 0.15 * gaussian, 0.3 * gaussian).astype(jnp.bfloat16)


def draw_cluster_route(key, part):
    key = jax.random.fold_in(key, 23)
    group_count = TOKENS // GROUP
    block_count = GROUP // TOK_DEV
    rows = jnp.arange(TOK_DEV, dtype=jnp.int32)
    long_end = NLONG * LONG_ROWS
    owner = jnp.where(rows < long_end, rows // LONG_ROWS, NLONG + (rows - long_end) // SHORT_ROWS).astype(jnp.int32)

    def one_head(head_key):
        order_key, rows_key = jax.random.split(head_key)
        placing = jax.random.permutation(order_key, TOK_DEV // SHARE)

        def one_block(block_key):
            noise = jax.random.permutation(block_key, TOK_DEV).astype(jnp.int32)
            within = jnp.argsort(owner * TOK_DEV + noise).astype(jnp.int32)
            return within.reshape(TOK_DEV // SHARE, SHARE)[placing].reshape(TOK_DEV)
        return jax.vmap(one_block)(jax.random.split(rows_key, block_count)).reshape(GROUP)
    head_keys = jax.random.split(key, group_count * H)
    return jax.vmap(one_head)(head_keys).reshape(group_count, H, GROUP).astype(jnp.int32)


def spiked(array, key, source, target, blocks, factor):
    def block_of(dim):
        return (jnp.arange(array.shape[dim]) // (array.shape[dim] // blocks)).reshape((-1,) + (1,) * (array.ndim - 1 - dim))

    first = jax.random.permutation(key, blocks)[block_of(target)]
    far = (block_of(target) + blocks // 2) % blocks
    return jnp.where((block_of(source) == first) | (block_of(source) == far), factor * array, array)


def level_of(rng, dims, pieces, least, high):
    level = 1.0
    for position, shards_of in pieces:
        heights = jax.random.uniform(jax.random.fold_in(jax.random.fold_in(rng, 6), position), (shards_of,), jnp.float32, least / len(pieces), high / len(pieces))
        level = level * jnp.repeat(jnp.exp(heights), dims[position] // shards_of).reshape((-1,) + (1,) * (len(dims) - 1 - position))
    return level


def bell_draw(rng, dims, scale, reach, cuts=(), kind=jnp.bfloat16):
    level = level_of(rng, dims, cuts, -0.22, 0.18) if cuts else 1.0
    result = jax.random.normal(rng, dims, jnp.float32) * scale * level
    return jnp.minimum(jnp.maximum(result, -reach), reach).astype(kind)


def noise_with(key, shape, width, most, cuts, heavy, held_as=jnp.bfloat16):
    result = width * jax.random.normal(key, shape, jnp.float32)
    if cuts:
        result = result * level_of(key, shape, cuts, -0.22, 0.18)
    return jnp.clip(spiked(result, jax.random.fold_in(key, 3), *heavy), -most, most).astype(held_as)


def setup_inputs(seed: int = 0) -> dict:
    splits = jax.random.split(jax.random.key(seed), 10)
    return {
        "tokens": noise_with(splits[0], (TOKENS, D), 1.0, 6.0, ((0, 32),), (0, 1, 32, 2.75)),
        "w_qkv": bell_draw(splits[1], (D, 3 * D), D ** -0.5, 0.21875, ((0, 32),)),
        "w_out": bell_draw(splits[2], (D, D), (D // 8) ** -0.5, 0.625, ((0, 32),)),
        "w_up": bell_draw(splits[3], (D, FF), D ** -0.5, 0.21875, ((0, 32),)),
        "w_down": bell_draw(splits[4], (FF, D), FF ** -0.5, 0.109375, ((0, 32),)),
        "vectors": draw_vectors(jax.random.fold_in(splits[9], 71), 0),
        "up_bias": bell_draw(splits[6], (FF,), 0.5, 3.0, ((0, 32),)),
        "cluster_route": draw_cluster_route(jax.random.fold_in(splits[9], 71), 0),
        "upstream": noise_with(splits[8], (TOKENS, D), 1.0, 6.0, ((0, 32),), (0, 1, 32, 2.75)),
    }


precise = lax.Precision.HIGHEST

@jax.custom_vjp
def low(v):
    return lax.optimization_barrier(v.astype(jnp.bfloat16)).astype(jnp.float32)

@jax.custom_vjp
def low_back(v):
    return v

def low_keep(v):
    return (low(v), None)

def low_pass(kept, grad):
    return (grad,)

def back_keep(v):
    return (v, None)

def back_low(kept, grad):
    return (low(grad),)
low.defvjp(low_keep, low_pass)
low_back.defvjp(back_keep, back_low)

def layer_norm(resid, norm_gain, norm_shift):
    average = lax.optimization_barrier(jnp.mean(resid, axis=-1, keepdims=True))
    centred = resid - average
    spread = lax.optimization_barrier(jnp.mean(centred * centred, axis=-1, keepdims=True))
    return centred * lax.rsqrt(spread + 1e-06) * norm_gain + norm_shift

def slot_order(route_rows):
    blocks = GROUP // TOK_DEV
    portion = TOK_DEV // blocks
    arranged = route_rows.reshape(H, blocks, blocks, portion)
    offset = (jnp.arange(blocks, dtype=jnp.int32) * TOK_DEV)[None, :, None, None]
    return jnp.transpose(arranged + offset, (0, 2, 3, 1)).reshape(H, GROUP).astype(jnp.int32)

def attend(packed):
    queries, key_rows, values, slot_tokens = packed
    slot_index = slot_tokens.T[:, :, None]
    clusters = GROUP // CL
    query_c = jnp.take_along_axis(queries, slot_index, axis=0).reshape(clusters, CL, H, DH)
    key_c = jnp.take_along_axis(key_rows, slot_index, axis=0).reshape(clusters, CL, H, DH)
    value_c = jnp.take_along_axis(values, slot_index, axis=0).reshape(clusters, CL, H, DH)
    scores = jnp.einsum('cahe,cbhe->hcab', query_c, key_c, precision=precise) * DH ** (-0.5)
    scores = low_back(scores)
    row_peak = lax.optimization_barrier(jnp.max(scores, axis=-1, keepdims=True))
    exponent = jnp.exp(scores - row_peak)
    soft_weights = low(exponent / lax.optimization_barrier(jnp.sum(exponent, axis=-1, keepdims=True)))
    heads_slot = jnp.einsum('hcab,cbhe->cahe', soft_weights, value_c, precision=precise)
    heads_slot = low(low_back(heads_slot.reshape(GROUP, H, DH)))
    head_ids = jnp.arange(H, dtype=jnp.int32)[:, None]
    ranks = jnp.broadcast_to(jnp.arange(GROUP, dtype=jnp.int32)[None, :], (H, GROUP))
    inverse = jnp.zeros((H, GROUP), jnp.int32).at[head_ids, slot_tokens].set(ranks)
    return jnp.take_along_axis(heads_slot, inverse.T[:, :, None], axis=0)

def forward(tokens, w_qkv, w_out, w_up, w_down, vectors, up_bias, slot_tokens):
    projected = jnp.dot(tokens, w_qkv, precision=precise)
    shifts = jnp.concatenate([vectors[0], jnp.zeros_like(vectors[0]), vectors[1]])
    projected = low(low_back(projected + shifts))
    split_qkv = projected.reshape(N_DP, GROUP, 3, H, DH)
    heads_out = lax.map(jax.checkpoint(attend), (split_qkv[:, :, 0], split_qkv[:, :, 1], split_qkv[:, :, 2], slot_tokens))
    mixed_heads = heads_out.reshape(TOKENS, D)
    attention = low_back(jnp.dot(mixed_heads, w_out, precision=precise) + vectors[2])
    first_norm = layer_norm(tokens + attention, vectors[4], vectors[5])
    widened = low_back(jnp.dot(low(first_norm), w_up, precision=precise) + up_bias)
    activated = low(jax.nn.gelu(widened, approximate=False))
    narrowed = low_back(jnp.dot(activated, w_down, precision=precise) + vectors[3])
    return layer_norm(first_norm + narrowed, vectors[6], vectors[7])

def reference(tokens, w_qkv, w_out, w_up, w_down, vectors, up_bias, cluster_route, upstream):
    slot_tokens = jax.vmap(slot_order)(cluster_route)

    def closed(tokens_f, qkv_f, out_f, up_f, down_f, vectors_f, bias_f):
        return forward(tokens_f, qkv_f, out_f, up_f, down_f, vectors_f, bias_f, slot_tokens)
    floats = (tokens.astype(jnp.float32), w_qkv.astype(jnp.float32), w_out.astype(jnp.float32), w_up.astype(jnp.float32), w_down.astype(jnp.float32), vectors.astype(jnp.float32), up_bias.astype(jnp.float32))
    output, pullback = jax.vjp(closed, *floats)
    gradients = pullback(upstream.astype(jnp.float32))
    return (output.astype(jnp.bfloat16), gradients[0].astype(jnp.bfloat16), gradients[1], gradients[2], gradients[3], gradients[4], gradients[5], gradients[6])
```

```python
import functools

import jax
import jax.numpy as jnp
from jax import lax
from jax.experimental import pallas as pl
from jax.experimental.pallas import tpu as pltpu
from jax.sharding import PartitionSpec as P

H = 12
CL = 128


epsilon = 1e-06


def normalize(resid, norm_gain, norm_shift):
    average = jnp.mean(resid, axis=-1, keepdims=True)
    centred = resid - average
    spread = jnp.mean(centred * centred, axis=-1, keepdims=True)
    scaled = lax.rsqrt(spread + epsilon)
    normed = centred * scaled
    return (normed * norm_gain + norm_shift, normed, scaled)


def norm_back(grad_output, normed, scaled, norm_gain):
    grad_norm = grad_output * norm_gain
    first_term = jnp.mean(grad_norm, axis=-1, keepdims=True)
    second_term = jnp.mean(grad_norm * normed, axis=-1, keepdims=True)
    return scaled * (grad_norm - first_term - normed * second_term)


def exact_gelu(value):
    return jax.nn.gelu(value, approximate=False)


def order_table(sending):
    heads, rows_here = sending.shape
    columns = jnp.arange(rows_here, dtype=jnp.int32)[None, None, :]
    return (sending[:, :, None] == columns).astype(jnp.bfloat16)


def to_slots(source_rows, table):
    moved = jnp.einsum("hrs,skhe->rkhe", table, source_rows, preferred_element_type=jnp.float32)
    return moved.astype(jnp.bfloat16)


def to_tokens(source_rows, table):
    moved = jnp.einsum("hrs,rkhe->skhe", table, source_rows, preferred_element_type=jnp.float32)
    return moved.astype(jnp.bfloat16)


def cluster_scores(query_c, key_c, scale_factor):
    return (
        jnp.einsum("cahe,cbhe->hcab", query_c, key_c, preferred_element_type=jnp.float32)
        * scale_factor
    )


def shards(tokens, w_qkv, w_out, w_up, w_down, vectors, up_bias, cluster_route, upstream):
    lane_count = lax.axis_size("seq")
    lane_index = lax.axis_index("seq")
    wide_qkv, wide_out, wide_up, wide_down, wide_vectors, wide_bias = (
        lax.all_gather(w_qkv, ("dp", "seq"), axis=0, tiled=True),
        lax.all_gather(w_out, ("dp", "seq"), axis=0, tiled=True),
        lax.all_gather(w_up, ("dp", "seq"), axis=0, tiled=True),
        lax.all_gather(w_down, ("dp", "seq"), axis=0, tiled=True),
        lax.all_gather(vectors, ("dp", "seq"), axis=1, tiled=True),
        lax.all_gather(up_bias, ("dp", "seq"), axis=0, tiled=True),
    )
    rows_here = tokens.shape[0]
    model_width = tokens.shape[1]
    head_size = model_width // H
    portion = rows_here // lane_count
    clusters = rows_here // CL
    scale_factor = head_size ** (-0.5)
    vector_rows = wide_vectors.astype(jnp.float32)
    route_rows = cluster_route[0]
    by_target = lax.dynamic_slice_in_dim(route_rows, lane_index * rows_here, rows_here, 1)
    sending = jnp.swapaxes(by_target.reshape(H, lane_count, portion), 1, 2).reshape(H, rows_here)
    table = order_table(sending)
    projected = jnp.dot(tokens, wide_qkv, preferred_element_type=jnp.float32)
    shifts = jnp.concatenate(
        [vector_rows[0], jnp.zeros((model_width,), jnp.float32), vector_rows[1]]
    )
    projected = (projected + shifts).astype(jnp.bfloat16).reshape(rows_here, 3, H, head_size)
    outgoing = to_slots(projected, table)
    arrived = lax.all_to_all(
        outgoing.reshape(portion, lane_count, 3 * model_width),
        "seq",
        split_axis=1,
        concat_axis=1,
        tiled=True,
    )
    slot_qkv = arrived.reshape(clusters, CL, 3, H, head_size)
    query_c = slot_qkv[:, :, 0]
    key_c = slot_qkv[:, :, 1]
    value_c = slot_qkv[:, :, 2]
    scores = cluster_scores(query_c, key_c, scale_factor)
    row_peak = jnp.max(scores, axis=-1, keepdims=True)
    exponent = jnp.exp(scores - row_peak)
    row_total = jnp.sum(exponent, axis=-1, keepdims=True)
    soft_weights = exponent / row_total
    log_total = row_peak + jnp.log(row_total)
    heads_slot = jnp.einsum(
        "hcab,cbhe->cahe",
        soft_weights.astype(jnp.bfloat16),
        value_c,
        preferred_element_type=jnp.float32,
    ).astype(jnp.bfloat16)
    returned = lax.all_to_all(
        heads_slot.reshape(portion, lane_count, model_width),
        "seq",
        split_axis=1,
        concat_axis=1,
        tiled=True,
    )
    mixed_heads = to_tokens(returned.reshape(rows_here, 1, H, head_size), table).reshape(
        rows_here, model_width
    )
    attention = jnp.dot(mixed_heads, wide_out, preferred_element_type=jnp.float32) + vector_rows[2]
    first_norm, first_normed, first_scaled = normalize(
        tokens.astype(jnp.float32) + attention, vector_rows[4], vector_rows[5]
    )
    first_low = first_norm.astype(jnp.bfloat16)
    widened = jnp.dot(first_low, wide_up, preferred_element_type=jnp.float32) + wide_bias.astype(
        jnp.float32
    )
    activated, gelu_pull = jax.vjp(exact_gelu, widened)
    activated_low = activated.astype(jnp.bfloat16)
    narrowed = (
        jnp.dot(activated_low, wide_down, preferred_element_type=jnp.float32) + vector_rows[3]
    )
    output, second_normed, second_scaled = normalize(
        first_norm + narrowed, vector_rows[6], vector_rows[7]
    )
    back_qkv, back_out, back_up, back_down = (
        lax.all_gather(w_qkv, ("dp", "seq"), axis=0, tiled=True),
        lax.all_gather(w_out, ("dp", "seq"), axis=0, tiled=True),
        lax.all_gather(w_up, ("dp", "seq"), axis=0, tiled=True),
        lax.all_gather(w_down, ("dp", "seq"), axis=0, tiled=True),
    )
    grad_output = upstream.astype(jnp.float32)
    grad_gain_two = jnp.sum(grad_output * second_normed, axis=0)
    grad_shift_two = jnp.sum(grad_output, axis=0)
    grad_second = norm_back(grad_output, second_normed, second_scaled, vector_rows[6])
    grad_narrow = grad_second.astype(jnp.bfloat16)
    grad_down_w = jnp.einsum(
        "tf,td->fd", activated_low, grad_narrow, preferred_element_type=jnp.float32
    )
    grad_down_bias = jnp.sum(grad_narrow.astype(jnp.float32), axis=0)
    grad_active = jnp.einsum(
        "td,fd->tf", grad_narrow, back_down, preferred_element_type=jnp.float32
    )
    grad_wide = gelu_pull(grad_active)[0].astype(jnp.bfloat16)
    grad_up_w = jnp.einsum("td,tf->df", first_low, grad_wide, preferred_element_type=jnp.float32)
    grad_lift_bias = jnp.sum(grad_wide.astype(jnp.float32), axis=0)
    grad_first = grad_second + jnp.einsum(
        "tf,df->td", grad_wide, back_up, preferred_element_type=jnp.float32
    )
    grad_gain_one = jnp.sum(grad_first * first_normed, axis=0)
    grad_shift_one = jnp.sum(grad_first, axis=0)
    grad_resid = norm_back(grad_first, first_normed, first_scaled, vector_rows[4])
    grad_attn = grad_resid.astype(jnp.bfloat16)
    grad_out_w = jnp.einsum("td,te->de", mixed_heads, grad_attn, preferred_element_type=jnp.float32)
    grad_out_bias = jnp.sum(grad_attn.astype(jnp.float32), axis=0)
    grad_mixed = jnp.einsum(
        "te,de->td", grad_attn, back_out, preferred_element_type=jnp.float32
    ).astype(jnp.bfloat16)
    grad_sending = to_slots(grad_mixed.reshape(rows_here, 1, H, head_size), table)
    grad_slot = lax.all_to_all(
        grad_sending.reshape(portion, lane_count, model_width),
        "seq",
        split_axis=1,
        concat_axis=1,
        tiled=True,
    )
    grad_slot = grad_slot.reshape(clusters, CL, H, head_size)
    scores = cluster_scores(query_c, key_c, scale_factor)
    soft_weights = jnp.exp(scores - log_total)
    grad_soft = jnp.einsum(
        "cahe,cbhe->hcab", grad_slot, value_c, preferred_element_type=jnp.float32
    )
    inner_sum = jnp.sum(soft_weights * grad_soft, axis=-1, keepdims=True)
    grad_scores = (soft_weights * (grad_soft - inner_sum)).astype(jnp.bfloat16)
    grad_query = (
        jnp.einsum("hcab,cbhe->cahe", grad_scores, key_c, preferred_element_type=jnp.float32)
        * scale_factor
    )
    grad_key = (
        jnp.einsum("hcab,cahe->cbhe", grad_scores, query_c, preferred_element_type=jnp.float32)
        * scale_factor
    )
    grad_value = jnp.einsum(
        "hcab,cahe->cbhe",
        soft_weights.astype(jnp.bfloat16),
        grad_slot,
        preferred_element_type=jnp.float32,
    )
    grad_slots = jnp.stack([grad_query, grad_key, grad_value], axis=2).astype(jnp.bfloat16)
    came_back = lax.all_to_all(
        grad_slots.reshape(portion, lane_count, 3 * model_width),
        "seq",
        split_axis=1,
        concat_axis=1,
        tiled=True,
    )
    grad_proj = to_tokens(came_back.reshape(rows_here, 3, H, head_size), table).reshape(
        rows_here, 3 * model_width
    )
    grad_qkv_w = jnp.einsum("td,tf->df", tokens, grad_proj, preferred_element_type=jnp.float32)
    bias_sums = jnp.sum(grad_proj.astype(jnp.float32), axis=0).reshape(3, model_width)
    grad_tokens = (
        jnp.einsum("tf,df->td", grad_proj, back_qkv, preferred_element_type=jnp.float32)
        + grad_resid
    ).astype(jnp.bfloat16)
    grad_vector_rows = jnp.stack(
        [
            bias_sums[0],
            bias_sums[2],
            grad_out_bias,
            grad_down_bias,
            grad_gain_one,
            grad_shift_one,
            grad_gain_two,
            grad_shift_two,
        ]
    )
    shares = (
        lax.psum_scatter(grad_qkv_w, ("dp", "seq"), scatter_dimension=0, tiled=True),
        lax.psum_scatter(grad_out_w, ("dp", "seq"), scatter_dimension=0, tiled=True),
        lax.psum_scatter(grad_up_w, ("dp", "seq"), scatter_dimension=0, tiled=True),
        lax.psum_scatter(grad_down_w, ("dp", "seq"), scatter_dimension=0, tiled=True),
        lax.psum_scatter(grad_vector_rows, ("dp", "seq"), scatter_dimension=1, tiled=True),
        lax.psum_scatter(grad_lift_bias, ("dp", "seq"), scatter_dimension=0, tiled=True),
    )
    return (
        output.astype(jnp.bfloat16),
        grad_tokens,
        shares[0],
        shares[1],
        shares[2],
        shares[3],
        shares[4],
        shares[5],
    )


MESH = pl.DeviceIdType.MESH
NZ = 4
BLK = 128

class Links:
    def __init__(self, send_sems, recv_sems):
        self.send_sems, self.recv_sems, self.count, self.drains = send_sems, recv_sems, 0, []
        self.dp, self.sq = lax.axis_index("dp"), lax.axis_index("seq")
        self.x, self.y = lax.rem(self.dp, 2), self.dp // 2
        self.core, self.z = lax.rem(self.sq, 2), self.sq // 2
        self.sib = self.sq + 1 - 2 * self.core
        self.dp_x = self.dp + 1 - 2 * self.x
        self.dp_y = self.dp + 2 - 4 * self.y

    def new(self):
        self.count += 1
        return self.count - 1

    def copy(self, i, src, dst, dp, sq):
        return pltpu.make_async_remote_copy(
            src_ref=src, dst_ref=dst, send_sem=self.send_sems.at[i], recv_sem=self.recv_sems.at[i],
            device_id=(dp, sq), device_id_type=MESH)

    def enter(self, near=True, line=True):
        barrier = pltpu.get_barrier_semaphore()
        n = 0
        if near:
            for dp in (self.dp_x, self.dp_y):
                pl.semaphore_signal(barrier, inc=1, device_id=(dp, self.sq), device_id_type=MESH)
                n += 1
        if line:
            for j in range(1, 2 * NZ):
                pl.semaphore_signal(barrier, inc=1, device_id=(self.dp, lax.rem(self.sq + j, 2 * NZ)), device_id_type=MESH)
                n += 1
        pl.semaphore_wait(barrier, n)

    def drain(self):
        for d in self.drains:
            d()


def mult(v, m):
    return pl.multiple_of(v, m)


def gather(L, shard, full, half_buf, r, split):
    half = full.shape[1] // 2
    a, b = split
    big = 2 * r
    mine = pl.ds(mult(L.core * half, 128), half)
    other = pl.ds(mult((1 - L.core) * half, 128), half)
    cols_a = pl.ds(mult(L.core * half, 128), a)
    cols_b = pl.ds(mult(L.core * half + a, 128), b)
    chip = lambda z: pl.ds(mult((L.dp * NZ + z) * big, 16), big)
    quarter = lambda dp, n=1: pl.ds(mult(dp * NZ * big, 16), n * NZ * big)
    i0 = L.new()
    fr = [None] + [L.new() for _ in range(3)]
    fl = [None] + [L.new() for _ in range(3)]
    ax, by, ay, bx0, bx1, c0, c1, c2 = [L.new() for _ in range(8)]
    first = L.copy(i0, shard.at[:, other], half_buf, L.dp, L.sib)

    def right(d, z0):
        return L.copy(fr[d], full.at[chip(z0), mine], full.at[chip(z0), mine], L.dp, L.sq + 2)

    def left(d, z0):
        return L.copy(fl[d], full.at[chip(z0), mine], full.at[chip(z0), mine], L.dp, L.sq - 2)

    def send_line(d):
        @pl.when((L.z >= d - 1) & (L.z < NZ - 1))
        def _():
            right(d, L.z - d + 1).start()

        @pl.when((L.z <= NZ - d) & (L.z > 0))
        def _():
            left(d, L.z + d - 1).start()

    def drain_line(d):
        @pl.when((L.z >= d - 1) & (L.z < NZ - 1))
        def _():
            right(d, L.z - d + 1).wait_send()

        @pl.when((L.z <= NZ - d) & (L.z > 0))
        def _():
            left(d, L.z + d - 1).wait_send()

    def recv_line(d):
        @pl.when(L.z >= d)
        def _():
            right(d, L.z - d).wait_recv()

        @pl.when(L.z + d <= NZ - 1)
        def _():
            left(d, L.z + d).wait_recv()

    def same(i, rows, cols, dp, sq):
        ref = full.at[rows, cols]
        return L.copy(i, ref, ref, dp, sq)

    def s0():
        first.start()
        L.drains.append(first.wait_send)

    def s1():
        first.wait_recv()
        own, got = shard[:, mine], half_buf[...]

        @pl.when(L.core == 0)
        def _():
            full[chip(L.z), mine] = jnp.concatenate([own, got], axis=0)

        @pl.when(L.core == 1)
        def _():
            full[chip(L.z), mine] = jnp.concatenate([got, own], axis=0)
        send_line(1)
        L.drains.append(functools.partial(drain_line, 1))

    def s2():
        recv_line(1)
        send_line(2)
        L.drains.append(functools.partial(drain_line, 2))

    def s3():
        recv_line(2)
        send_line(3)
        L.drains.append(functools.partial(drain_line, 3))

    def go(cs):
        for c in cs:
            c.start()
            L.drains.append(c.wait_send)

    def s4():
        recv_line(3)
        q = quarter(L.dp)
        go([same(ax, q, cols_a, L.dp_x, L.sq), same(by, q, cols_b, L.dp_y, L.sq), same(c0, q, mine, L.dp, L.sib)])

    def s5():
        same(ax, quarter(L.dp_x), cols_a, L.dp_x, L.sq).wait_recv()
        go([same(ay, quarter(2 * L.y, 2), cols_a, L.dp_y, L.sq)])
        same(by, quarter(L.dp_y), cols_b, L.dp_y, L.sq).wait_recv()
        go([same(bx0, quarter(L.dp), cols_b, L.dp_x, L.sq), same(bx1, quarter(L.dp_y), cols_b, L.dp_x, L.sq)])

    def s6():
        same(bx0, quarter(L.dp_x), cols_b, L.dp_x, L.sq).wait_recv()
        go([same(c1, quarter(L.dp_x), mine, L.dp, L.sib)])
        same(ay, quarter(2 * (1 - L.y), 2), cols_a, L.dp_y, L.sq).wait_recv()
        same(bx1, quarter(3 - L.dp), cols_b, L.dp_x, L.sq).wait_recv()
        go([same(c2, quarter(2 * (1 - L.y), 2), mine, L.dp, L.sib)])

    def s7():
        same(c0, quarter(L.dp), other, L.dp, L.sib).wait_recv()
        same(c1, quarter(L.dp_x), other, L.dp, L.sib).wait_recv()
        same(c2, quarter(2 * (1 - L.y), 2), other, L.dp, L.sib).wait_recv()
    return [s0, s1, s2, s3, s4, s5, s6, s7]


def spread(L, src, dst, local_sem):
    ids = [None] + [L.new() for _ in range(2 * NZ - 1)]
    block = lambda s: pl.ds(mult(s * BLK, BLK), BLK)
    keep = pltpu.make_async_copy(src.at[block(L.sq)], dst.at[block(L.sq)], local_sem)

    def move(j, to, frm):
        return L.copy(ids[j], src.at[block(to)], dst.at[block(frm)], L.dp, to)

    def begin():
        keep.start()
        for j in range(1, 2 * NZ):
            c = move(j, lax.rem(L.sq + j, 2 * NZ), L.sq)
            c.start()
            L.drains.append(c.wait_send)

    def finish():
        keep.wait()
        for j in range(1, 2 * NZ):
            move(j, L.sq, lax.rem(L.sq + 2 * NZ - j, 2 * NZ)).wait_recv()
    return begin, finish


def add_into(dst, rows0, cols, src, n):
    step = 48

    def one(i, _):
        here = pl.ds(mult(i * step, 16), step)
        there = pl.ds(mult(rows0 + i * step, 16), step)
        dst[there, cols] = (dst[there, cols].astype(jnp.float32) + src[here, :].astype(jnp.float32)).astype(jnp.bfloat16)
        return 0
    lax.fori_loop(0, n // step, one, 0)


def reduce_scratch(r, c, split):
    half, (a, b), big = c // 2, split, 2 * r
    bf = lambda *s: pltpu.VMEM(s, jnp.bfloat16)
    return [bf(32 * r, half), bf(8 * big, a), bf(4 * big, b), bf(4 * big, b), bf(4 * big, a), bf(4 * big, b),
            bf(3, big, half), bf(3, big, half), pltpu.VMEM((2, r, half), jnp.float32), pltpu.VMEM((r, half), jnp.float32)]


N_REDUCE = 14


def reduce(L, part, out, scratch, r, split):
    acc, a1, b1x, b1y, a2, b2, from_l, from_r, fin, got = scratch
    half = part.shape[1] // 2
    a, b = split
    big = 2 * r
    mine = pl.ds(mult(L.core * half, 128), half)
    other = pl.ds(mult((1 - L.core) * half, 128), half)
    ca, cb = pl.ds(0, a), pl.ds(a, b)
    quarter = lambda dp, n=1: pl.ds(mult(dp * NZ * big, 16), n * NZ * big)
    chip = lambda z: pl.ds(mult((L.dp * NZ + z) * big, 16), big)
    i0, ia1, ibx, iby, ia2, ib2, ifin = [L.new() for _ in range(7)]
    ir = [None] + [L.new() for _ in range(3)]
    il = [L.new() for _ in range(3)]
    q = lambda dp: dp * NZ * big
    other_y = quarter(2 * (1 - L.y), 2)

    def go(*cs):
        for c in cs:
            c.start()
            L.drains.append(c.wait_send)

    core_copy = L.copy(i0, part.at[:, other], acc, L.dp, L.sib)
    a1_copy = L.copy(ia1, acc.at[other_y, ca], a1, L.dp_y, L.sq)
    bx_copy = L.copy(ibx, acc.at[quarter(L.dp_x), cb], b1x, L.dp_x, L.sq)
    by_copy = L.copy(iby, acc.at[quarter(3 - L.dp), cb], b1y, L.dp_x, L.sq)
    a2_copy = L.copy(ia2, acc.at[quarter(L.dp_x), ca], a2, L.dp_x, L.sq)
    b2_copy = L.copy(ib2, acc.at[quarter(L.dp_y), cb], b2, L.dp_y, L.sq)

    def s0():
        go(core_copy)

    def s1():
        core_copy.wait_recv()
        step = 48

        def one(i, _):
            here = pl.ds(mult(i * step, 16), step)
            acc[here, :] = (acc[here, :].astype(jnp.float32) + part[here, mine].astype(jnp.float32)).astype(jnp.bfloat16)
            return 0
        lax.fori_loop(0, acc.shape[0] // step, one, 0)
        go(a1_copy, bx_copy, by_copy)

    def s2():
        a1_copy.wait_recv()
        add_into(acc, q(2 * L.y), ca, a1, 8 * big)
        go(a2_copy)
        bx_copy.wait_recv()
        by_copy.wait_recv()
        add_into(acc, q(L.dp_y), cb, b1y, 4 * big)
        go(b2_copy)
        add_into(acc, q(L.dp), cb, b1x, 4 * big)

    def s3():
        a2_copy.wait_recv()
        add_into(acc, q(L.dp), ca, a2, 4 * big)
        b2_copy.wait_recv()
        add_into(acc, q(L.dp), cb, b2, 4 * big)

    full_cols = pl.ds(0, half)

    def hop_r(t, src):
        return L.copy(ir[t], src, from_l.at[t - 1], L.dp, L.sq + 2)

    def hop_l(t, src):
        return L.copy(il[t], src, from_r.at[t], L.dp, L.sq - 2)

    def merge(buf, k, t):
        buf[k] = (buf[k].astype(jnp.float32) + acc[chip(t), :].astype(jnp.float32)).astype(jnp.bfloat16)

    def line(s):
        @pl.when(L.z == s)
        def _():
            for t in range(NZ - 1, s, -1):
                if s == 0:
                    hop_r(t, acc.at[chip(t), full_cols]).start()
                else:
                    hop_r(t, from_l.at[t - 1]).wait_recv()
                    merge(from_l, t - 1, t)
                    hop_r(t, from_l.at[t - 1]).start()

        @pl.when(L.z == NZ - 1 - s)
        def _():
            for t in range(0, NZ - 1 - s):
                if s == 0:
                    hop_l(t, acc.at[chip(t), full_cols]).start()
                else:
                    hop_l(t, from_r.at[t]).wait_recv()
                    merge(from_r, t, t)
                    hop_l(t, from_r.at[t]).start()

        def drain():
            @pl.when(L.z == s)
            def _():
                for t in range(NZ - 1, s, -1):
                    hop_r(t, from_l.at[t - 1]).wait_send()

            @pl.when(L.z == NZ - 1 - s)
            def _():
                for t in range(0, NZ - 1 - s):
                    hop_l(t, from_r.at[t]).wait_send()
        L.drains.append(drain)

    fin_copy = L.copy(ifin, fin.at[1 - L.core], got, L.dp, L.sib)

    def s7():
        for z in range(NZ):
            @pl.when(L.z == z)
            def _(z=z):
                total = acc[chip(z), :].astype(jnp.float32)
                if z > 0:
                    hop_r(z, from_l.at[z - 1]).wait_recv()
                    total = total + from_l[z - 1].astype(jnp.float32)
                if z < NZ - 1:
                    hop_l(z, from_r.at[z]).wait_recv()
                    total = total + from_r[z].astype(jnp.float32)
                fin[...] = total.reshape(2, r, half)
        go(fin_copy)

    def s8():
        out[:, mine] = fin[L.core]
        fin_copy.wait_recv()
        out[:, other] = got[...]
    return [s0, s1, s2, s3] + [functools.partial(line, s) for s in range(3)] + [s7, s8]


def one_hot(slots, rows):
    row = lax.broadcasted_iota(jnp.int32, (rows, slots.shape[1]), 0)
    return jnp.where(slots == row, 1.0, 0.0).astype(jnp.bfloat16)


def head_lanes(width):
    row = lax.broadcasted_iota(jnp.int32, (2 * BLK, width), 0)
    lane = lax.rem(lax.broadcasted_iota(jnp.int32, (2 * BLK, width), 1), 128)
    return (row < BLK) == (lane < 64)


def dot(a, b, ca, cb):
    return lax.dot_general(a, b, (((ca,), (cb,)), ((), ())), preferred_element_type=jnp.float32)


def attend_fwd(scale, q_ref, k_ref, v_ref, perm_ref, mixed_ref, slot_ref, prob_ref, head_ref):
    nblk = q_ref.shape[0] // BLK
    share = BLK // nblk
    keep = head_lanes(384)
    for k in range(nblk):
        here = pl.ds(k * BLK, BLK)
        packed = jnp.concatenate([q_ref[here, :], k_ref[here, :], v_ref[here, :]], axis=1)
        table = one_hot(perm_ref[0, k:k + 1, :], BLK)
        moved = jnp.where(keep, dot(table, packed, 0, 0), 0.0).astype(jnp.bfloat16)
        slot_ref[0, :, :, pl.ds(k * share, share), :] = moved.reshape(2, nblk, share, 384)
    for h in range(2):
        for c in range(nblk):
            q, kk, v = slot_ref[0, h, c, :, 0:128], slot_ref[0, h, c, :, 128:256], slot_ref[0, h, c, :, 256:384]
            scores = dot(q, kk, 1, 1) * scale
            e = jnp.exp(scores - jnp.max(scores, axis=-1, keepdims=True))
            probs = (e / jnp.sum(e, axis=-1, keepdims=True)).astype(jnp.bfloat16)
            prob_ref[0, h, c] = probs
            head_ref[h, c] = dot(probs, v, 1, 0).astype(jnp.bfloat16)
    for k in range(nblk):
        table = one_hot(perm_ref[0, k:k + 1, :], BLK)
        back = head_ref[:, :, pl.ds(k * share, share), :].reshape(2 * BLK, BLK)
        mixed_ref[pl.ds(k * BLK, BLK), :] = dot(table, back, 1, 0).astype(jnp.bfloat16)


def attend_bwd(scale, dm_ref, perm_ref, slot_ref, prob_ref, dq_ref, dk_ref, dv_ref, sums_ref, up_ref, grad_ref):
    nblk = dm_ref.shape[0] // BLK
    share = BLK // nblk
    keep = head_lanes(128)
    for k in range(nblk):
        table = one_hot(perm_ref[0, k:k + 1, :], BLK)
        moved = jnp.where(keep, dot(table, dm_ref[pl.ds(k * BLK, BLK), :], 0, 0), 0.0).astype(jnp.bfloat16)
        up_ref[:, :, pl.ds(k * share, share), :] = moved.reshape(2, nblk, share, 128)
    for h in range(2):
        for c in range(nblk):
            q, kk, v = slot_ref[0, h, c, :, 0:128], slot_ref[0, h, c, :, 128:256], slot_ref[0, h, c, :, 256:384]
            probs, up = prob_ref[0, h, c], up_ref[h, c]
            dprobs = dot(up, v, 1, 1)
            p32 = probs.astype(jnp.float32)
            inner = jnp.sum(p32 * dprobs, axis=-1, keepdims=True)
            dscores = (p32 * (dprobs - inner)).astype(jnp.bfloat16)
            grad_ref[h, c, :, 0:128] = (dot(dscores, kk, 1, 0) * scale).astype(jnp.bfloat16)
            grad_ref[h, c, :, 128:256] = (dot(dscores, q, 0, 0) * scale).astype(jnp.bfloat16)
            grad_ref[h, c, :, 256:384] = dot(probs, up, 0, 0).astype(jnp.bfloat16)
    total = jnp.zeros((1, 384), jnp.float32)
    for k in range(nblk):
        table = one_hot(perm_ref[0, k:k + 1, :], BLK)
        back = grad_ref[:, :, pl.ds(k * share, share), :].reshape(2 * BLK, 384)
        here = pl.ds(k * BLK, BLK)
        moved = dot(table, back, 1, 0)
        total = total + jnp.sum(moved, axis=0, keepdims=True)
        moved = moved.astype(jnp.bfloat16)
        dq_ref[here, :] = moved[:, 0:128]
        dk_ref[here, :] = moved[:, 128:256]
        dv_ref[here, :] = moved[:, 256:384]
    sums_ref[...] = jnp.broadcast_to(total, (8, 384))


SIZES = {"qkv": (24, 2560, (640, 640)), "out": (24, 768, (256, 128)), "up": (24, 3072, (768, 768)), "down": (96, 768, (128, 256))}
ALL = ("dp", "seq")
VM = pl.BlockSpec(memory_space=pltpu.VMEM)
BF = jnp.bfloat16
LIMIT = 60 * 2**20


def gather_kernel(names, na, *refs):
    n = len(names)
    ins, outs, sc = refs[:n + na], refs[n + na:2 * (n + na)], refs[2 * (n + na):]
    L = Links(sc[n], sc[n + 1])
    L.enter()
    progs = [gather(L, ins[i], outs[i], sc[i], SIZES[nm][0], SIZES[nm][2]) for i, nm in enumerate(names)]
    sp = [spread(L, ins[n + i], outs[n + i], sc[n + 2].at[i]) for i in range(na)]
    for k in range(8):
        for p in progs:
            p[k]()
        if k == 3:
            for b, _ in sp:
                b()
    for _, f in sp:
        f()
    L.drain()


def gather_call(names, shards, rows):
    na, n = len(rows), len(names)
    count = 15 * n + 7 * na
    outs = [jax.ShapeDtypeStruct((32 * SIZES[nm][0], SIZES[nm][1]), BF) for nm in names]
    outs += [jax.ShapeDtypeStruct(a.shape, BF) for a in rows]
    return pl.pallas_call(
        functools.partial(gather_kernel, names, na), out_shape=outs, in_specs=[VM] * (n + na), out_specs=[VM] * (n + na),
        scratch_shapes=[pltpu.VMEM((SIZES[nm][0], SIZES[nm][1] // 2), BF) for nm in names]
        + [pltpu.SemaphoreType.DMA((count,)), pltpu.SemaphoreType.DMA((count,)), pltpu.SemaphoreType.DMA((max(na, 1),))],
        compiler_params=pltpu.CompilerParams(collective_id=0, has_side_effects=True, vmem_limit_bytes=LIMIT),
    )(*shards, *rows)


def reduce_kernel(names, na, *refs):
    n = len(names)
    ins, outs, sc = refs[:n + na], refs[n + na:2 * (n + na)], refs[2 * (n + na):]
    L = Links(sc[10 * n], sc[10 * n + 1])
    L.enter()
    progs = [reduce(L, ins[i], outs[i], sc[10 * i:10 * i + 10], SIZES[nm][0], SIZES[nm][2]) for i, nm in enumerate(names)]
    sp = [spread(L, ins[n + i], outs[n + i], sc[10 * n + 2].at[i]) for i in range(na)]
    for b, _ in sp:
        b()
    for k in range(9):
        for p in progs:
            p[k]()
    for _, f in sp:
        f()
    L.drain()


def reduce_call(names, parts, rows, cid):
    na, n = len(rows), len(names)
    count = N_REDUCE * n + 7 * na
    outs = [jax.ShapeDtypeStruct(SIZES[nm][:2], jnp.float32) for nm in names]
    outs += [jax.ShapeDtypeStruct(a.shape, BF) for a in rows]
    return pl.pallas_call(
        functools.partial(reduce_kernel, names, na), out_shape=outs, in_specs=[VM] * (n + na), out_specs=[VM] * (n + na),
        scratch_shapes=sum([reduce_scratch(*SIZES[nm]) for nm in names], [])
        + [pltpu.SemaphoreType.DMA((count,)), pltpu.SemaphoreType.DMA((count,)), pltpu.SemaphoreType.DMA((max(na, 1),))],
        compiler_params=pltpu.CompilerParams(collective_id=cid, has_side_effects=True, vmem_limit_bytes=LIMIT),
    )(*parts, *rows)


def slot_rows(route, me):
    heads, n = route.shape[0], 2 * NZ
    per = route.reshape(heads, n, -1)
    mine = (per[:, 0] // BLK) == me
    place = jnp.cumsum(mine.astype(jnp.int32), axis=1) - 1
    pick = (mine[:, None, :] & (place[:, None, :] == jnp.arange(BLK)[None, :, None])).astype(BF)
    local = jnp.where(mine[:, None, :], per - me * BLK, 0).astype(BF)
    rows = jnp.einsum("hke,hse->hks", local, pick, preferred_element_type=jnp.float32).astype(jnp.int32)
    return rows.reshape(heads // 2, 2, n, BLK).transpose(0, 2, 1, 3).reshape(heads // 2, n, 2 * BLK)


def homes(tokens, w_qkv, w_out, w_up, w_down, vectors, up_bias, cluster_route, upstream):
    me = lax.axis_index("seq")
    rows_here, width = tokens.shape
    pairs = H // 2
    scale = (width // H) ** -0.5
    aux = jnp.pad(vectors.T, ((0, 0), (0, 248))) + jnp.pad(up_bias[None, :], ((0, 23), (8, 152)))
    full_qkv, full_out, full_up, full_down, x, g = gather_call(
        ("qkv", "out", "up", "down"), [jnp.concatenate([w_qkv, aux], axis=1), w_out, w_up, w_down], [tokens, upstream])
    perm = slot_rows(cluster_route[0], me)
    vec = full_qkv[:, 2304:2312].T.astype(jnp.float32)
    ub = full_qkv[::24, 2312:2408].reshape(-1).astype(jnp.float32)
    w = full_qkv[:, :2304]
    shifts = jnp.concatenate([vec[0], jnp.zeros((width,), jnp.float32), vec[1]])
    qkv = (jnp.dot(x, w, preferred_element_type=jnp.float32) + shifts).astype(BF)
    col = lambda o: pl.BlockSpec((rows_here, 128), lambda p, o=o: (0, p + o))
    perm_spec = pl.BlockSpec((1, 8, 256), lambda p: (p, 0, 0))
    slot_spec = pl.BlockSpec((1, 2, 8, BLK, 384), lambda p: (p, 0, 0, 0, 0))
    prob_spec = pl.BlockSpec((1, 2, 8, BLK, BLK), lambda p: (p, 0, 0, 0, 0))
    mixed, slots, probs = pl.pallas_call(
        functools.partial(attend_fwd, scale), grid=(pairs,),
        out_shape=[jax.ShapeDtypeStruct((rows_here, width), BF), jax.ShapeDtypeStruct((pairs, 2, 8, BLK, 384), BF),
                   jax.ShapeDtypeStruct((pairs, 2, 8, BLK, BLK), BF)],
        in_specs=[col(0), col(pairs), col(2 * pairs), perm_spec], out_specs=[col(0), slot_spec, prob_spec],
        scratch_shapes=[pltpu.VMEM((2, 8, BLK, BLK), BF)],
        compiler_params=pltpu.CompilerParams(vmem_limit_bytes=LIMIT),
    )(qkv, qkv, qkv, perm)
    attention = jnp.dot(mixed, full_out, preferred_element_type=jnp.float32) + vec[2]
    first, n1, s1 = normalize(x.astype(jnp.float32) + attention, vec[4], vec[5])
    low = first.astype(BF)
    wide = jnp.dot(low, full_up, preferred_element_type=jnp.float32) + ub
    act, pull = jax.vjp(exact_gelu, wide)
    act = act.astype(BF)
    narrow = jnp.dot(act, full_down, preferred_element_type=jnp.float32) + vec[3]
    out, n2, s2 = normalize(first + narrow, vec[6], vec[7])
    gf = g.astype(jnp.float32)
    gain2, shift2 = jnp.sum(gf * n2, axis=0), jnp.sum(gf, axis=0)
    d_second = norm_back(gf, n2, s2, vec[6])
    d_narrow = d_second.astype(BF)
    g_down = jnp.einsum("tf,td->fd", act, d_narrow, preferred_element_type=jnp.float32).astype(BF)
    down_bias = jnp.sum(d_narrow.astype(jnp.float32), axis=0)
    d_wide = pull(jnp.einsum("td,fd->tf", d_narrow, full_down, preferred_element_type=jnp.float32))[0].astype(BF)
    g_up = jnp.einsum("td,tf->df", low, d_wide, preferred_element_type=jnp.float32).astype(BF)
    g_ub = jnp.sum(d_wide.astype(jnp.float32), axis=0)
    d_first = d_second + jnp.einsum("tf,df->td", d_wide, full_up, preferred_element_type=jnp.float32)
    gain1, shift1 = jnp.sum(d_first * n1, axis=0), jnp.sum(d_first, axis=0)
    d_res = norm_back(d_first, n1, s1, vec[4])
    d_attn = d_res.astype(BF)
    g_out = jnp.einsum("td,te->de", mixed, d_attn, preferred_element_type=jnp.float32).astype(BF)
    out_bias = jnp.sum(d_attn.astype(jnp.float32), axis=0)
    d_mixed = jnp.einsum("te,de->td", d_attn, full_out, preferred_element_type=jnp.float32).astype(BF)
    dq, dk, dv, sums = pl.pallas_call(
        functools.partial(attend_bwd, scale), grid=(pairs,),
        out_shape=[jax.ShapeDtypeStruct((rows_here, width), BF)] * 3 + [jax.ShapeDtypeStruct((8 * pairs, 384), jnp.float32)],
        in_specs=[col(0), perm_spec, slot_spec, prob_spec], out_specs=[col(0)] * 3 + [pl.BlockSpec((8, 384), lambda p: (p, 0))],
        scratch_shapes=[pltpu.VMEM((2, 8, BLK, BLK), BF), pltpu.VMEM((2, 8, BLK, 384), BF)],
        compiler_params=pltpu.CompilerParams(vmem_limit_bytes=LIMIT),
    )(d_mixed, perm, slots, probs)
    sums = sums[::8].reshape(pairs, 3, 128)
    d_proj = jnp.concatenate([dq, dk, dv], axis=1)
    g_qkv = jnp.einsum("td,tf->df", x, d_proj, preferred_element_type=jnp.float32).astype(BF)
    gx = (jnp.einsum("tf,df->td", d_proj, w, preferred_element_type=jnp.float32) + d_res).astype(BF)
    g_vec = jnp.stack([sums[:, 0].reshape(-1), sums[:, 2].reshape(-1), out_bias, down_bias, gain1, shift1, gain2, shift2])
    g_aux = jnp.pad(g_vec.T, ((0, 0), (0, 248)))
    g_aux = g_aux.reshape(32, 24, 256) + jnp.pad(g_ub.reshape(32, 1, 96), ((0, 0), (0, 23), (8, 152)))
    part = jnp.concatenate([g_qkv, g_aux.reshape(768, 256).astype(BF)], axis=1)
    r_out, r_up, r_down, out_rows = reduce_call(("out", "up", "down"), [g_out, g_up, g_down], [out.astype(BF)], 1)
    r_qkv, gx_rows = reduce_call(("qkv",), [part], [gx], 2)
    return (out_rows, gx_rows, r_qkv[:, :2304], r_out, r_up, r_down, r_qkv[:, 2304:2312].T, r_qkv[0, 2312:2408])


def solution(mesh):
    small = dict(mesh.shape) == {"dp": 4, "seq": 2 * NZ}
    rows = P(ALL, None)
    return jax.shard_map(
        homes if small else shards, mesh=mesh,
        in_specs=(rows,) * 5 + (P(None, ALL), P(ALL), P("dp", None, None), rows),
        out_specs=(rows,) * 6 + (P(None, ALL), P(ALL)),
        check_vma=False,
    )
```

```python
import functools

import jax
import jax.numpy as jnp
from jax import lax
from jax.experimental import pallas as pl
from jax.experimental.pallas import tpu as pltpu
from jax.sharding import PartitionSpec as P

H = 12
CL = 128


epsilon = 1e-06


def normalize(resid, norm_gain, norm_shift):
    average = jnp.mean(resid, axis=-1, keepdims=True)
    centred = resid - average
    spread = jnp.mean(centred * centred, axis=-1, keepdims=True)
    scaled = lax.rsqrt(spread + epsilon)
    normed = centred * scaled
    return (normed * norm_gain + norm_shift, normed, scaled)


def norm_back(grad_output, normed, scaled, norm_gain):
    grad_norm = grad_output * norm_gain
    first_term = jnp.mean(grad_norm, axis=-1, keepdims=True)
    second_term = jnp.mean(grad_norm * normed, axis=-1, keepdims=True)
    return scaled * (grad_norm - first_term - normed * second_term)


def exact_gelu(value):
    return jax.nn.gelu(value, approximate=False)


def order_table(sending):
    heads, rows_here = sending.shape
    columns = jnp.arange(rows_here, dtype=jnp.int32)[None, None, :]
    return (sending[:, :, None] == columns).astype(jnp.bfloat16)


def to_slots(source_rows, table):
    moved = jnp.einsum("hrs,skhe->rkhe", table, source_rows, preferred_element_type=jnp.float32)
    return moved.astype(jnp.bfloat16)


def to_tokens(source_rows, table):
    moved = jnp.einsum("hrs,rkhe->skhe", table, source_rows, preferred_element_type=jnp.float32)
    return moved.astype(jnp.bfloat16)


def cluster_scores(query_c, key_c, scale_factor):
    return (
        jnp.einsum("cahe,cbhe->hcab", query_c, key_c, preferred_element_type=jnp.float32)
        * scale_factor
    )


def shards(tokens, w_qkv, w_out, w_up, w_down, vectors, up_bias, cluster_route, upstream):
    lane_count = lax.axis_size("seq")
    lane_index = lax.axis_index("seq")
    wide_qkv, wide_out, wide_up, wide_down, wide_vectors, wide_bias = (
        lax.all_gather(w_qkv, ("dp", "seq"), axis=0, tiled=True),
        lax.all_gather(w_out, ("dp", "seq"), axis=0, tiled=True),
        lax.all_gather(w_up, ("dp", "seq"), axis=0, tiled=True),
        lax.all_gather(w_down, ("dp", "seq"), axis=0, tiled=True),
        lax.all_gather(vectors, ("dp", "seq"), axis=1, tiled=True),
        lax.all_gather(up_bias, ("dp", "seq"), axis=0, tiled=True),
    )
    rows_here = tokens.shape[0]
    model_width = tokens.shape[1]
    head_size = model_width // H
    portion = rows_here // lane_count
    clusters = rows_here // CL
    scale_factor = head_size ** (-0.5)
    vector_rows = wide_vectors.astype(jnp.float32)
    route_rows = cluster_route[0]
    by_target = lax.dynamic_slice_in_dim(route_rows, lane_index * rows_here, rows_here, 1)
    sending = jnp.swapaxes(by_target.reshape(H, lane_count, portion), 1, 2).reshape(H, rows_here)
    table = order_table(sending)
    projected = jnp.dot(tokens, wide_qkv, preferred_element_type=jnp.float32)
    shifts = jnp.concatenate(
        [vector_rows[0], jnp.zeros((model_width,), jnp.float32), vector_rows[1]]
    )
    projected = (projected + shifts).astype(jnp.bfloat16).reshape(rows_here, 3, H, head_size)
    outgoing = to_slots(projected, table)
    arrived = lax.all_to_all(
        outgoing.reshape(portion, lane_count, 3 * model_width),
        "seq",
        split_axis=1,
        concat_axis=1,
        tiled=True,
    )
    slot_qkv = arrived.reshape(clusters, CL, 3, H, head_size)
    query_c = slot_qkv[:, :, 0]
    key_c = slot_qkv[:, :, 1]
    value_c = slot_qkv[:, :, 2]
    scores = cluster_scores(query_c, key_c, scale_factor)
    row_peak = jnp.max(scores, axis=-1, keepdims=True)
    exponent = jnp.exp(scores - row_peak)
    row_total = jnp.sum(exponent, axis=-1, keepdims=True)
    soft_weights = exponent / row_total
    log_total = row_peak + jnp.log(row_total)
    heads_slot = jnp.einsum(
        "hcab,cbhe->cahe",
        soft_weights.astype(jnp.bfloat16),
        value_c,
        preferred_element_type=jnp.float32,
    ).astype(jnp.bfloat16)
    returned = lax.all_to_all(
        heads_slot.reshape(portion, lane_count, model_width),
        "seq",
        split_axis=1,
        concat_axis=1,
        tiled=True,
    )
    mixed_heads = to_tokens(returned.reshape(rows_here, 1, H, head_size), table).reshape(
        rows_here, model_width
    )
    attention = jnp.dot(mixed_heads, wide_out, preferred_element_type=jnp.float32) + vector_rows[2]
    first_norm, first_normed, first_scaled = normalize(
        tokens.astype(jnp.float32) + attention, vector_rows[4], vector_rows[5]
    )
    first_low = first_norm.astype(jnp.bfloat16)
    widened = jnp.dot(first_low, wide_up, preferred_element_type=jnp.float32) + wide_bias.astype(
        jnp.float32
    )
    activated, gelu_pull = jax.vjp(exact_gelu, widened)
    activated_low = activated.astype(jnp.bfloat16)
    narrowed = (
        jnp.dot(activated_low, wide_down, preferred_element_type=jnp.float32) + vector_rows[3]
    )
    output, second_normed, second_scaled = normalize(
        first_norm + narrowed, vector_rows[6], vector_rows[7]
    )
    back_qkv, back_out, back_up, back_down = (
        lax.all_gather(w_qkv, ("dp", "seq"), axis=0, tiled=True),
        lax.all_gather(w_out, ("dp", "seq"), axis=0, tiled=True),
        lax.all_gather(w_up, ("dp", "seq"), axis=0, tiled=True),
        lax.all_gather(w_down, ("dp", "seq"), axis=0, tiled=True),
    )
    grad_output = upstream.astype(jnp.float32)
    grad_gain_two = jnp.sum(grad_output * second_normed, axis=0)
    grad_shift_two = jnp.sum(grad_output, axis=0)
    grad_second = norm_back(grad_output, second_normed, second_scaled, vector_rows[6])
    grad_narrow = grad_second.astype(jnp.bfloat16)
    grad_down_w = jnp.einsum(
        "tf,td->fd", activated_low, grad_narrow, preferred_element_type=jnp.float32
    )
    grad_down_bias = jnp.sum(grad_narrow.astype(jnp.float32), axis=0)
    grad_active = jnp.einsum(
        "td,fd->tf", grad_narrow, back_down, preferred_element_type=jnp.float32
    )
    grad_wide = gelu_pull(grad_active)[0].astype(jnp.bfloat16)
    grad_up_w = jnp.einsum("td,tf->df", first_low, grad_wide, preferred_element_type=jnp.float32)
    grad_lift_bias = jnp.sum(grad_wide.astype(jnp.float32), axis=0)
    grad_first = grad_second + jnp.einsum(
        "tf,df->td", grad_wide, back_up, preferred_element_type=jnp.float32
    )
    grad_gain_one = jnp.sum(grad_first * first_normed, axis=0)
    grad_shift_one = jnp.sum(grad_first, axis=0)
    grad_resid = norm_back(grad_first, first_normed, first_scaled, vector_rows[4])
    grad_attn = grad_resid.astype(jnp.bfloat16)
    grad_out_w = jnp.einsum("td,te->de", mixed_heads, grad_attn, preferred_element_type=jnp.float32)
    grad_out_bias = jnp.sum(grad_attn.astype(jnp.float32), axis=0)
    grad_mixed = jnp.einsum(
        "te,de->td", grad_attn, back_out, preferred_element_type=jnp.float32
    ).astype(jnp.bfloat16)
    grad_sending = to_slots(grad_mixed.reshape(rows_here, 1, H, head_size), table)
    grad_slot = lax.all_to_all(
        grad_sending.reshape(portion, lane_count, model_width),
        "seq",
        split_axis=1,
        concat_axis=1,
        tiled=True,
    )
    grad_slot = grad_slot.reshape(clusters, CL, H, head_size)
    scores = cluster_scores(query_c, key_c, scale_factor)
    soft_weights = jnp.exp(scores - log_total)
    grad_soft = jnp.einsum(
        "cahe,cbhe->hcab", grad_slot, value_c, preferred_element_type=jnp.float32
    )
    inner_sum = jnp.sum(soft_weights * grad_soft, axis=-1, keepdims=True)
    grad_scores = (soft_weights * (grad_soft - inner_sum)).astype(jnp.bfloat16)
    grad_query = (
        jnp.einsum("hcab,cbhe->cahe", grad_scores, key_c, preferred_element_type=jnp.float32)
        * scale_factor
    )
    grad_key = (
        jnp.einsum("hcab,cahe->cbhe", grad_scores, query_c, preferred_element_type=jnp.float32)
        * scale_factor
    )
    grad_value = jnp.einsum(
        "hcab,cahe->cbhe",
        soft_weights.astype(jnp.bfloat16),
        grad_slot,
        preferred_element_type=jnp.float32,
    )
    grad_slots = jnp.stack([grad_query, grad_key, grad_value], axis=2).astype(jnp.bfloat16)
    came_back = lax.all_to_all(
        grad_slots.reshape(portion, lane_count, 3 * model_width),
        "seq",
        split_axis=1,
        concat_axis=1,
        tiled=True,
    )
    grad_proj = to_tokens(came_back.reshape(rows_here, 3, H, head_size), table).reshape(
        rows_here, 3 * model_width
    )
    grad_qkv_w = jnp.einsum("td,tf->df", tokens, grad_proj, preferred_element_type=jnp.float32)
    bias_sums = jnp.sum(grad_proj.astype(jnp.float32), axis=0).reshape(3, model_width)
    grad_tokens = (
        jnp.einsum("tf,df->td", grad_proj, back_qkv, preferred_element_type=jnp.float32)
        + grad_resid
    ).astype(jnp.bfloat16)
    grad_vector_rows = jnp.stack(
        [
            bias_sums[0],
            bias_sums[2],
            grad_out_bias,
            grad_down_bias,
            grad_gain_one,
            grad_shift_one,
            grad_gain_two,
            grad_shift_two,
        ]
    )
    shares = (
        lax.psum_scatter(grad_qkv_w, ("dp", "seq"), scatter_dimension=0, tiled=True),
        lax.psum_scatter(grad_out_w, ("dp", "seq"), scatter_dimension=0, tiled=True),
        lax.psum_scatter(grad_up_w, ("dp", "seq"), scatter_dimension=0, tiled=True),
        lax.psum_scatter(grad_down_w, ("dp", "seq"), scatter_dimension=0, tiled=True),
        lax.psum_scatter(grad_vector_rows, ("dp", "seq"), scatter_dimension=1, tiled=True),
        lax.psum_scatter(grad_lift_bias, ("dp", "seq"), scatter_dimension=0, tiled=True),
    )
    return (
        output.astype(jnp.bfloat16),
        grad_tokens,
        shares[0],
        shares[1],
        shares[2],
        shares[3],
        shares[4],
        shares[5],
    )


MESH = pl.DeviceIdType.MESH
NZ = 4
BLK = 128

class Links:
    def __init__(self, send_sems, recv_sems):
        self.send_sems, self.recv_sems, self.count, self.drains = send_sems, recv_sems, 0, []
        self.dp, self.sq = lax.axis_index("dp"), lax.axis_index("seq")
        self.x, self.y = lax.rem(self.dp, 2), self.dp // 2
        self.core, self.z = lax.rem(self.sq, 2), self.sq // 2
        self.sib = self.sq + 1 - 2 * self.core
        self.dp_x = self.dp + 1 - 2 * self.x
        self.dp_y = self.dp + 2 - 4 * self.y

    def new(self):
        self.count += 1
        return self.count - 1

    def copy(self, i, src, dst, dp, sq):
        return pltpu.make_async_remote_copy(
            src_ref=src, dst_ref=dst, send_sem=self.send_sems.at[i], recv_sem=self.recv_sems.at[i],
            device_id=(dp, sq), device_id_type=MESH)

    def enter(self, near=True, line=True):
        barrier = pltpu.get_barrier_semaphore()
        n = 0
        if near:
            for dp in (self.dp_x, self.dp_y):
                pl.semaphore_signal(barrier, inc=1, device_id=(dp, self.sq), device_id_type=MESH)
                n += 1
        if line:
            for j in range(1, 2 * NZ):
                pl.semaphore_signal(barrier, inc=1, device_id=(self.dp, lax.rem(self.sq + j, 2 * NZ)), device_id_type=MESH)
                n += 1
        pl.semaphore_wait(barrier, n)

    def go(self, *makers):
        for make in makers:
            make().start()
            self.drains.append(lambda make=make: make().wait_send())

    def drain(self):
        for d in self.drains:
            d()


def mult(v, m):
    return pl.multiple_of(v, m)


def gather(L, shard, full, half_buf, r, split):
    half = full.shape[1] // 2
    a, b = split
    big = 2 * r
    mine = pl.ds(mult(L.core * half, 128), half)
    other = pl.ds(mult((1 - L.core) * half, 128), half)
    cols_a = pl.ds(mult(L.core * half, 128), a)
    cols_b = pl.ds(mult(L.core * half + a, 128), b)
    chip = lambda z: pl.ds(mult((L.dp * NZ + z) * big, 16), big)
    quarter = lambda dp, n=1: pl.ds(mult(dp * NZ * big, 16), n * NZ * big)
    i0 = L.new()
    fr = [None] + [L.new() for _ in range(3)]
    fl = [None] + [L.new() for _ in range(3)]
    ax, by, ay, bx0, bx1, c0, c1, c2 = [L.new() for _ in range(8)]
    first = lambda: L.copy(i0, shard.at[:, other], half_buf, L.dp, L.sib)

    def right(d, z0):
        return L.copy(fr[d], full.at[chip(z0), mine], full.at[chip(z0), mine], L.dp, L.sq + 2)

    def left(d, z0):
        return L.copy(fl[d], full.at[chip(z0), mine], full.at[chip(z0), mine], L.dp, L.sq - 2)

    def send_line(d):
        @pl.when((L.z >= d - 1) & (L.z < NZ - 1))
        def _():
            right(d, L.z - d + 1).start()

        @pl.when((L.z <= NZ - d) & (L.z > 0))
        def _():
            left(d, L.z + d - 1).start()

    def drain_line(d):
        @pl.when((L.z >= d - 1) & (L.z < NZ - 1))
        def _():
            right(d, L.z - d + 1).wait_send()

        @pl.when((L.z <= NZ - d) & (L.z > 0))
        def _():
            left(d, L.z + d - 1).wait_send()

    def recv_line(d):
        @pl.when(L.z >= d)
        def _():
            right(d, L.z - d).wait_recv()

        @pl.when(L.z + d <= NZ - 1)
        def _():
            left(d, L.z + d).wait_recv()

    def same(i, rows, cols, dp, sq):
        ref = full.at[rows, cols]
        return L.copy(i, ref, ref, dp, sq)

    def s0():
        L.go(first)

    def s1():
        first().wait_recv()
        own, got = shard[:, mine], half_buf[...]

        @pl.when(L.core == 0)
        def _():
            full[chip(L.z), mine] = jnp.concatenate([own, got], axis=0)

        @pl.when(L.core == 1)
        def _():
            full[chip(L.z), mine] = jnp.concatenate([got, own], axis=0)
        send_line(1)
        L.drains.append(functools.partial(drain_line, 1))

    def s2():
        recv_line(1)
        send_line(2)
        L.drains.append(functools.partial(drain_line, 2))

    def s3():
        recv_line(2)
        send_line(3)
        L.drains.append(functools.partial(drain_line, 3))

    def s4():
        recv_line(3)
        q = lambda: quarter(L.dp)
        L.go(lambda: same(ax, q(), cols_a, L.dp_x, L.sq), lambda: same(by, q(), cols_b, L.dp_y, L.sq),
             lambda: same(c0, q(), mine, L.dp, L.sib))

    def s5():
        same(ax, quarter(L.dp_x), cols_a, L.dp_x, L.sq).wait_recv()
        L.go(lambda: same(ay, quarter(2 * L.y, 2), cols_a, L.dp_y, L.sq))
        same(by, quarter(L.dp_y), cols_b, L.dp_y, L.sq).wait_recv()
        L.go(lambda: same(bx0, quarter(L.dp), cols_b, L.dp_x, L.sq), lambda: same(bx1, quarter(L.dp_y), cols_b, L.dp_x, L.sq))

    def s6():
        same(bx0, quarter(L.dp_x), cols_b, L.dp_x, L.sq).wait_recv()
        L.go(lambda: same(c1, quarter(L.dp_x), mine, L.dp, L.sib))
        same(ay, quarter(2 * (1 - L.y), 2), cols_a, L.dp_y, L.sq).wait_recv()
        same(bx1, quarter(3 - L.dp), cols_b, L.dp_x, L.sq).wait_recv()
        L.go(lambda: same(c2, quarter(2 * (1 - L.y), 2), mine, L.dp, L.sib))

    def s7():
        same(c0, quarter(L.dp), other, L.dp, L.sib).wait_recv()
        same(c1, quarter(L.dp_x), other, L.dp, L.sib).wait_recv()
        same(c2, quarter(2 * (1 - L.y), 2), other, L.dp, L.sib).wait_recv()
    return [s0, s1, s2, s3, s4, s5, s6, s7]


def spread(L, src, dst, local_sem):
    ids = [None] + [L.new() for _ in range(2 * NZ - 1)]
    block = lambda s: pl.ds(mult(s * BLK, BLK), BLK)
    keep = pltpu.make_async_copy(src.at[block(L.sq)], dst.at[block(L.sq)], local_sem)

    def move(j, to, frm):
        return L.copy(ids[j], src.at[block(to)], dst.at[block(frm)], L.dp, to)

    def begin():
        keep.start()
        for j in range(1, 2 * NZ):
            L.go(lambda j=j: move(j, lax.rem(L.sq + j, 2 * NZ), L.sq))

    def finish():
        keep.wait()
        for j in range(1, 2 * NZ):
            move(j, L.sq, lax.rem(L.sq + 2 * NZ - j, 2 * NZ)).wait_recv()
    return begin, finish


def add_into(dst, rows0, cols, src, n):
    step = 48

    def one(i, _):
        here = pl.ds(mult(i * step, 16), step)
        there = pl.ds(mult(rows0 + i * step, 16), step)
        dst[there, cols] = (dst[there, cols].astype(jnp.float32) + src[here, :].astype(jnp.float32)).astype(jnp.bfloat16)
        return 0
    lax.fori_loop(0, n // step, one, 0)


def reduce_scratch(r, c, split):
    half, (a, b), big = c // 2, split, 2 * r
    bf = lambda *s: pltpu.VMEM(s, jnp.bfloat16)
    return [bf(32 * r, half), bf(8 * big, a), bf(4 * big, b), bf(4 * big, b), bf(4 * big, a), bf(4 * big, b),
            bf(3, big, half), bf(3, big, half), pltpu.VMEM((2, r, half), jnp.float32), pltpu.VMEM((r, half), jnp.float32)]


N_REDUCE = 14


def reduce(L, part, out, scratch, r, split):
    acc, a1, b1x, b1y, a2, b2, from_l, from_r, fin, got = scratch
    half = part.shape[1] // 2
    a, b = split
    big = 2 * r
    mine = pl.ds(mult(L.core * half, 128), half)
    other = pl.ds(mult((1 - L.core) * half, 128), half)
    ca, cb = pl.ds(0, a), pl.ds(a, b)
    quarter = lambda dp, n=1: pl.ds(mult(dp * NZ * big, 16), n * NZ * big)
    chip = lambda z: pl.ds(mult((L.dp * NZ + z) * big, 16), big)
    i0, ia1, ibx, iby, ia2, ib2, ifin = [L.new() for _ in range(7)]
    ir = [None] + [L.new() for _ in range(3)]
    il = [L.new() for _ in range(3)]
    q = lambda dp: dp * NZ * big
    other_y = quarter(2 * (1 - L.y), 2)

    core_copy = lambda: L.copy(i0, part.at[:, other], acc, L.dp, L.sib)
    a1_copy = lambda: L.copy(ia1, acc.at[other_y, ca], a1, L.dp_y, L.sq)
    bx_copy = lambda: L.copy(ibx, acc.at[quarter(L.dp_x), cb], b1x, L.dp_x, L.sq)
    by_copy = lambda: L.copy(iby, acc.at[quarter(3 - L.dp), cb], b1y, L.dp_x, L.sq)
    a2_copy = lambda: L.copy(ia2, acc.at[quarter(L.dp_x), ca], a2, L.dp_x, L.sq)
    b2_copy = lambda: L.copy(ib2, acc.at[quarter(L.dp_y), cb], b2, L.dp_y, L.sq)

    def s0():
        L.go(core_copy)

    def s1():
        core_copy().wait_recv()
        step = 48

        def one(i, _):
            here = pl.ds(mult(i * step, 16), step)
            acc[here, :] = (acc[here, :].astype(jnp.float32) + part[here, mine].astype(jnp.float32)).astype(jnp.bfloat16)
            return 0
        lax.fori_loop(0, acc.shape[0] // step, one, 0)
        L.go(a1_copy, bx_copy, by_copy)

    def s2():
        a1_copy().wait_recv()
        add_into(acc, q(2 * L.y), ca, a1, 8 * big)
        L.go(a2_copy)
        bx_copy().wait_recv()
        by_copy().wait_recv()
        add_into(acc, q(L.dp_y), cb, b1y, 4 * big)
        L.go(b2_copy)
        add_into(acc, q(L.dp), cb, b1x, 4 * big)

    def s3():
        a2_copy().wait_recv()
        add_into(acc, q(L.dp), ca, a2, 4 * big)
        b2_copy().wait_recv()
        add_into(acc, q(L.dp), cb, b2, 4 * big)

    full_cols = pl.ds(0, half)

    def hop_r(t, src):
        return L.copy(ir[t], src, from_l.at[t - 1], L.dp, L.sq + 2)

    def hop_l(t, src):
        return L.copy(il[t], src, from_r.at[t], L.dp, L.sq - 2)

    def merge(buf, k, t):
        buf[k] = (buf[k].astype(jnp.float32) + acc[chip(t), :].astype(jnp.float32)).astype(jnp.bfloat16)

    def line(s):
        @pl.when(L.z == s)
        def _():
            for t in range(NZ - 1, s, -1):
                if s == 0:
                    hop_r(t, acc.at[chip(t), full_cols]).start()
                else:
                    hop_r(t, from_l.at[t - 1]).wait_recv()
                    merge(from_l, t - 1, t)
                    hop_r(t, from_l.at[t - 1]).start()

        @pl.when(L.z == NZ - 1 - s)
        def _():
            for t in range(0, NZ - 1 - s):
                if s == 0:
                    hop_l(t, acc.at[chip(t), full_cols]).start()
                else:
                    hop_l(t, from_r.at[t]).wait_recv()
                    merge(from_r, t, t)
                    hop_l(t, from_r.at[t]).start()

        def drain():
            @pl.when(L.z == s)
            def _():
                for t in range(NZ - 1, s, -1):
                    hop_r(t, from_l.at[t - 1]).wait_send()

            @pl.when(L.z == NZ - 1 - s)
            def _():
                for t in range(0, NZ - 1 - s):
                    hop_l(t, from_r.at[t]).wait_send()
        L.drains.append(drain)

    fin_copy = lambda: L.copy(ifin, fin.at[1 - L.core], got, L.dp, L.sib)

    def s7():
        for z in range(NZ):
            @pl.when(L.z == z)
            def _(z=z):
                total = acc[chip(z), :].astype(jnp.float32)
                if z > 0:
                    hop_r(z, from_l.at[z - 1]).wait_recv()
                    total = total + from_l[z - 1].astype(jnp.float32)
                if z < NZ - 1:
                    hop_l(z, from_r.at[z]).wait_recv()
                    total = total + from_r[z].astype(jnp.float32)
                fin[...] = total.reshape(2, r, half)
        L.go(fin_copy)

    def s8():
        out[:, mine] = fin[L.core]
        fin_copy().wait_recv()
        out[:, other] = got[...]
    return [s0, s1, s2, s3] + [functools.partial(line, s) for s in range(3)] + [s7, s8]


def one_hot(slots, rows):
    row = lax.broadcasted_iota(jnp.int32, (rows, slots.shape[1]), 0)
    return jnp.where(slots == row, 1.0, 0.0).astype(jnp.bfloat16)


def head_lanes(width):
    row = lax.broadcasted_iota(jnp.int32, (2 * BLK, width), 0)
    lane = lax.rem(lax.broadcasted_iota(jnp.int32, (2 * BLK, width), 1), 128)
    return (row < BLK) == (lane < 64)


def dot(a, b, ca, cb):
    return lax.dot_general(a, b, (((ca,), (cb,)), ((), ())), preferred_element_type=jnp.float32)


def bdot(a, b, ca, cb):
    return lax.dot_general(a, b, (((ca,), (cb,)), ((0,), (0,))), preferred_element_type=jnp.float32)


BATCH = 8


def attend_fwd(scale, q_ref, k_ref, v_ref, perm_ref, mixed_ref, slot_ref, prob_ref, head_ref):
    nblk = q_ref.shape[0] // BLK
    share = BLK // nblk
    keep = head_lanes(384)
    for k in range(nblk):
        here = pl.ds(k * BLK, BLK)
        packed = jnp.concatenate([q_ref[here, :], k_ref[here, :], v_ref[here, :]], axis=1)
        table = one_hot(perm_ref[0, k:k + 1, :], BLK)
        moved = jnp.where(keep, dot(table, packed, 0, 0), 0.0).astype(jnp.bfloat16)
        slot_ref[0, :, :, pl.ds(k * share, share), :] = moved.reshape(2, nblk, share, 384)
    for h in range(2):
        for c in range(0, nblk, BATCH):
            cs = pl.ds(c, BATCH)
            q, kk, v = slot_ref[0, h, cs, :, 0:128], slot_ref[0, h, cs, :, 128:256], slot_ref[0, h, cs, :, 256:384]
            scores = bdot(q, kk, 2, 2) * scale
            e = jnp.exp(scores - jnp.max(scores, axis=-1, keepdims=True))
            probs = (e * (1.0 / jnp.sum(e, axis=-1, keepdims=True))).astype(jnp.bfloat16)
            prob_ref[0, h, cs] = probs
            head_ref[h, cs] = bdot(probs, v, 2, 1).astype(jnp.bfloat16)
    for k in range(nblk):
        table = one_hot(perm_ref[0, k:k + 1, :], BLK)
        back = head_ref[:, :, pl.ds(k * share, share), :].reshape(2 * BLK, BLK)
        mixed_ref[pl.ds(k * BLK, BLK), :] = dot(table, back, 1, 0).astype(jnp.bfloat16)


def attend_bwd(scale, dm_ref, perm_ref, slot_ref, prob_ref, dq_ref, dk_ref, dv_ref, sums_ref, up_ref, grad_ref):
    nblk = dm_ref.shape[0] // BLK
    share = BLK // nblk
    keep = head_lanes(128)
    for k in range(nblk):
        table = one_hot(perm_ref[0, k:k + 1, :], BLK)
        moved = jnp.where(keep, dot(table, dm_ref[pl.ds(k * BLK, BLK), :], 0, 0), 0.0).astype(jnp.bfloat16)
        up_ref[:, :, pl.ds(k * share, share), :] = moved.reshape(2, nblk, share, 128)
    for h in range(2):
        for c in range(0, nblk, BATCH):
            cs = pl.ds(c, BATCH)
            q, kk, v = slot_ref[0, h, cs, :, 0:128], slot_ref[0, h, cs, :, 128:256], slot_ref[0, h, cs, :, 256:384]
            probs, up = prob_ref[0, h, cs], up_ref[h, cs]
            dprobs = bdot(up, v, 2, 2)
            p32 = probs.astype(jnp.float32)
            pd = p32 * dprobs
            dscores = (pd - p32 * jnp.sum(pd, axis=-1, keepdims=True)).astype(jnp.bfloat16)
            grad_ref[h, cs, :, 0:128] = (bdot(dscores, kk, 2, 1) * scale).astype(jnp.bfloat16)
            grad_ref[h, cs, :, 128:256] = (bdot(dscores, q, 1, 1) * scale).astype(jnp.bfloat16)
            grad_ref[h, cs, :, 256:384] = bdot(probs, up, 1, 1).astype(jnp.bfloat16)
    total = jnp.zeros((1, 384), jnp.float32)
    for k in range(nblk):
        table = one_hot(perm_ref[0, k:k + 1, :], BLK)
        back = grad_ref[:, :, pl.ds(k * share, share), :].reshape(2 * BLK, 384)
        here = pl.ds(k * BLK, BLK)
        moved = dot(table, back, 1, 0)
        total = total + jnp.sum(moved, axis=0, keepdims=True)
        moved = moved.astype(jnp.bfloat16)
        dq_ref[here, :] = moved[:, 0:128]
        dk_ref[here, :] = moved[:, 128:256]
        dv_ref[here, :] = moved[:, 256:384]
    sums_ref[...] = jnp.broadcast_to(total, (8, 384))


SIZES = {"qkv": (24, 2560, (640, 640)), "out": (24, 768, (256, 128)), "up": (24, 3072, (768, 768)), "down": (96, 768, (128, 256))}
ALL = ("dp", "seq")
VM = pl.BlockSpec(memory_space=pltpu.VMEM)
BF = jnp.bfloat16
LIMIT = 60 * 2**20


def gather_kernel(names, na, *refs):
    n = len(names)
    ins, outs, sc = refs[:n + na], refs[n + na:2 * (n + na)], refs[2 * (n + na):]
    L = Links(sc[n], sc[n + 1])
    L.enter()
    progs = [gather(L, ins[i], outs[i], sc[i], SIZES[nm][0], SIZES[nm][2]) for i, nm in enumerate(names)]
    sp = [spread(L, ins[n + i], outs[n + i], sc[n + 2].at[i]) for i in range(na)]
    for k in range(8):
        for p in progs:
            p[k]()
        if k == 5:
            for b, _ in sp:
                b()
    for _, f in sp:
        f()
    L.drain()


def gather_call(names, shards, rows):
    na, n = len(rows), len(names)
    count = 15 * n + 7 * na
    outs = [jax.ShapeDtypeStruct((32 * SIZES[nm][0], SIZES[nm][1]), BF) for nm in names]
    outs += [jax.ShapeDtypeStruct(a.shape, BF) for a in rows]
    return pl.pallas_call(
        functools.partial(gather_kernel, names, na), out_shape=outs, in_specs=[VM] * (n + na), out_specs=[VM] * (n + na),
        scratch_shapes=[pltpu.VMEM((SIZES[nm][0], SIZES[nm][1] // 2), BF) for nm in names]
        + [pltpu.SemaphoreType.DMA((count,)), pltpu.SemaphoreType.DMA((count,)), pltpu.SemaphoreType.DMA((max(na, 1),))],
        compiler_params=pltpu.CompilerParams(collective_id=0, has_side_effects=True, vmem_limit_bytes=LIMIT),
    )(*shards, *rows)


def reduce_kernel(names, na, *refs):
    n = len(names)
    ins, outs, sc = refs[:n + na], refs[n + na:2 * (n + na)], refs[2 * (n + na):]
    L = Links(sc[10 * n], sc[10 * n + 1])
    L.enter()
    progs = [reduce(L, ins[i], outs[i], sc[10 * i:10 * i + 10], SIZES[nm][0], SIZES[nm][2]) for i, nm in enumerate(names)]
    sp = [spread(L, ins[n + i], outs[n + i], sc[10 * n + 2].at[i]) for i in range(na)]
    for b, _ in sp:
        b()
    for k in range(9):
        for p in progs:
            p[k]()
    for _, f in sp:
        f()
    L.drain()


def reduce_call(names, parts, rows, cid):
    na, n = len(rows), len(names)
    count = N_REDUCE * n + 7 * na
    outs = [jax.ShapeDtypeStruct(SIZES[nm][:2], jnp.float32) for nm in names]
    outs += [jax.ShapeDtypeStruct(a.shape, BF) for a in rows]
    return pl.pallas_call(
        functools.partial(reduce_kernel, names, na), out_shape=outs, in_specs=[VM] * (n + na), out_specs=[VM] * (n + na),
        scratch_shapes=sum([reduce_scratch(*SIZES[nm]) for nm in names], [])
        + [pltpu.SemaphoreType.DMA((count,)), pltpu.SemaphoreType.DMA((count,)), pltpu.SemaphoreType.DMA((max(na, 1),))],
        compiler_params=pltpu.CompilerParams(collective_id=cid, has_side_effects=True, vmem_limit_bytes=LIMIT),
    )(*parts, *rows)


def loop(n, body, hooks=()):
    def one(i, _):
        body(i)
        for at, stage in hooks:
            pl.when(i == at)(stage)
        return 0
    lax.fori_loop(0, n, one, 0)


def moments(v):
    mean = jnp.mean(v, axis=-1, keepdims=True)
    centred = v - mean
    inv = lax.rsqrt(jnp.mean(centred * centred, axis=-1, keepdims=True) + epsilon)
    return centred * inv, inv


TB = 256
FB = 512


def dense_kernel(mixed, x, w_out, w_up, down_shard, up_rows, vec, ub,
                 d_res, d_mixed, g_up, g_out, sums, ubsum, out_rows, r_down,
                 w_down, half_buf, n1, s1, low, act, gp, up, outb, dn, da, gd, *rest):
    red, (ss, rs, ls, cs) = rest[:10], rest[10:]
    rows_here, width = x.shape
    ff = w_up.shape[1]
    L = Links(ss, rs)
    L.enter()
    ga = gather(L, down_shard, w_down, half_buf, SIZES["down"][0], SIZES["down"][2])
    up_begin, up_finish = spread(L, up_rows, up, ls.at[0])
    out_begin, out_finish = spread(L, outb, out_rows, ls.at[1])
    rd = reduce(L, gd, r_down, red, SIZES["down"][0], SIZES["down"][2])
    sums[...] = jnp.zeros_like(sums)
    ubsum[...] = jnp.zeros_like(ubsum)
    row = lambda i: vec[i:i + 1, :]
    ga[0]()
    ga[1]()

    def first_half(m):
        here = pl.ds(mult(m * TB, TB), TB)
        r1 = x[here, :].astype(jnp.float32) + dot(mixed[here, :], w_out[...], 1, 0) + row(2)
        norm, inv = moments(r1)
        n1[here, :] = norm
        s1[here, :] = inv
        lo = (norm * row(4) + row(5)).astype(jnp.bfloat16)
        low[here, :] = lo
        for f in range(0, ff, FB):
            c = pl.ds(f, FB)
            wide = dot(lo, w_up[:, c], 1, 0) + ub[:, c]
            cdf = 0.5 + 0.5 * lax.erf(wide * 0.7071067811865476)
            act[here, c] = (wide * cdf).astype(jnp.bfloat16)
            gp[here, c] = (cdf + wide * (0.3989422804014327 * jnp.exp(-0.5 * wide * wide))).astype(jnp.bfloat16)

    loop(rows_here // TB, first_half, HOOK_A(ga, up_begin))
    for stage in REST_A(ga):
        stage()
    up_finish()

    def second_half(m):
        here = pl.ds(mult(m * TB, TB), TB)
        first = n1[here, :] * row(4) + row(5)
        r2 = first + dot(act[here, :], w_down[...], 1, 0) + row(3)
        n2, s2 = moments(r2)
        outb[here, :] = (n2 * row(6) + row(7)).astype(jnp.bfloat16)
        g = up[here, :].astype(jnp.float32)
        sums[4:5, :] += jnp.sum(g * n2, axis=0, keepdims=True)
        sums[5:6, :] += jnp.sum(g, axis=0, keepdims=True)
        d = norm_back(g, n2, s2, row(6))
        d_res[here, :] = d
        lo = d.astype(jnp.bfloat16)
        dn[here, :] = lo
        sums[1:2, :] += jnp.sum(lo.astype(jnp.float32), axis=0, keepdims=True)

    loop(rows_here // TB, second_half)
    out_begin()

    def grad_down(i):
        c = pl.ds(mult(i * FB, FB), FB)
        gd[c, :] = dot(act[:, c], dn[...], 0, 0).astype(jnp.bfloat16)

    loop(ff // FB, grad_down)
    rd[0]()

    def third(m):
        here = pl.ds(mult(m * TB, TB), TB)
        total = d_res[here, :]
        lo = dn[here, :]
        for f in range(0, ff, FB):
            c = pl.ds(f, FB)
            dw = (dot(lo, w_down[c, :], 1, 1) * gp[here, c].astype(jnp.float32)).astype(jnp.bfloat16)
            gp[here, c] = dw
            ubsum[0:1, c] += jnp.sum(dw.astype(jnp.float32), axis=0, keepdims=True)
            total = total + dot(dw, w_up[:, c], 1, 1)
        norm = n1[here, :]
        sums[2:3, :] += jnp.sum(total * norm, axis=0, keepdims=True)
        sums[3:4, :] += jnp.sum(total, axis=0, keepdims=True)
        d = norm_back(total, norm, s1[here, :], row(4))
        d_res[here, :] = d
        lo = d.astype(jnp.bfloat16)
        da[here, :] = lo
        sums[0:1, :] += jnp.sum(lo.astype(jnp.float32), axis=0, keepdims=True)
        d_mixed[here, :] = dot(lo, w_out[...], 1, 1).astype(jnp.bfloat16)

    loop(rows_here // TB, third, HOOK_C(rd))

    def grad_up(i):
        c = pl.ds(mult(i * FB, FB), FB)
        act[pl.ds(0, width), c] = dot(low[...], gp[:, c], 0, 0).astype(jnp.bfloat16)

    loop(ff // FB, grad_up, HOOK_D(rd))
    flush = pltpu.make_async_copy(act.at[pl.ds(0, width), :], g_up, cs.at[0])
    flush.start()
    g_out[...] = dot(mixed[...], da[...], 0, 0).astype(jnp.bfloat16)
    for stage in REST_D(rd):
        stage()
    out_finish()
    flush.wait()
    L.drain()


def HOOK_A(ga, up_begin):
    return [(0, ga[2]), (1, ga[3]), (2, ga[4]), (2, up_begin), (3, ga[5])]


def REST_A(ga):
    return ga[6:]


def HOOK_C(rd):
    return [(0, rd[1]), (1, rd[2]), (2, rd[3]), (3, rd[4])]


def HOOK_D(rd):
    return [(0, rd[5]), (2, rd[6]), (4, rd[7])]


def REST_D(rd):
    return rd[8:]


def dense_call(mixed, x, w_out, w_up, w_down, upstream, vec, ub):
    rows_here, width = x.shape
    ff = w_up.shape[1]
    r, cols, split = SIZES["down"]
    count = 15 + 14 + N_REDUCE
    f32 = lambda *s: jax.ShapeDtypeStruct(s, jnp.float32)
    bf = lambda *s: jax.ShapeDtypeStruct(s, BF)
    vbf = lambda *s: pltpu.VMEM(s, BF)
    vf = lambda *s: pltpu.VMEM(s, jnp.float32)
    hbm = pl.BlockSpec(memory_space=pl.ANY)
    return pl.pallas_call(
        dense_kernel,
        out_shape=[f32(rows_here, width), bf(rows_here, width), bf(width, ff), bf(width, width), f32(8, width), f32(8, ff),
                   bf(rows_here, width), f32(r, cols)],
        in_specs=[VM] * 5 + [hbm] + [VM] * 2,
        out_specs=[VM, VM, hbm] + [VM] * 5,
        scratch_shapes=[vbf(ff, width), vbf(r, cols // 2), vf(rows_here, width), vf(rows_here, 1), vbf(rows_here, width),
                        vbf(rows_here, ff), vbf(rows_here, ff), vbf(rows_here, width), vbf(rows_here, width),
                        vbf(rows_here, width), vbf(rows_here, width), vbf(ff, width)]
        + reduce_scratch(r, cols, split)
        + [pltpu.SemaphoreType.DMA((count,)), pltpu.SemaphoreType.DMA((count,)), pltpu.SemaphoreType.DMA((2,)),
           pltpu.SemaphoreType.DMA((1,))],
        compiler_params=pltpu.CompilerParams(collective_id=1, has_side_effects=True, vmem_limit_bytes=62 * 2**20),
    )(mixed, x, w_out, w_up, w_down, upstream, vec, ub)


def slot_rows(route, me):
    heads, n = route.shape[0], 2 * NZ
    per = route.reshape(heads, n, -1)
    mine = (per[:, 0] // BLK) == me
    place = jnp.cumsum(mine.astype(jnp.int32), axis=1) - 1
    pick = (mine[:, None, :] & (place[:, None, :] == jnp.arange(BLK)[None, :, None])).astype(BF)
    local = jnp.where(mine[:, None, :], per - me * BLK, 0).astype(BF)
    rows = jnp.einsum("hke,hse->hks", local, pick, preferred_element_type=jnp.float32).astype(jnp.int32)
    return rows.reshape(heads // 2, 2, n, BLK).transpose(0, 2, 1, 3).reshape(heads // 2, n, 2 * BLK)


def homes(tokens, w_qkv, w_out, w_up, w_down, vectors, up_bias, cluster_route, upstream):
    me = lax.axis_index("seq")
    rows_here, width = tokens.shape
    pairs = H // 2
    scale = (width // H) ** -0.5
    aux = jnp.pad(vectors.T, ((0, 0), (0, 248))) + jnp.pad(up_bias[None, :], ((0, 23), (8, 152)))
    full_qkv, full_out, full_up, x = gather_call(
        ("qkv", "out", "up"), [jnp.concatenate([w_qkv, aux], axis=1), w_out, w_up], [tokens])
    perm = slot_rows(cluster_route[0], me)
    vec = full_qkv[:, 2304:2312].T.astype(jnp.float32)
    ub = full_qkv[::24, 2312:2408].reshape(-1).astype(jnp.float32)
    w = full_qkv[:, :2304]
    shifts = jnp.concatenate([vec[0], jnp.zeros((width,), jnp.float32), vec[1]])
    qkv = (jnp.dot(x, w, preferred_element_type=jnp.float32) + shifts).astype(BF)
    col = lambda o: pl.BlockSpec((rows_here, 128), lambda p, o=o: (0, p + o))
    perm_spec = pl.BlockSpec((1, 8, 256), lambda p: (p, 0, 0))
    slot_spec = pl.BlockSpec((1, 2, 8, BLK, 384), lambda p: (p, 0, 0, 0, 0))
    prob_spec = pl.BlockSpec((1, 2, 8, BLK, BLK), lambda p: (p, 0, 0, 0, 0))
    mixed, slots, probs = pl.pallas_call(
        functools.partial(attend_fwd, scale), grid=(pairs,),
        out_shape=[jax.ShapeDtypeStruct((rows_here, width), BF), jax.ShapeDtypeStruct((pairs, 2, 8, BLK, 384), BF),
                   jax.ShapeDtypeStruct((pairs, 2, 8, BLK, BLK), BF)],
        in_specs=[col(0), col(pairs), col(2 * pairs), perm_spec], out_specs=[col(0), slot_spec, prob_spec],
        scratch_shapes=[pltpu.VMEM((2, 8, BLK, BLK), BF)],
        compiler_params=pltpu.CompilerParams(vmem_limit_bytes=LIMIT),
    )(qkv, qkv, qkv, perm)
    d_res, d_mixed, g_up, g_out, sums1, ubsum, out_rows, r_down = dense_call(mixed, x, full_out, full_up, w_down, upstream, vec, ub[None])
    dq, dk, dv, sums = pl.pallas_call(
        functools.partial(attend_bwd, scale), grid=(pairs,),
        out_shape=[jax.ShapeDtypeStruct((rows_here, width), BF)] * 3 + [jax.ShapeDtypeStruct((8 * pairs, 384), jnp.float32)],
        in_specs=[col(0), perm_spec, slot_spec, prob_spec], out_specs=[col(0)] * 3 + [pl.BlockSpec((8, 384), lambda p: (p, 0))],
        scratch_shapes=[pltpu.VMEM((2, 8, BLK, BLK), BF), pltpu.VMEM((2, 8, BLK, 384), BF)],
        compiler_params=pltpu.CompilerParams(vmem_limit_bytes=LIMIT),
    )(d_mixed, perm, slots, probs)
    sums = sums[::8].reshape(pairs, 3, 128)
    d_proj = jnp.concatenate([dq, dk, dv], axis=1)
    g_qkv = jnp.einsum("td,tf->df", x, d_proj, preferred_element_type=jnp.float32).astype(BF)
    gx = (jnp.einsum("tf,df->td", d_proj, w, preferred_element_type=jnp.float32) + d_res).astype(BF)
    g_vec = jnp.concatenate([sums[:, 0].reshape(1, -1), sums[:, 2].reshape(1, -1), sums1[:6]])
    g_aux = jnp.pad(g_vec.T, ((0, 0), (0, 248)))
    g_aux = g_aux.reshape(32, 24, 256) + jnp.pad(ubsum[0].reshape(32, 1, 96), ((0, 0), (0, 23), (8, 152)))
    part = jnp.concatenate([g_qkv, g_aux.reshape(768, 256).astype(BF)], axis=1)
    r_out, r_up, r_qkv, gx_rows = reduce_call(("out", "up", "qkv"), [g_out, g_up, part], [gx], 2)
    return (out_rows, gx_rows, r_qkv[:, :2304], r_out, r_up, r_down, r_qkv[:, 2304:2312].T, r_qkv[0, 2312:2408])


def solution(mesh):
    small = dict(mesh.shape) == {"dp": 4, "seq": 2 * NZ}
    rows = P(ALL, None)
    return jax.shard_map(
        homes if small else shards, mesh=mesh,
        in_specs=(rows,) * 5 + (P(None, ALL), P(ALL), P("dp", None, None), rows),
        out_specs=(rows,) * 6 + (P(None, ALL), P(ALL)),
        check_vma=False,
    )
```

```python
import functools

import jax
import jax.numpy as jnp
from jax import lax
from jax.experimental import pallas as pl
from jax.experimental.pallas import tpu as pltpu
from jax.sharding import PartitionSpec as P

H = 12
CL = 128


epsilon = 1e-06


def normalize(resid, norm_gain, norm_shift):
    average = jnp.mean(resid, axis=-1, keepdims=True)
    centred = resid - average
    spread = jnp.mean(centred * centred, axis=-1, keepdims=True)
    scaled = lax.rsqrt(spread + epsilon)
    normed = centred * scaled
    return (normed * norm_gain + norm_shift, normed, scaled)


def norm_back(grad_output, normed, scaled, norm_gain):
    grad_norm = grad_output * norm_gain
    first_term = jnp.mean(grad_norm, axis=-1, keepdims=True)
    second_term = jnp.mean(grad_norm * normed, axis=-1, keepdims=True)
    return scaled * (grad_norm - first_term - normed * second_term)


def exact_gelu(value):
    return jax.nn.gelu(value, approximate=False)


def order_table(sending):
    heads, rows_here = sending.shape
    columns = jnp.arange(rows_here, dtype=jnp.int32)[None, None, :]
    return (sending[:, :, None] == columns).astype(jnp.bfloat16)


def to_slots(source_rows, table):
    moved = jnp.einsum("hrs,skhe->rkhe", table, source_rows, preferred_element_type=jnp.float32)
    return moved.astype(jnp.bfloat16)


def to_tokens(source_rows, table):
    moved = jnp.einsum("hrs,rkhe->skhe", table, source_rows, preferred_element_type=jnp.float32)
    return moved.astype(jnp.bfloat16)


def cluster_scores(query_c, key_c, scale_factor):
    return (
        jnp.einsum("cahe,cbhe->hcab", query_c, key_c, preferred_element_type=jnp.float32)
        * scale_factor
    )


def shards(tokens, w_qkv, w_out, w_up, w_down, vectors, up_bias, cluster_route, upstream):
    lane_count = lax.axis_size("seq")
    lane_index = lax.axis_index("seq")
    wide_qkv, wide_out, wide_up, wide_down, wide_vectors, wide_bias = (
        lax.all_gather(w_qkv, ("dp", "seq"), axis=0, tiled=True),
        lax.all_gather(w_out, ("dp", "seq"), axis=0, tiled=True),
        lax.all_gather(w_up, ("dp", "seq"), axis=0, tiled=True),
        lax.all_gather(w_down, ("dp", "seq"), axis=0, tiled=True),
        lax.all_gather(vectors, ("dp", "seq"), axis=1, tiled=True),
        lax.all_gather(up_bias, ("dp", "seq"), axis=0, tiled=True),
    )
    rows_here = tokens.shape[0]
    model_width = tokens.shape[1]
    head_size = model_width // H
    portion = rows_here // lane_count
    clusters = rows_here // CL
    scale_factor = head_size ** (-0.5)
    vector_rows = wide_vectors.astype(jnp.float32)
    route_rows = cluster_route[0]
    by_target = lax.dynamic_slice_in_dim(route_rows, lane_index * rows_here, rows_here, 1)
    sending = jnp.swapaxes(by_target.reshape(H, lane_count, portion), 1, 2).reshape(H, rows_here)
    table = order_table(sending)
    projected = jnp.dot(tokens, wide_qkv, preferred_element_type=jnp.float32)
    shifts = jnp.concatenate(
        [vector_rows[0], jnp.zeros((model_width,), jnp.float32), vector_rows[1]]
    )
    projected = (projected + shifts).astype(jnp.bfloat16).reshape(rows_here, 3, H, head_size)
    outgoing = to_slots(projected, table)
    arrived = lax.all_to_all(
        outgoing.reshape(portion, lane_count, 3 * model_width),
        "seq",
        split_axis=1,
        concat_axis=1,
        tiled=True,
    )
    slot_qkv = arrived.reshape(clusters, CL, 3, H, head_size)
    query_c = slot_qkv[:, :, 0]
    key_c = slot_qkv[:, :, 1]
    value_c = slot_qkv[:, :, 2]
    scores = cluster_scores(query_c, key_c, scale_factor)
    row_peak = jnp.max(scores, axis=-1, keepdims=True)
    exponent = jnp.exp(scores - row_peak)
    row_total = jnp.sum(exponent, axis=-1, keepdims=True)
    soft_weights = exponent / row_total
    log_total = row_peak + jnp.log(row_total)
    heads_slot = jnp.einsum(
        "hcab,cbhe->cahe",
        soft_weights.astype(jnp.bfloat16),
        value_c,
        preferred_element_type=jnp.float32,
    ).astype(jnp.bfloat16)
    returned = lax.all_to_all(
        heads_slot.reshape(portion, lane_count, model_width),
        "seq",
        split_axis=1,
        concat_axis=1,
        tiled=True,
    )
    mixed_heads = to_tokens(returned.reshape(rows_here, 1, H, head_size), table).reshape(
        rows_here, model_width
    )
    attention = jnp.dot(mixed_heads, wide_out, preferred_element_type=jnp.float32) + vector_rows[2]
    first_norm, first_normed, first_scaled = normalize(
        tokens.astype(jnp.float32) + attention, vector_rows[4], vector_rows[5]
    )
    first_low = first_norm.astype(jnp.bfloat16)
    widened = jnp.dot(first_low, wide_up, preferred_element_type=jnp.float32) + wide_bias.astype(
        jnp.float32
    )
    activated, gelu_pull = jax.vjp(exact_gelu, widened)
    activated_low = activated.astype(jnp.bfloat16)
    narrowed = (
        jnp.dot(activated_low, wide_down, preferred_element_type=jnp.float32) + vector_rows[3]
    )
    output, second_normed, second_scaled = normalize(
        first_norm + narrowed, vector_rows[6], vector_rows[7]
    )
    back_qkv, back_out, back_up, back_down = (
        lax.all_gather(w_qkv, ("dp", "seq"), axis=0, tiled=True),
        lax.all_gather(w_out, ("dp", "seq"), axis=0, tiled=True),
        lax.all_gather(w_up, ("dp", "seq"), axis=0, tiled=True),
        lax.all_gather(w_down, ("dp", "seq"), axis=0, tiled=True),
    )
    grad_output = upstream.astype(jnp.float32)
    grad_gain_two = jnp.sum(grad_output * second_normed, axis=0)
    grad_shift_two = jnp.sum(grad_output, axis=0)
    grad_second = norm_back(grad_output, second_normed, second_scaled, vector_rows[6])
    grad_narrow = grad_second.astype(jnp.bfloat16)
    grad_down_w = jnp.einsum(
        "tf,td->fd", activated_low, grad_narrow, preferred_element_type=jnp.float32
    )
    grad_down_bias = jnp.sum(grad_narrow.astype(jnp.float32), axis=0)
    grad_active = jnp.einsum(
        "td,fd->tf", grad_narrow, back_down, preferred_element_type=jnp.float32
    )
    grad_wide = gelu_pull(grad_active)[0].astype(jnp.bfloat16)
    grad_up_w = jnp.einsum("td,tf->df", first_low, grad_wide, preferred_element_type=jnp.float32)
    grad_lift_bias = jnp.sum(grad_wide.astype(jnp.float32), axis=0)
    grad_first = grad_second + jnp.einsum(
        "tf,df->td", grad_wide, back_up, preferred_element_type=jnp.float32
    )
    grad_gain_one = jnp.sum(grad_first * first_normed, axis=0)
    grad_shift_one = jnp.sum(grad_first, axis=0)
    grad_resid = norm_back(grad_first, first_normed, first_scaled, vector_rows[4])
    grad_attn = grad_resid.astype(jnp.bfloat16)
    grad_out_w = jnp.einsum("td,te->de", mixed_heads, grad_attn, preferred_element_type=jnp.float32)
    grad_out_bias = jnp.sum(grad_attn.astype(jnp.float32), axis=0)
    grad_mixed = jnp.einsum(
        "te,de->td", grad_attn, back_out, preferred_element_type=jnp.float32
    ).astype(jnp.bfloat16)
    grad_sending = to_slots(grad_mixed.reshape(rows_here, 1, H, head_size), table)
    grad_slot = lax.all_to_all(
        grad_sending.reshape(portion, lane_count, model_width),
        "seq",
        split_axis=1,
        concat_axis=1,
        tiled=True,
    )
    grad_slot = grad_slot.reshape(clusters, CL, H, head_size)
    scores = cluster_scores(query_c, key_c, scale_factor)
    soft_weights = jnp.exp(scores - log_total)
    grad_soft = jnp.einsum(
        "cahe,cbhe->hcab", grad_slot, value_c, preferred_element_type=jnp.float32
    )
    inner_sum = jnp.sum(soft_weights * grad_soft, axis=-1, keepdims=True)
    grad_scores = (soft_weights * (grad_soft - inner_sum)).astype(jnp.bfloat16)
    grad_query = (
        jnp.einsum("hcab,cbhe->cahe", grad_scores, key_c, preferred_element_type=jnp.float32)
        * scale_factor
    )
    grad_key = (
        jnp.einsum("hcab,cahe->cbhe", grad_scores, query_c, preferred_element_type=jnp.float32)
        * scale_factor
    )
    grad_value = jnp.einsum(
        "hcab,cahe->cbhe",
        soft_weights.astype(jnp.bfloat16),
        grad_slot,
        preferred_element_type=jnp.float32,
    )
    grad_slots = jnp.stack([grad_query, grad_key, grad_value], axis=2).astype(jnp.bfloat16)
    came_back = lax.all_to_all(
        grad_slots.reshape(portion, lane_count, 3 * model_width),
        "seq",
        split_axis=1,
        concat_axis=1,
        tiled=True,
    )
    grad_proj = to_tokens(came_back.reshape(rows_here, 3, H, head_size), table).reshape(
        rows_here, 3 * model_width
    )
    grad_qkv_w = jnp.einsum("td,tf->df", tokens, grad_proj, preferred_element_type=jnp.float32)
    bias_sums = jnp.sum(grad_proj.astype(jnp.float32), axis=0).reshape(3, model_width)
    grad_tokens = (
        jnp.einsum("tf,df->td", grad_proj, back_qkv, preferred_element_type=jnp.float32)
        + grad_resid
    ).astype(jnp.bfloat16)
    grad_vector_rows = jnp.stack(
        [
            bias_sums[0],
            bias_sums[2],
            grad_out_bias,
            grad_down_bias,
            grad_gain_one,
            grad_shift_one,
            grad_gain_two,
            grad_shift_two,
        ]
    )
    shares = (
        lax.psum_scatter(grad_qkv_w, ("dp", "seq"), scatter_dimension=0, tiled=True),
        lax.psum_scatter(grad_out_w, ("dp", "seq"), scatter_dimension=0, tiled=True),
        lax.psum_scatter(grad_up_w, ("dp", "seq"), scatter_dimension=0, tiled=True),
        lax.psum_scatter(grad_down_w, ("dp", "seq"), scatter_dimension=0, tiled=True),
        lax.psum_scatter(grad_vector_rows, ("dp", "seq"), scatter_dimension=1, tiled=True),
        lax.psum_scatter(grad_lift_bias, ("dp", "seq"), scatter_dimension=0, tiled=True),
    )
    return (
        output.astype(jnp.bfloat16),
        grad_tokens,
        shares[0],
        shares[1],
        shares[2],
        shares[3],
        shares[4],
        shares[5],
    )


MESH = pl.DeviceIdType.MESH
NZ = 4
BLK = 128

class Links:
    def __init__(self, send_sems, recv_sems):
        self.send_sems, self.recv_sems, self.count, self.drains, self.key = send_sems, recv_sems, 0, {}, None
        self.dp, self.sq = lax.axis_index("dp"), lax.axis_index("seq")
        self.x, self.y = lax.rem(self.dp, 2), self.dp // 2
        self.core, self.z = lax.rem(self.sq, 2), self.sq // 2
        self.sib = self.sq + 1 - 2 * self.core
        self.dp_x = self.dp + 1 - 2 * self.x
        self.dp_y = self.dp + 2 - 4 * self.y

    def new(self):
        self.count += 1
        return self.count - 1

    def copy(self, i, src, dst, dp, sq):
        return pltpu.make_async_remote_copy(
            src_ref=src, dst_ref=dst, send_sem=self.send_sems.at[i], recv_sem=self.recv_sems.at[i],
            device_id=(dp, sq), device_id_type=MESH)

    def enter(self, near=True, line=True):
        barrier = pltpu.get_barrier_semaphore()
        n = 0
        if near:
            for dp in (self.dp_x, self.dp_y):
                pl.semaphore_signal(barrier, inc=1, device_id=(dp, self.sq), device_id_type=MESH)
                n += 1
        if line:
            for j in range(1, 2 * NZ):
                pl.semaphore_signal(barrier, inc=1, device_id=(self.dp, lax.rem(self.sq + j, 2 * NZ)), device_id_type=MESH)
                n += 1
        pl.semaphore_wait(barrier, n)

    def go(self, *makers):
        for make in makers:
            make().start()
            self.add(lambda make=make: make().wait_send())

    def drain(self, keys=None):
        for key in list(self.drains) if keys is None else keys:
            for d in self.drains.pop(key, []):
                d()

    def add(self, d):
        self.drains.setdefault(self.key, []).append(d)

    def under(self, key, stages):
        def run(stage):
            before, self.key = self.key, key
            stage()
            self.key = before
        return [functools.partial(run, stage) for stage in stages]


def mult(v, m):
    return pl.multiple_of(v, m)


def gather(L, shard, full, half_buf, r, split):
    half = full.shape[1] // 2
    a, b = split
    big = 2 * r
    mine = pl.ds(mult(L.core * half, 128), half)
    other = pl.ds(mult((1 - L.core) * half, 128), half)
    cols_a = pl.ds(mult(L.core * half, 128), a)
    cols_b = pl.ds(mult(L.core * half + a, 128), b)
    chip = lambda z: pl.ds(mult((L.dp * NZ + z) * big, 16), big)
    quarter = lambda dp, n=1: pl.ds(mult(dp * NZ * big, 16), n * NZ * big)
    i0 = L.new()
    fr = [None] + [L.new() for _ in range(3)]
    fl = [None] + [L.new() for _ in range(3)]
    ax, by, ay, bx0, bx1, c0, c1, c2 = [L.new() for _ in range(8)]
    first = lambda: L.copy(i0, shard.at[:, other], half_buf, L.dp, L.sib)

    def right(d, z0):
        return L.copy(fr[d], full.at[chip(z0), mine], full.at[chip(z0), mine], L.dp, L.sq + 2)

    def left(d, z0):
        return L.copy(fl[d], full.at[chip(z0), mine], full.at[chip(z0), mine], L.dp, L.sq - 2)

    def send_line(d):
        @pl.when((L.z >= d - 1) & (L.z < NZ - 1))
        def _():
            right(d, L.z - d + 1).start()

        @pl.when((L.z <= NZ - d) & (L.z > 0))
        def _():
            left(d, L.z + d - 1).start()

    def drain_line(d):
        @pl.when((L.z >= d - 1) & (L.z < NZ - 1))
        def _():
            right(d, L.z - d + 1).wait_send()

        @pl.when((L.z <= NZ - d) & (L.z > 0))
        def _():
            left(d, L.z + d - 1).wait_send()

    def recv_line(d):
        @pl.when(L.z >= d)
        def _():
            right(d, L.z - d).wait_recv()

        @pl.when(L.z + d <= NZ - 1)
        def _():
            left(d, L.z + d).wait_recv()

    def same(i, rows, cols, dp, sq):
        ref = full.at[rows, cols]
        return L.copy(i, ref, ref, dp, sq)

    def s0():
        L.go(first)

    def s1():
        first().wait_recv()
        own, got = shard[:, mine], half_buf[...]

        @pl.when(L.core == 0)
        def _():
            full[chip(L.z), mine] = jnp.concatenate([own, got], axis=0)

        @pl.when(L.core == 1)
        def _():
            full[chip(L.z), mine] = jnp.concatenate([got, own], axis=0)
        send_line(1)
        L.add(functools.partial(drain_line, 1))

    def s2():
        recv_line(1)
        send_line(2)
        L.add(functools.partial(drain_line, 2))

    def s3():
        recv_line(2)
        send_line(3)
        L.add(functools.partial(drain_line, 3))

    def s4():
        recv_line(3)
        q = lambda: quarter(L.dp)
        L.go(lambda: same(ax, q(), cols_a, L.dp_x, L.sq), lambda: same(by, q(), cols_b, L.dp_y, L.sq),
             lambda: same(c0, q(), mine, L.dp, L.sib))

    def s5():
        same(ax, quarter(L.dp_x), cols_a, L.dp_x, L.sq).wait_recv()
        L.go(lambda: same(ay, quarter(2 * L.y, 2), cols_a, L.dp_y, L.sq))
        same(by, quarter(L.dp_y), cols_b, L.dp_y, L.sq).wait_recv()
        L.go(lambda: same(bx0, quarter(L.dp), cols_b, L.dp_x, L.sq), lambda: same(bx1, quarter(L.dp_y), cols_b, L.dp_x, L.sq))

    def s6():
        same(bx0, quarter(L.dp_x), cols_b, L.dp_x, L.sq).wait_recv()
        L.go(lambda: same(c1, quarter(L.dp_x), mine, L.dp, L.sib))
        same(ay, quarter(2 * (1 - L.y), 2), cols_a, L.dp_y, L.sq).wait_recv()
        same(bx1, quarter(3 - L.dp), cols_b, L.dp_x, L.sq).wait_recv()
        L.go(lambda: same(c2, quarter(2 * (1 - L.y), 2), mine, L.dp, L.sib))

    def s7():
        same(c0, quarter(L.dp), other, L.dp, L.sib).wait_recv()
        same(c1, quarter(L.dp_x), other, L.dp, L.sib).wait_recv()
        same(c2, quarter(2 * (1 - L.y), 2), other, L.dp, L.sib).wait_recv()
    return [s0, s1, s2, s3, s4, s5, s6, s7]


def spread(L, src, dst, local_sem):
    ids = [None] + [L.new() for _ in range(2 * NZ - 1)]
    block = lambda s: pl.ds(mult(s * BLK, BLK), BLK)
    keep = pltpu.make_async_copy(src.at[block(L.sq)], dst.at[block(L.sq)], local_sem)

    def move(j, to, frm):
        return L.copy(ids[j], src.at[block(to)], dst.at[block(frm)], L.dp, to)

    def begin():
        keep.start()
        for j in range(1, 2 * NZ):
            L.go(lambda j=j: move(j, lax.rem(L.sq + j, 2 * NZ), L.sq))

    def finish():
        keep.wait()
        for j in range(1, 2 * NZ):
            move(j, L.sq, lax.rem(L.sq + 2 * NZ - j, 2 * NZ)).wait_recv()
    return begin, finish


def add_into(dst, rows0, cols, src, n):
    step = 48

    def one(i, _):
        here = pl.ds(mult(i * step, 16), step)
        there = pl.ds(mult(rows0 + i * step, 16), step)
        dst[there, cols] = (dst[there, cols].astype(jnp.float32) + src[here, :].astype(jnp.float32)).astype(jnp.bfloat16)
        return 0
    lax.fori_loop(0, n // step, one, 0)


def reduce_scratch(r, c, split):
    half, (a, b), big = c // 2, split, 2 * r
    bf = lambda *s: pltpu.VMEM(s, jnp.bfloat16)
    return [bf(32 * r, half), bf(8 * big, a), bf(4 * big, b), bf(4 * big, b), bf(4 * big, a), bf(4 * big, b),
            bf(3, big, half), bf(3, big, half), pltpu.VMEM((2, r, half), jnp.float32), pltpu.VMEM((r, half), jnp.float32)]


N_REDUCE = 14


def reduce(L, part, out, scratch, r, split, own=None, sem=None):
    acc, a1, b1x, b1y, a2, b2, from_l, from_r, fin, got = scratch
    half = part.shape[1] // 2
    a, b = split
    big = 2 * r
    mine = pl.ds(mult(L.core * half, 128), half)
    other = pl.ds(mult((1 - L.core) * half, 128), half)
    ca, cb = pl.ds(0, a), pl.ds(a, b)
    quarter = lambda dp, n=1: pl.ds(mult(dp * NZ * big, 16), n * NZ * big)
    chip = lambda z: pl.ds(mult((L.dp * NZ + z) * big, 16), big)
    i0, ia1, ibx, iby, ia2, ib2, ifin = [L.new() for _ in range(7)]
    ir = [None] + [L.new() for _ in range(3)]
    il = [L.new() for _ in range(3)]
    q = lambda dp: dp * NZ * big
    other_y = quarter(2 * (1 - L.y), 2)

    core_copy = lambda: L.copy(i0, part.at[:, other], acc, L.dp, L.sib)
    a1_copy = lambda: L.copy(ia1, acc.at[other_y, ca], a1, L.dp_y, L.sq)
    bx_copy = lambda: L.copy(ibx, acc.at[quarter(L.dp_x), cb], b1x, L.dp_x, L.sq)
    by_copy = lambda: L.copy(iby, acc.at[quarter(3 - L.dp), cb], b1y, L.dp_x, L.sq)
    a2_copy = lambda: L.copy(ia2, acc.at[quarter(L.dp_x), ca], a2, L.dp_x, L.sq)
    b2_copy = lambda: L.copy(ib2, acc.at[quarter(L.dp_y), cb], b2, L.dp_y, L.sq)

    mine_copy = lambda: pltpu.make_async_copy(part.at[:, mine], own, sem)

    def s0():
        L.go(core_copy)
        if own is not None:
            mine_copy().start()

    def s1():
        core_copy().wait_recv()
        if own is not None:
            mine_copy().wait()
        step = 48

        def one(i, _):
            here = pl.ds(mult(i * step, 16), step)
            add = part[here, mine] if own is None else own[here, :]
            acc[here, :] = (acc[here, :].astype(jnp.float32) + add.astype(jnp.float32)).astype(jnp.bfloat16)
            return 0
        lax.fori_loop(0, acc.shape[0] // step, one, 0)
        L.go(a1_copy, bx_copy, by_copy)

    def s2():
        a1_copy().wait_recv()
        add_into(acc, q(2 * L.y), ca, a1, 8 * big)
        L.go(a2_copy)
        bx_copy().wait_recv()
        by_copy().wait_recv()
        add_into(acc, q(L.dp_y), cb, b1y, 4 * big)
        L.go(b2_copy)
        add_into(acc, q(L.dp), cb, b1x, 4 * big)

    def s3():
        a2_copy().wait_recv()
        add_into(acc, q(L.dp), ca, a2, 4 * big)
        b2_copy().wait_recv()
        add_into(acc, q(L.dp), cb, b2, 4 * big)

    full_cols = pl.ds(0, half)

    def hop_r(t, src):
        return L.copy(ir[t], src, from_l.at[t - 1], L.dp, L.sq + 2)

    def hop_l(t, src):
        return L.copy(il[t], src, from_r.at[t], L.dp, L.sq - 2)

    def merge(buf, k, t):
        buf[k] = (buf[k].astype(jnp.float32) + acc[chip(t), :].astype(jnp.float32)).astype(jnp.bfloat16)

    def line(s):
        @pl.when(L.z == s)
        def _():
            for t in range(NZ - 1, s, -1):
                if s == 0:
                    hop_r(t, acc.at[chip(t), full_cols]).start()
                else:
                    hop_r(t, from_l.at[t - 1]).wait_recv()
                    merge(from_l, t - 1, t)
                    hop_r(t, from_l.at[t - 1]).start()

        @pl.when(L.z == NZ - 1 - s)
        def _():
            for t in range(0, NZ - 1 - s):
                if s == 0:
                    hop_l(t, acc.at[chip(t), full_cols]).start()
                else:
                    hop_l(t, from_r.at[t]).wait_recv()
                    merge(from_r, t, t)
                    hop_l(t, from_r.at[t]).start()

        def drain():
            @pl.when(L.z == s)
            def _():
                for t in range(NZ - 1, s, -1):
                    hop_r(t, from_l.at[t - 1]).wait_send()

            @pl.when(L.z == NZ - 1 - s)
            def _():
                for t in range(0, NZ - 1 - s):
                    hop_l(t, from_r.at[t]).wait_send()
        L.add(drain)

    fin_copy = lambda: L.copy(ifin, fin.at[1 - L.core], got, L.dp, L.sib)

    def s7():
        for z in range(NZ):
            @pl.when(L.z == z)
            def _(z=z):
                total = acc[chip(z), :].astype(jnp.float32)
                if z > 0:
                    hop_r(z, from_l.at[z - 1]).wait_recv()
                    total = total + from_l[z - 1].astype(jnp.float32)
                if z < NZ - 1:
                    hop_l(z, from_r.at[z]).wait_recv()
                    total = total + from_r[z].astype(jnp.float32)
                fin[...] = total.reshape(2, r, half)
        L.go(fin_copy)

    def s8():
        out[:, mine] = fin[L.core]
        fin_copy().wait_recv()
        out[:, other] = got[...]
    return [s0, s1, s2, s3] + [functools.partial(line, s) for s in range(3)] + [s7, s8]


def one_hot(slots, rows):
    row = lax.broadcasted_iota(jnp.int32, (rows, slots.shape[1]), 0)
    return jnp.where(slots == row, 1.0, 0.0).astype(jnp.bfloat16)


def head_lanes(width):
    row = lax.broadcasted_iota(jnp.int32, (2 * BLK, width), 0)
    lane = lax.rem(lax.broadcasted_iota(jnp.int32, (2 * BLK, width), 1), 128)
    return (row < BLK) == (lane < 64)


def dot(a, b, ca, cb):
    return lax.dot_general(a, b, (((ca,), (cb,)), ((), ())), preferred_element_type=jnp.float32)


def bdot(a, b, ca, cb):
    return lax.dot_general(a, b, (((ca,), (cb,)), ((0,), (0,))), preferred_element_type=jnp.float32)


BATCH = 8


SIZES = {"qkv": (24, 2560, (640, 640)), "out": (24, 768, (256, 128)), "up": (24, 3072, (768, 768)), "down": (96, 768, (128, 256))}
ALL = ("dp", "seq")
VM = pl.BlockSpec(memory_space=pltpu.VMEM)
BF = jnp.bfloat16
LIMIT = 60 * 2**20


def place_rows(route, perm, me):
    heads, n, size = route.shape
    base = me * BLK
    head_row = jnp.concatenate([route[h, 0:1, :] for h in range(heads)] + [jnp.full((16 - heads, size), -1, jnp.int32)], axis=0)
    mine = (head_row >= base) & (head_row < base + BLK)
    flags = jnp.where(mine, 1.0, 0.0).astype(jnp.bfloat16)
    before = []
    for c in range(0, size, 128):
        row = lax.broadcasted_iota(jnp.int32, (size, 128), 0)
        col = lax.broadcasted_iota(jnp.int32, (size, 128), 1) + c
        before.append(dot(flags, jnp.where(row < col, 1.0, 0.0).astype(jnp.bfloat16), 1, 0))
    slot = jnp.where(mine, jnp.concatenate(before, axis=1).astype(jnp.int32), -1)
    for h in range(heads):
        per = route[h]
        local = jnp.where((per >= base) & (per < base + BLK), per - base, 0).astype(jnp.float32).astype(jnp.bfloat16)
        pick = jnp.where(slot[h:h + 1, :] == lax.broadcasted_iota(jnp.int32, (BLK, size), 0), 1.0, 0.0).astype(jnp.bfloat16)
        perm[h // 2, :, pl.ds((h % 2) * BLK, BLK)] = dot(local, pick, 1, 1).astype(jnp.int32)


def front_pair(scale, qkv, width, perm, mixed, pool, head_ref, p, par):
    nblk = qkv.shape[0] // BLK
    share = BLK // nblk
    keep = head_lanes(384)
    cols = pl.ds(mult(par * 384, 128), 384)
    lane = lambda o: pl.ds(mult(par * 384 + o, 128), 128)
    col = lambda o: pl.ds(mult(p * 128 + o * width, 128), 128)
    half = nblk * BLK
    for k in range(nblk):
        here = pl.ds(k * BLK, BLK)
        packed = jnp.concatenate([qkv[here, col(0)], qkv[here, col(1)], qkv[here, col(2)]], axis=1)
        table = one_hot(perm[p, k:k + 1, :], BLK)
        moved = jnp.where(keep, dot(table, packed, 0, 0), 0.0).astype(jnp.bfloat16)
        for c in range(2 * nblk):
            pool[pl.ds(c * BLK + k * share, share), cols] = moved[c * share:(c + 1) * share]
    for h in range(2):
        rows = pl.ds(h * half, half)
        q, kk, v = [pool[rows, lane(o)].reshape(nblk, BLK, 128) for o in (0, 128, 256)]
        scores = bdot(q, kk, 2, 2) * scale
        e = jnp.exp(scores - jnp.max(scores, axis=-1, keepdims=True))
        probs = (e * (1.0 / jnp.sum(e, axis=-1, keepdims=True))).astype(jnp.bfloat16)
        pool[pl.ds(2 * half, half), pl.ds(mult((2 * par + h) * 128, 128), 128)] = probs.reshape(half, BLK)
        head_ref[rows, :] = bdot(probs, v, 2, 1).reshape(half, BLK).astype(jnp.bfloat16)
    for k in range(nblk):
        table = one_hot(perm[p, k:k + 1, :], BLK)
        back = jnp.concatenate([head_ref[pl.ds(c * BLK + k * share, share), :] for c in range(2 * nblk)], axis=0)
        mixed[pl.ds(k * BLK, BLK), col(0)] = dot(table, back, 1, 0).astype(jnp.bfloat16)


def loop(n, body, hooks=()):
    def one(i, _):
        body(i)
        for at, stage in hooks:
            pl.when(i == at)(stage)
        return 0
    lax.fori_loop(0, n, one, 0)


def moments(v):
    mean = jnp.mean(v, axis=-1, keepdims=True)
    centred = v - mean
    inv = lax.rsqrt(jnp.mean(centred * centred, axis=-1, keepdims=True) + epsilon)
    return centred * inv, inv


TB = 256
FB = 768


def front_kernel(scale, qkv_shard, out_shard, up_shard, down_shard, route, x_rows, up_rows,
                 x_home, w_home, slots, probs, perm, d_res, d_mixed, g_up, g_out, sums, ubsum, out_rows, r_down,
                 w_out, w_up, w_down, act, gp, x, mixed, n1, s1, low, up, outb, dn, gd, head_ref, vec, ub, auxf,
                 bq, bo, bu, bd, *rest):
    red, (ss, rs, ls, cs) = rest[:10], rest[10:]
    rows_here, width = x.shape
    ff = w_up.shape[1]
    pairs = perm.shape[0]
    w = gp.at[pl.ds(0, width), pl.ds(0, qkv_shard.shape[1])]
    da = up
    L = Links(ss, rs)
    L.enter()
    Q = L.under("qkv", gather(L, qkv_shard, w, bq, *SIZES["qkv"][::2]))
    O = L.under("out", gather(L, out_shard, w_out, bo, *SIZES["out"][::2]))
    U = gather(L, up_shard, w_up, bu, *SIZES["up"][::2])
    D = gather(L, down_shard, w_down, bd, *SIZES["down"][::2])
    x_begin, x_finish = spread(L, x_rows, x, ls.at[0])
    up_begin, up_finish = spread(L, up_rows, up, ls.at[1])
    out_begin, out_finish = spread(L, outb, out_rows, ls.at[2])
    R = reduce(L, gd, r_down, red, *SIZES["down"][::2])
    plan = PLAN(Q, O, U, D, x_begin, up_begin, R)
    row = lambda i: vec[i:i + 1, :]

    def run(stages):
        for stage in stages:
            stage()

    run(plan["start"])
    sums[...] = jnp.zeros_like(sums)
    ubsum[...] = jnp.zeros_like(ubsum)
    place_rows(route, perm, L.sq)
    run(plan["placed"])
    vec[...] = w[:, 2304:2432].astype(jnp.float32).T[0:8, :]
    auxf[...] = w[:, 2432:2560].astype(jnp.float32)
    step = ff // 32
    for i in range(32):
        ub[:, i * step:(i + 1) * step] = auxf[i * 24:i * 24 + 1, 0:step]
    w_flush = pltpu.make_async_copy(w, w_home, cs.at[0])
    w_flush.start()
    run(plan["weights"])
    x_finish()
    x_flush = pltpu.make_async_copy(x, x_home, cs.at[1])
    x_flush.start()

    def project(m):
        here = pl.ds(mult(m * TB, TB), TB)
        for j in range(3):
            c = pl.ds(j * width, width)
            r = dot(x[here, :], w[:, c], 1, 0)
            if j != 1:
                r = r + row(j // 2)
            act[here, c] = r.astype(jnp.bfloat16)

    loop(rows_here // TB, project, plan["project"])

    def kept(p, par):
        half = rows_here
        return [pltpu.make_async_copy(gd.at[pl.ds(0, 2 * half), pl.ds(mult(par * 384, 128), 384)], slots.at[p], cs.at[2 + 3 * par])] + [
            pltpu.make_async_copy(gd.at[pl.ds(2 * half, half), pl.ds(mult((2 * par + h) * 128, 128), 128)], probs.at[p, h],
                                  cs.at[3 + 3 * par + h]) for h in range(2)]

    def attend(p):
        par = lax.rem(p, 2)

        @pl.when(p >= 2)
        def _():
            for c in kept(p - 2, par):
                c.wait()
        front_pair(scale, act, width, perm, mixed, gd, head_ref, p, par)
        for c in kept(p, par):
            c.start()

    loop(pairs, attend, plan["attend"])
    w_flush.wait()
    L.drain(["qkv", "out"])

    def first_half(m):
        here = pl.ds(mult(m * TB, TB), TB)
        r1 = x[here, :].astype(jnp.float32) + dot(mixed[here, :], w_out[...], 1, 0) + row(2)
        norm, inv = moments(r1)
        n1[here, :] = norm
        s1[here, :] = inv
        lo = (norm * row(4) + row(5)).astype(jnp.bfloat16)
        low[here, :] = lo
        for f in range(0, ff, FB):
            c = pl.ds(f, FB)
            wide = dot(lo, w_up[:, c], 1, 0) + ub[:, c]
            cdf = 0.5 + 0.5 * lax.erf(wide * 0.7071067811865476)
            act[here, c] = (wide * cdf).astype(jnp.bfloat16)
            gp[here, c] = (cdf + wide * (0.3989422804014327 * jnp.exp(-0.5 * wide * wide))).astype(jnp.bfloat16)

    loop(rows_here // TB, first_half, plan["first"])
    run(plan["firsts"])
    up_finish()
    for p in range(pairs - 2, pairs):
        for c in kept(p, p % 2):
            c.wait()
    x_flush.wait()

    def second_half(m):
        here = pl.ds(mult(m * TB, TB), TB)
        first = n1[here, :] * row(4) + row(5)
        r2 = first + dot(act[here, :], w_down[...], 1, 0) + row(3)
        n2, s2 = moments(r2)
        outb[here, :] = (n2 * row(6) + row(7)).astype(jnp.bfloat16)
        g = up[here, :].astype(jnp.float32)
        sums[4:5, :] += jnp.sum(g * n2, axis=0, keepdims=True)
        sums[5:6, :] += jnp.sum(g, axis=0, keepdims=True)
        d = norm_back(g, n2, s2, row(6))
        d_res[here, :] = d
        lo = d.astype(jnp.bfloat16)
        dn[here, :] = lo
        sums[1:2, :] += jnp.sum(lo.astype(jnp.float32), axis=0, keepdims=True)

    loop(rows_here // TB, second_half)
    out_begin()

    def grad_down(i):
        c = pl.ds(mult(i * FB, FB), FB)
        gd[c, :] = dot(act[:, c], dn[...], 0, 0).astype(jnp.bfloat16)

    loop(ff // FB, grad_down)
    R[0]()

    def third(m):
        here = pl.ds(mult(m * TB, TB), TB)
        total = d_res[here, :]
        lo = dn[here, :]
        for f in range(0, ff, FB):
            c = pl.ds(f, FB)
            dw = (dot(lo, w_down[c, :], 1, 1) * gp[here, c].astype(jnp.float32)).astype(jnp.bfloat16)
            gp[here, c] = dw
            ubsum[0:1, c] += jnp.sum(dw.astype(jnp.float32), axis=0, keepdims=True)
            total = total + dot(dw, w_up[:, c], 1, 1)
        norm = n1[here, :]
        sums[2:3, :] += jnp.sum(total * norm, axis=0, keepdims=True)
        sums[3:4, :] += jnp.sum(total, axis=0, keepdims=True)
        d = norm_back(total, norm, s1[here, :], row(4))
        d_res[here, :] = d
        lo = d.astype(jnp.bfloat16)
        da[here, :] = lo
        sums[0:1, :] += jnp.sum(lo.astype(jnp.float32), axis=0, keepdims=True)
        x[here, :] = dot(lo, w_out[...], 1, 1).astype(jnp.bfloat16)

    loop(rows_here // TB, third, plan["third"])
    flush = [pltpu.make_async_copy(x, d_mixed, cs.at[0])]
    flush[0].start()

    def grad_up(i):
        c = pl.ds(mult(i * FB, FB), FB)
        act[pl.ds(0, width), c] = dot(low[...], gp[:, c], 0, 0).astype(jnp.bfloat16)

    loop(ff // FB, grad_up, plan["grad_up"])
    flush.append(pltpu.make_async_copy(act.at[pl.ds(0, width), :], g_up, cs.at[1]))
    flush[1].start()
    w_out[...] = dot(mixed[...], da[...], 0, 0).astype(jnp.bfloat16)
    flush.append(pltpu.make_async_copy(w_out, g_out, cs.at[2]))
    flush[2].start()
    run(plan["end"])
    out_finish()
    for f in flush:
        f.wait()
    L.drain()


def PLAN(Q, O, U, D, x_begin, up_begin, R):
    return {
        "start": [Q[0], O[0], U[0], D[0], Q[1], O[1], U[1], Q[2], O[2], U[2], Q[3], O[3], U[3], x_begin, Q[4], D[1]],
        "placed": [Q[5], O[4], U[4], Q[6], O[5], U[5], Q[7]],
        "weights": [O[6], U[6]],
        "project": [(3, D[2])],
        "attend": [(0, O[7]), (0, U[7]), (1, D[3]), (1, up_begin), (3, D[4])],
        "first": [(0, D[5]), (3, D[6])],
        "firsts": [D[7]],
        "third": [(0, R[1]), (3, R[2])],
        "grad_up": [(1, R[3]), (1, R[4])],
        "end": [R[5], R[6], R[7], R[8]],
    }


def front_call(scale, pairs, qkv_shard, w_out, w_up, w_down, route, tokens, upstream):
    rows_here, width = tokens.shape
    ff = w_up.shape[1]
    r, cols, split = SIZES["down"]
    count = 4 * 15 + 3 * 7 + N_REDUCE
    f32 = lambda *s: jax.ShapeDtypeStruct(s, jnp.float32)
    bf = lambda *s: jax.ShapeDtypeStruct(s, BF)
    vbf = lambda *s: pltpu.VMEM(s, BF)
    vf = lambda *s: pltpu.VMEM(s, jnp.float32)
    hbm = pl.BlockSpec(memory_space=pl.ANY)
    wq = qkv_shard.shape[1]
    return pl.pallas_call(
        functools.partial(front_kernel, scale),
        out_shape=[bf(rows_here, width), bf(width, wq), bf(pairs, 2 * rows_here, 384), bf(pairs, 2, rows_here, BLK),
                   jax.ShapeDtypeStruct((pairs, 2 * NZ, 2 * BLK), jnp.int32), f32(rows_here, width), bf(rows_here, width),
                   bf(width, ff), bf(width, width), f32(8, width), f32(8, ff), bf(rows_here, width), f32(r, cols)],
        in_specs=[VM] * 5 + [hbm] * 2,
        out_specs=[hbm] * 4 + [VM] * 2 + [hbm] * 3 + [VM] * 2 + [hbm, VM],
        scratch_shapes=[vbf(width, width), vbf(width, ff), vbf(ff, width), vbf(rows_here, ff), vbf(rows_here, ff),
                        vbf(rows_here, width), vbf(rows_here, width), vf(rows_here, width), vf(rows_here, 1)]
        + [vbf(rows_here, width)] * 4
        + [vbf(ff, width), vbf(2 * rows_here, BLK), vf(8, width), vf(1, ff), vf(width, BLK)]
        + [vbf(SIZES[n][0], SIZES[n][1] // 2) for n in ("qkv", "out", "up", "down")]
        + reduce_scratch(r, cols, split)
        + [pltpu.SemaphoreType.DMA((count,)), pltpu.SemaphoreType.DMA((count,)), pltpu.SemaphoreType.DMA((3,)),
           pltpu.SemaphoreType.DMA((8,))],
        compiler_params=pltpu.CompilerParams(collective_id=0, has_side_effects=True, vmem_limit_bytes=62 * 2**20),
    )(qkv_shard, w_out, w_up, w_down, route, tokens, upstream)


def back_pair(scale, dm_ref, perm_ref, slot_ref, prob_ref, up_ref, grad_ref, dp_ref):
    nblk = dm_ref.shape[0] // BLK
    share = BLK // nblk
    keep = head_lanes(128)
    for k in range(nblk):
        table = one_hot(perm_ref[0, k:k + 1, :], BLK)
        moved = jnp.where(keep, dot(table, dm_ref[pl.ds(k * BLK, BLK), :], 0, 0), 0.0).astype(jnp.bfloat16)
        up_ref[:, :, pl.ds(k * share, share), :] = moved.reshape(2, nblk, share, 128)
    for h in range(2):
        for c in range(0, nblk, BATCH):
            cs = pl.ds(c, BATCH)
            rows = pl.ds((h * nblk + c) * BLK, BATCH * BLK)
            q, kk, v = [slot_ref[0, rows, o:o + 128].reshape(BATCH, BLK, 128) for o in (0, 128, 256)]
            probs, up = prob_ref[0, h, pl.ds(c * BLK, BATCH * BLK), :].reshape(BATCH, BLK, BLK), up_ref[h, cs]
            dprobs = bdot(up, v, 2, 2)
            p32 = probs.astype(jnp.float32)
            pd = p32 * dprobs
            dscores = (pd - p32 * jnp.sum(pd, axis=-1, keepdims=True)).astype(jnp.bfloat16)
            grad_ref[h, cs, :, 0:128] = (bdot(dscores, kk, 2, 1) * scale).astype(jnp.bfloat16)
            grad_ref[h, cs, :, 128:256] = (bdot(dscores, q, 1, 1) * scale).astype(jnp.bfloat16)
            grad_ref[h, cs, :, 256:384] = bdot(probs, up, 1, 1).astype(jnp.bfloat16)
    total = jnp.zeros((1, 384), jnp.float32)
    for k in range(nblk):
        table = one_hot(perm_ref[0, k:k + 1, :], BLK)
        back = grad_ref[:, :, pl.ds(k * share, share), :].reshape(2 * BLK, 384)
        moved = dot(table, back, 1, 0)
        total = total + jnp.sum(moved, axis=0, keepdims=True)
        dp_ref[pl.ds(k * BLK, BLK), :] = moved.astype(jnp.bfloat16)
    return total


A_PAIRS = 4


def back_kernel(scale, pairs, dm_ref, perm_ref, slot_ref, prob_ref, x_hbm, w_hbm, dres_hbm, gup_hbm, gout_hbm, sums1, ubsum,
                r_qkv, r_up, r_out, gx_rows,
                up_ref, grad_ref, dp_ref, x, xt, w, gx, gxb, part_a, part_b, own_up, own_out, vsum, ubs, ra, rb, *rest):
    red = [rest[10 * i:10 * i + 10] for i in range(4)]
    ss, rs, ls, cs = rest[40:]
    width = x.shape[1]
    p = pl.program_id(0)
    L = Links(ss, rs)
    up = reduce(L, gup_hbm, r_up, red[0], *SIZES["up"][::2], own=own_up, sem=cs.at[0])
    ou = reduce(L, gout_hbm, r_out, red[1], *SIZES["out"][::2], own=own_out, sem=cs.at[1])
    qa = reduce(L, part_a, ra, red[2], 24, (384, 384))
    qb = reduce(L, part_b, rb, red[3], 24, (256, 256))
    begin, finish = spread(L, gxb, gx_rows, ls.at[0])
    loads = [(x_hbm, x, 2), (w_hbm, w, 3), (dres_hbm, gx, 4)]

    @pl.when(p == 0)
    def _():
        for a, b, i in loads:
            pltpu.make_async_copy(a, b, cs.at[i]).start()
        vsum[...] = jnp.zeros_like(vsum)
        vsum[2:8, :] = sums1[0:6, :]
        L.enter()
        ou[0]()
        up[0]()

    total = back_pair(scale, dm_ref, perm_ref, slot_ref, prob_ref, up_ref, grad_ref, dp_ref)
    col = lambda o: pl.ds(mult(p * 128 + o * width, 128), 128)
    vsum[0:1, col(0)] = total[:, 0:128]
    vsum[1:2, col(0)] = total[:, 256:384]

    @pl.when(p == 0)
    def _():
        for a, b, i in loads:
            pltpu.make_async_copy(a, b, cs.at[i]).wait()
        xt[...] = x[...].T

    dp = dp_ref[...]
    wp = jnp.concatenate([w[:, col(0)], w[:, col(1)], w[:, col(2)]], axis=1)
    for m in range(0, x.shape[0], 256):
        gx[m:m + 256, :] += dot(dp[m:m + 256], wp, 1, 1)
    g = dot(xt[...], dp, 1, 0).astype(jnp.bfloat16)

    @pl.when(p < A_PAIRS)
    def _():
        part_a[:, pl.ds(mult(p * 384, 128), 384)] = g

    @pl.when(p >= A_PAIRS)
    def _():
        part_b[:, pl.ds(mult((p - A_PAIRS) * 384, 128), 384)] = g

    for at, stage in BACK_PLAN(up, ou, qa):
        pl.when(p == at)(stage)

    @pl.when(p == pairs - 1)
    def _():
        gxb[...] = gx[...].astype(jnp.bfloat16)
        ubs[...] = jnp.zeros_like(ubs)
        step = ubsum.shape[1] // 32
        for i in range(32):
            ubs[i, 0:1, 0:step] = ubsum[0:1, i * step:(i + 1) * step]
        wide = jnp.concatenate([vsum[...], jnp.zeros((120, width), jnp.float32)], axis=0)
        part_b[:, 768:896] = wide.T.astype(jnp.bfloat16)
        part_b[:, 896:1024] = ubs[...].reshape(width, 128).astype(jnp.bfloat16)
        for stage in BACK_TAIL(up, ou, qa, qb, begin):
            stage()
        finish()
        for b in range(20):
            src = ra[:, b * 128:(b + 1) * 128] if b < 12 else rb[:, (b - 12) * 128:(b - 11) * 128]
            dst = (b // 3 + (b % 3) * pairs) if b < 18 else b
            r_qkv[:, dst * 128:(dst + 1) * 128] = src
        L.drain()


def BACK_PLAN(up, ou, qa):
    return [(0, ou[1]), (0, up[1]), (1, ou[2]), (1, up[2]), (2, ou[3]), (2, up[3]), (2, ou[4]), (2, up[4]),
            (3, qa[0]), (3, ou[5]), (3, up[5]), (4, ou[6]), (4, up[6]), (4, qa[1])]


def BACK_TAIL(up, ou, qa, qb, begin):
    return [qb[0], begin, qa[2], qb[1], ou[7], up[7], qa[3], qb[2], qa[4], qb[3], ou[8], up[8], qb[4], qa[5], qb[5],
            qa[6], qb[6], qa[7], qb[7], qa[8], qb[8]]


def back_call(scale, d_mixed, perm, slots, probs, x, w, d_res, g_up, g_out, sums1, ubsum):
    pairs = perm.shape[0]
    rows_here, width = x.shape
    count = 4 * N_REDUCE + 7
    hbm = pl.BlockSpec(memory_space=pl.ANY)
    vbf = lambda *s: pltpu.VMEM(s, BF)
    vf = lambda *s: pltpu.VMEM(s, jnp.float32)
    f32 = lambda *s: jax.ShapeDtypeStruct(s, jnp.float32)
    whole = lambda *s: pl.BlockSpec(s, lambda p: (0,) * len(s))
    r, cu = SIZES["up"][:2]
    co = SIZES["out"][1]
    return pl.pallas_call(
        functools.partial(back_kernel, scale, pairs), grid=(pairs,),
        out_shape=[f32(r, 2560), f32(r, cu), f32(r, co), jax.ShapeDtypeStruct((rows_here, width), BF)],
        in_specs=[pl.BlockSpec((rows_here, 128), lambda p: (0, p)), pl.BlockSpec((1, 8, 256), lambda p: (p, 0, 0)),
                  pl.BlockSpec((1, 2 * rows_here, 384), lambda p: (p, 0, 0)),
                  pl.BlockSpec((1, 2, rows_here, BLK), lambda p: (p, 0, 0, 0))] + [hbm] * 5
        + [whole(*sums1.shape), whole(*ubsum.shape)],
        out_specs=[whole(r, 2560), whole(r, cu), whole(r, co), hbm],
        scratch_shapes=[vbf(2, 8, BLK, BLK), vbf(2, 8, BLK, 384), vbf(rows_here, 384), vbf(rows_here, width),
                        vbf(width, rows_here), vbf(*w.shape), vf(rows_here, width), vbf(rows_here, width),
                        vbf(width, 1536), vbf(width, 1024), vbf(32 * r, cu // 2), vbf(32 * r, co // 2),
                        vf(8, width), vf(32, r, 128), vf(r, 1536), vf(r, 1024)]
        + reduce_scratch(*SIZES["up"]) + reduce_scratch(*SIZES["out"]) + reduce_scratch(r, 1536, (384, 384))
        + reduce_scratch(r, 1024, (256, 256))
        + [pltpu.SemaphoreType.DMA((count,)), pltpu.SemaphoreType.DMA((count,)), pltpu.SemaphoreType.DMA((1,)),
           pltpu.SemaphoreType.DMA((5,))],
        compiler_params=pltpu.CompilerParams(collective_id=1, has_side_effects=True, vmem_limit_bytes=LIMIT),
    )(d_mixed, perm, slots, probs, x, w, d_res, g_up, g_out, sums1, ubsum)


def homes(tokens, w_qkv, w_out, w_up, w_down, vectors, up_bias, cluster_route, upstream):
    pairs = H // 2
    scale = (tokens.shape[1] // H) ** -0.5
    step = up_bias.shape[0]
    aux = jnp.pad(vectors.T, ((0, 0), (0, 248))) + jnp.pad(up_bias[None, :], ((0, 23), (128, 128 - step)))
    x, w, slots, probs, perm, d_res, d_mixed, g_up, g_out, sums, ubsum, out_rows, r_down = front_call(
        scale, pairs, jnp.concatenate([w_qkv, aux], axis=1), w_out, w_up, w_down,
        cluster_route[0].reshape(H, 2 * NZ, -1), tokens, upstream)
    r_qkv, r_up, r_out, gx_rows = back_call(scale, d_mixed, perm, slots, probs, x, w, d_res, g_up, g_out, sums, ubsum)
    return (out_rows, gx_rows, r_qkv[:, :2304], r_out, r_up, r_down, r_qkv[:, 2304:2312].T, r_qkv[0, 2432:2432 + step])


def solution(mesh):
    small = dict(mesh.shape) == {"dp": 4, "seq": 2 * NZ}
    rows = P(ALL, None)
    return jax.shard_map(
        homes if small else shards, mesh=mesh,
        in_specs=(rows,) * 5 + (P(None, ALL), P(ALL), P("dp", None, None), rows),
        out_specs=(rows,) * 6 + (P(None, ALL), P(ALL)),
        check_vma=False,
    )
```

```python
import functools

import jax
import jax.numpy as jnp
from jax import lax
from jax.experimental import pallas as pl
from jax.experimental.pallas import tpu as pltpu
from jax.sharding import PartitionSpec as P

H = 12
CL = 128


epsilon = 1e-06


def normalize(resid, norm_gain, norm_shift):
    average = jnp.mean(resid, axis=-1, keepdims=True)
    centred = resid - average
    spread = jnp.mean(centred * centred, axis=-1, keepdims=True)
    scaled = lax.rsqrt(spread + epsilon)
    normed = centred * scaled
    return (normed * norm_gain + norm_shift, normed, scaled)


def norm_back(grad_output, normed, scaled, norm_gain):
    grad_norm = grad_output * norm_gain
    first_term = jnp.mean(grad_norm, axis=-1, keepdims=True)
    second_term = jnp.mean(grad_norm * normed, axis=-1, keepdims=True)
    return scaled * (grad_norm - first_term - normed * second_term)


def exact_gelu(value):
    return jax.nn.gelu(value, approximate=False)


def order_table(sending):
    heads, rows_here = sending.shape
    columns = jnp.arange(rows_here, dtype=jnp.int32)[None, None, :]
    return (sending[:, :, None] == columns).astype(jnp.bfloat16)


def to_slots(source_rows, table):
    moved = jnp.einsum("hrs,skhe->rkhe", table, source_rows, preferred_element_type=jnp.float32)
    return moved.astype(jnp.bfloat16)


def to_tokens(source_rows, table):
    moved = jnp.einsum("hrs,rkhe->skhe", table, source_rows, preferred_element_type=jnp.float32)
    return moved.astype(jnp.bfloat16)


def cluster_scores(query_c, key_c, scale_factor):
    return (
        jnp.einsum("cahe,cbhe->hcab", query_c, key_c, preferred_element_type=jnp.float32)
        * scale_factor
    )


def shards(tokens, w_qkv, w_out, w_up, w_down, vectors, up_bias, cluster_route, upstream):
    lane_count = lax.axis_size("seq")
    lane_index = lax.axis_index("seq")
    wide_qkv, wide_out, wide_up, wide_down, wide_vectors, wide_bias = (
        lax.all_gather(w_qkv, ("dp", "seq"), axis=0, tiled=True),
        lax.all_gather(w_out, ("dp", "seq"), axis=0, tiled=True),
        lax.all_gather(w_up, ("dp", "seq"), axis=0, tiled=True),
        lax.all_gather(w_down, ("dp", "seq"), axis=0, tiled=True),
        lax.all_gather(vectors, ("dp", "seq"), axis=1, tiled=True),
        lax.all_gather(up_bias, ("dp", "seq"), axis=0, tiled=True),
    )
    rows_here = tokens.shape[0]
    model_width = tokens.shape[1]
    head_size = model_width // H
    portion = rows_here // lane_count
    clusters = rows_here // CL
    scale_factor = head_size ** (-0.5)
    vector_rows = wide_vectors.astype(jnp.float32)
    route_rows = cluster_route[0]
    by_target = lax.dynamic_slice_in_dim(route_rows, lane_index * rows_here, rows_here, 1)
    sending = jnp.swapaxes(by_target.reshape(H, lane_count, portion), 1, 2).reshape(H, rows_here)
    table = order_table(sending)
    projected = jnp.dot(tokens, wide_qkv, preferred_element_type=jnp.float32)
    shifts = jnp.concatenate(
        [vector_rows[0], jnp.zeros((model_width,), jnp.float32), vector_rows[1]]
    )
    projected = (projected + shifts).astype(jnp.bfloat16).reshape(rows_here, 3, H, head_size)
    outgoing = to_slots(projected, table)
    arrived = lax.all_to_all(
        outgoing.reshape(portion, lane_count, 3 * model_width),
        "seq",
        split_axis=1,
        concat_axis=1,
        tiled=True,
    )
    slot_qkv = arrived.reshape(clusters, CL, 3, H, head_size)
    query_c = slot_qkv[:, :, 0]
    key_c = slot_qkv[:, :, 1]
    value_c = slot_qkv[:, :, 2]
    scores = cluster_scores(query_c, key_c, scale_factor)
    row_peak = jnp.max(scores, axis=-1, keepdims=True)
    exponent = jnp.exp(scores - row_peak)
    row_total = jnp.sum(exponent, axis=-1, keepdims=True)
    soft_weights = exponent / row_total
    log_total = row_peak + jnp.log(row_total)
    heads_slot = jnp.einsum(
        "hcab,cbhe->cahe",
        soft_weights.astype(jnp.bfloat16),
        value_c,
        preferred_element_type=jnp.float32,
    ).astype(jnp.bfloat16)
    returned = lax.all_to_all(
        heads_slot.reshape(portion, lane_count, model_width),
        "seq",
        split_axis=1,
        concat_axis=1,
        tiled=True,
    )
    mixed_heads = to_tokens(returned.reshape(rows_here, 1, H, head_size), table).reshape(
        rows_here, model_width
    )
    attention = jnp.dot(mixed_heads, wide_out, preferred_element_type=jnp.float32) + vector_rows[2]
    first_norm, first_normed, first_scaled = normalize(
        tokens.astype(jnp.float32) + attention, vector_rows[4], vector_rows[5]
    )
    first_low = first_norm.astype(jnp.bfloat16)
    widened = jnp.dot(first_low, wide_up, preferred_element_type=jnp.float32) + wide_bias.astype(
        jnp.float32
    )
    activated, gelu_pull = jax.vjp(exact_gelu, widened)
    activated_low = activated.astype(jnp.bfloat16)
    narrowed = (
        jnp.dot(activated_low, wide_down, preferred_element_type=jnp.float32) + vector_rows[3]
    )
    output, second_normed, second_scaled = normalize(
        first_norm + narrowed, vector_rows[6], vector_rows[7]
    )
    back_qkv, back_out, back_up, back_down = (
        lax.all_gather(w_qkv, ("dp", "seq"), axis=0, tiled=True),
        lax.all_gather(w_out, ("dp", "seq"), axis=0, tiled=True),
        lax.all_gather(w_up, ("dp", "seq"), axis=0, tiled=True),
        lax.all_gather(w_down, ("dp", "seq"), axis=0, tiled=True),
    )
    grad_output = upstream.astype(jnp.float32)
    grad_gain_two = jnp.sum(grad_output * second_normed, axis=0)
    grad_shift_two = jnp.sum(grad_output, axis=0)
    grad_second = norm_back(grad_output, second_normed, second_scaled, vector_rows[6])
    grad_narrow = grad_second.astype(jnp.bfloat16)
    grad_down_w = jnp.einsum(
        "tf,td->fd", activated_low, grad_narrow, preferred_element_type=jnp.float32
    )
    grad_down_bias = jnp.sum(grad_narrow.astype(jnp.float32), axis=0)
    grad_active = jnp.einsum(
        "td,fd->tf", grad_narrow, back_down, preferred_element_type=jnp.float32
    )
    grad_wide = gelu_pull(grad_active)[0].astype(jnp.bfloat16)
    grad_up_w = jnp.einsum("td,tf->df", first_low, grad_wide, preferred_element_type=jnp.float32)
    grad_lift_bias = jnp.sum(grad_wide.astype(jnp.float32), axis=0)
    grad_first = grad_second + jnp.einsum(
        "tf,df->td", grad_wide, back_up, preferred_element_type=jnp.float32
    )
    grad_gain_one = jnp.sum(grad_first * first_normed, axis=0)
    grad_shift_one = jnp.sum(grad_first, axis=0)
    grad_resid = norm_back(grad_first, first_normed, first_scaled, vector_rows[4])
    grad_attn = grad_resid.astype(jnp.bfloat16)
    grad_out_w = jnp.einsum("td,te->de", mixed_heads, grad_attn, preferred_element_type=jnp.float32)
    grad_out_bias = jnp.sum(grad_attn.astype(jnp.float32), axis=0)
    grad_mixed = jnp.einsum(
        "te,de->td", grad_attn, back_out, preferred_element_type=jnp.float32
    ).astype(jnp.bfloat16)
    grad_sending = to_slots(grad_mixed.reshape(rows_here, 1, H, head_size), table)
    grad_slot = lax.all_to_all(
        grad_sending.reshape(portion, lane_count, model_width),
        "seq",
        split_axis=1,
        concat_axis=1,
        tiled=True,
    )
    grad_slot = grad_slot.reshape(clusters, CL, H, head_size)
    scores = cluster_scores(query_c, key_c, scale_factor)
    soft_weights = jnp.exp(scores - log_total)
    grad_soft = jnp.einsum(
        "cahe,cbhe->hcab", grad_slot, value_c, preferred_element_type=jnp.float32
    )
    inner_sum = jnp.sum(soft_weights * grad_soft, axis=-1, keepdims=True)
    grad_scores = (soft_weights * (grad_soft - inner_sum)).astype(jnp.bfloat16)
    grad_query = (
        jnp.einsum("hcab,cbhe->cahe", grad_scores, key_c, preferred_element_type=jnp.float32)
        * scale_factor
    )
    grad_key = (
        jnp.einsum("hcab,cahe->cbhe", grad_scores, query_c, preferred_element_type=jnp.float32)
        * scale_factor
    )
    grad_value = jnp.einsum(
        "hcab,cahe->cbhe",
        soft_weights.astype(jnp.bfloat16),
        grad_slot,
        preferred_element_type=jnp.float32,
    )
    grad_slots = jnp.stack([grad_query, grad_key, grad_value], axis=2).astype(jnp.bfloat16)
    came_back = lax.all_to_all(
        grad_slots.reshape(portion, lane_count, 3 * model_width),
        "seq",
        split_axis=1,
        concat_axis=1,
        tiled=True,
    )
    grad_proj = to_tokens(came_back.reshape(rows_here, 3, H, head_size), table).reshape(
        rows_here, 3 * model_width
    )
    grad_qkv_w = jnp.einsum("td,tf->df", tokens, grad_proj, preferred_element_type=jnp.float32)
    bias_sums = jnp.sum(grad_proj.astype(jnp.float32), axis=0).reshape(3, model_width)
    grad_tokens = (
        jnp.einsum("tf,df->td", grad_proj, back_qkv, preferred_element_type=jnp.float32)
        + grad_resid
    ).astype(jnp.bfloat16)
    grad_vector_rows = jnp.stack(
        [
            bias_sums[0],
            bias_sums[2],
            grad_out_bias,
            grad_down_bias,
            grad_gain_one,
            grad_shift_one,
            grad_gain_two,
            grad_shift_two,
        ]
    )
    shares = (
        lax.psum_scatter(grad_qkv_w, ("dp", "seq"), scatter_dimension=0, tiled=True),
        lax.psum_scatter(grad_out_w, ("dp", "seq"), scatter_dimension=0, tiled=True),
        lax.psum_scatter(grad_up_w, ("dp", "seq"), scatter_dimension=0, tiled=True),
        lax.psum_scatter(grad_down_w, ("dp", "seq"), scatter_dimension=0, tiled=True),
        lax.psum_scatter(grad_vector_rows, ("dp", "seq"), scatter_dimension=1, tiled=True),
        lax.psum_scatter(grad_lift_bias, ("dp", "seq"), scatter_dimension=0, tiled=True),
    )
    return (
        output.astype(jnp.bfloat16),
        grad_tokens,
        shares[0],
        shares[1],
        shares[2],
        shares[3],
        shares[4],
        shares[5],
    )


MESH = pl.DeviceIdType.MESH
NZ = 4
BLK = 128

class Links:
    def __init__(self, send_sems, recv_sems):
        self.send_sems, self.recv_sems, self.count, self.drains, self.key = send_sems, recv_sems, 0, {}, None
        self.dp, self.sq = lax.axis_index("dp"), lax.axis_index("seq")
        self.x, self.y = lax.rem(self.dp, 2), self.dp // 2
        self.core, self.z = lax.rem(self.sq, 2), self.sq // 2
        self.sib = self.sq + 1 - 2 * self.core
        self.dp_x = self.dp + 1 - 2 * self.x
        self.dp_y = self.dp + 2 - 4 * self.y

    def peers(self):
        return jnp.where(self.core == 0, self.dp_x, self.dp_y), jnp.where(self.core == 0, self.dp_y, self.dp_x)

    def new(self):
        self.count += 1
        return self.count - 1

    def copy(self, i, src, dst, dp, sq):
        return pltpu.make_async_remote_copy(
            src_ref=src, dst_ref=dst, send_sem=self.send_sems.at[i], recv_sem=self.recv_sems.at[i],
            device_id=(dp, sq), device_id_type=MESH)

    def enter(self, near=True, line=True):
        barrier = pltpu.get_barrier_semaphore()
        n = 0
        if near:
            for dp in (self.dp_x, self.dp_y):
                pl.semaphore_signal(barrier, inc=1, device_id=(dp, self.sq), device_id_type=MESH)
                n += 1
        if line:
            for j in range(1, 2 * NZ):
                pl.semaphore_signal(barrier, inc=1, device_id=(self.dp, lax.rem(self.sq + j, 2 * NZ)), device_id_type=MESH)
                n += 1
        pl.semaphore_wait(barrier, n)

    def go(self, *makers):
        for make in makers:
            make().start()
            self.add(lambda make=make: make().wait_send())

    def drain(self, keys=None):
        for key in list(self.drains) if keys is None else keys:
            for d in self.drains.pop(key, []):
                d()

    def add(self, d):
        self.drains.setdefault(self.key, []).append(d)

    def under(self, key, stages):
        def run(stage):
            before, self.key = self.key, key
            stage()
            self.key = before
        return [functools.partial(run, stage) for stage in stages]


def mult(v, m):
    return pl.multiple_of(v, m)


def gather(L, shard, full, half_buf, r, split):
    half = full.shape[1] // 2
    a, b = split
    big = 2 * r
    mine = pl.ds(mult(L.core * half, 128), half)
    other = pl.ds(mult((1 - L.core) * half, 128), half)
    cols_a = pl.ds(mult(L.core * half, 128), a)
    cols_b = pl.ds(mult(L.core * half + a, 128), b)
    chip = lambda z: pl.ds(mult((L.dp * NZ + z) * big, 16), big)
    quarter = lambda dp, n=1: pl.ds(mult(dp * NZ * big, 16), n * NZ * big)
    i0 = L.new()
    fr = [None] + [L.new() for _ in range(3)]
    fl = [None] + [L.new() for _ in range(3)]
    a1, b1, a2, a3, b2, b3, c0, c1, c2 = [L.new() for _ in range(9)]
    fa, fb = L.peers()
    opposite = 3 - L.dp
    first = lambda: L.copy(i0, shard.at[:, other], half_buf, L.dp, L.sib)

    def right(d, z0):
        return L.copy(fr[d], full.at[chip(z0), mine], full.at[chip(z0), mine], L.dp, L.sq + 2)

    def left(d, z0):
        return L.copy(fl[d], full.at[chip(z0), mine], full.at[chip(z0), mine], L.dp, L.sq - 2)

    def send_line(d):
        @pl.when((L.z >= d - 1) & (L.z < NZ - 1))
        def _():
            right(d, L.z - d + 1).start()

        @pl.when((L.z <= NZ - d) & (L.z > 0))
        def _():
            left(d, L.z + d - 1).start()

    def drain_line(d):
        @pl.when((L.z >= d - 1) & (L.z < NZ - 1))
        def _():
            right(d, L.z - d + 1).wait_send()

        @pl.when((L.z <= NZ - d) & (L.z > 0))
        def _():
            left(d, L.z + d - 1).wait_send()

    def recv_line(d):
        @pl.when(L.z >= d)
        def _():
            right(d, L.z - d).wait_recv()

        @pl.when(L.z + d <= NZ - 1)
        def _():
            left(d, L.z + d).wait_recv()

    def same(i, rows, cols, dp, sq):
        ref = full.at[rows, cols]
        return L.copy(i, ref, ref, dp, sq)

    def s0():
        L.go(first)

    def s1():
        first().wait_recv()
        own, got = shard[:, mine], half_buf[...]

        @pl.when(L.core == 0)
        def _():
            full[chip(L.z), mine] = jnp.concatenate([own, got], axis=0)

        @pl.when(L.core == 1)
        def _():
            full[chip(L.z), mine] = jnp.concatenate([got, own], axis=0)
        send_line(1)
        L.add(functools.partial(drain_line, 1))

    def s2():
        recv_line(1)
        send_line(2)
        L.add(functools.partial(drain_line, 2))

    def s3():
        recv_line(2)
        send_line(3)
        L.add(functools.partial(drain_line, 3))

    def s4():
        recv_line(3)
        q = lambda: quarter(L.dp)
        L.go(lambda: same(a1, q(), cols_a, fa, L.sq), lambda: same(b1, q(), cols_b, fb, L.sq),
             lambda: same(c0, q(), mine, L.dp, L.sib))

    def s5():
        same(a1, quarter(fa), cols_a, fa, L.sq).wait_recv()
        L.go(lambda: same(a2, quarter(L.dp), cols_a, fb, L.sq), lambda: same(a3, quarter(fa), cols_a, fb, L.sq))
        same(b1, quarter(fb), cols_b, fb, L.sq).wait_recv()
        L.go(lambda: same(b2, quarter(L.dp), cols_b, fa, L.sq), lambda: same(b3, quarter(fb), cols_b, fa, L.sq))

    def s6():
        same(a2, quarter(fb), cols_a, fb, L.sq).wait_recv()
        same(b2, quarter(fa), cols_b, fa, L.sq).wait_recv()
        L.go(lambda: same(c1, quarter(L.dp_x), mine, L.dp, L.sib))
        same(a3, quarter(opposite), cols_a, fb, L.sq).wait_recv()
        same(b3, quarter(opposite), cols_b, fa, L.sq).wait_recv()
        L.go(lambda: same(c2, quarter(2 * (1 - L.y), 2), mine, L.dp, L.sib))

    def s7():
        same(c0, quarter(L.dp), other, L.dp, L.sib).wait_recv()
        same(c1, quarter(L.dp_x), other, L.dp, L.sib).wait_recv()
        same(c2, quarter(2 * (1 - L.y), 2), other, L.dp, L.sib).wait_recv()
    return [s0, s1, s2, s3, s4, s5, s6, s7]


def spread(L, src, dst, local_sem, parts=1):
    ids = [[L.new() for _ in range(2 * NZ - 1)] for _ in range(parts)]
    n = BLK // parts
    rows = lambda s, i: pl.ds(mult(s * BLK + i * n, n), n)

    def keep(i):
        return pltpu.make_async_copy(src.at[rows(L.sq, i)], dst.at[rows(L.sq, i)], local_sem.at[i])

    def move(i, j, to, frm):
        return L.copy(ids[i][j - 1], src.at[rows(to, i)], dst.at[rows(frm, i)], L.dp, to)

    def begin(i=0):
        keep(i).start()
        for j in range(1, 2 * NZ):
            L.go(lambda j=j: move(i, j, lax.rem(L.sq + j, 2 * NZ), L.sq))

    def finish():
        for i in range(parts):
            keep(i).wait()
            for j in range(1, 2 * NZ):
                move(i, j, L.sq, lax.rem(L.sq + 2 * NZ - j, 2 * NZ)).wait_recv()
    return begin, finish


def add_into(dst, rows0, cols, src, n):
    step = 48

    def one(i, _):
        here = pl.ds(mult(i * step, 16), step)
        there = pl.ds(mult(rows0 + i * step, 16), step)
        dst[there, cols] = (dst[there, cols].astype(jnp.float32) + src[here, :].astype(jnp.float32)).astype(jnp.bfloat16)
        return 0
    lax.fori_loop(0, n // step, one, 0)


def reduce_scratch(r, c, split):
    half, (a, b), big = c // 2, split, 2 * r
    bf = lambda *s: pltpu.VMEM(s, jnp.bfloat16)
    return [bf(32 * r, half), bf(2, 4 * big, a), bf(2, 4 * big, b), bf(4 * big, a), bf(4 * big, b),
            bf(3, big, half), bf(3, big, half), pltpu.VMEM((2, r, half), jnp.float32), pltpu.VMEM((r, half), jnp.float32)]


N_REDUCE = 15
N_GATHER = 16
N_SCRATCH = 9


def reduce(L, part, out, scratch, r, split, own=None, sem=None):
    acc, a1, b1, a2, b2, from_l, from_r, fin, got = scratch
    half = part.shape[1] // 2
    a, b = split
    big = 2 * r
    mine = pl.ds(mult(L.core * half, 128), half)
    other = pl.ds(mult((1 - L.core) * half, 128), half)
    ca, cb = pl.ds(0, a), pl.ds(a, b)
    quarter = lambda dp, n=1: pl.ds(mult(dp * NZ * big, 16), n * NZ * big)
    chip = lambda z: pl.ds(mult((L.dp * NZ + z) * big, 16), big)
    i0, ia0, ia1, ib0, ib1, ia2, ib2, ifin = [L.new() for _ in range(8)]
    fb, fa = L.peers()
    opposite = 3 - L.dp
    ir = [None] + [L.new() for _ in range(3)]
    il = [L.new() for _ in range(3)]
    q = lambda dp: dp * NZ * big

    core_copy = lambda: L.copy(i0, part.at[:, other], acc, L.dp, L.sib)
    def part_copy(i, dp, cols, to, peer):
        return L.copy(i, acc.at[quarter(dp), cols], to, peer, L.sq)

    a_copies = [lambda: part_copy(ia0, opposite, ca, a1.at[0], fa), lambda: part_copy(ia1, fa, ca, a1.at[1], fa)]
    b_copies = [lambda: part_copy(ib0, opposite, cb, b1.at[0], fb), lambda: part_copy(ib1, fb, cb, b1.at[1], fb)]
    a2_copy = lambda: part_copy(ia2, fb, ca, a2, fb)
    b2_copy = lambda: part_copy(ib2, fa, cb, b2, fa)
    mine_copy = lambda: pltpu.make_async_copy(part.at[:, mine], own, sem)

    def s0():
        L.go(core_copy)
        if own is not None:
            mine_copy().start()

    def s1():
        core_copy().wait_recv()
        if own is not None:
            mine_copy().wait()
        step = 48

        def one(i, _):
            here = pl.ds(mult(i * step, 16), step)
            add = part[here, mine] if own is None else own[here, :]
            acc[here, :] = (acc[here, :].astype(jnp.float32) + add.astype(jnp.float32)).astype(jnp.bfloat16)
            return 0
        lax.fori_loop(0, acc.shape[0] // step, one, 0)
        L.go(a_copies[0], b_copies[0], a_copies[1], b_copies[1])

    def s2():
        a_copies[0]().wait_recv()
        add_into(acc, q(fb), ca, a1.at[0], 4 * big)
        L.go(a2_copy)
        b_copies[0]().wait_recv()
        add_into(acc, q(fa), cb, b1.at[0], 4 * big)
        L.go(b2_copy)
        a_copies[1]().wait_recv()
        add_into(acc, q(L.dp), ca, a1.at[1], 4 * big)
        b_copies[1]().wait_recv()
        add_into(acc, q(L.dp), cb, b1.at[1], 4 * big)

    def s3():
        a2_copy().wait_recv()
        add_into(acc, q(L.dp), ca, a2, 4 * big)
        b2_copy().wait_recv()
        add_into(acc, q(L.dp), cb, b2, 4 * big)

    full_cols = pl.ds(0, half)

    def hop_r(t, src):
        return L.copy(ir[t], src, from_l.at[t - 1], L.dp, L.sq + 2)

    def hop_l(t, src):
        return L.copy(il[t], src, from_r.at[t], L.dp, L.sq - 2)

    def merge(buf, k, t):
        buf[k] = (buf[k].astype(jnp.float32) + acc[chip(t), :].astype(jnp.float32)).astype(jnp.bfloat16)

    def line(s):
        @pl.when(L.z == s)
        def _():
            for t in range(NZ - 1, s, -1):
                if s == 0:
                    hop_r(t, acc.at[chip(t), full_cols]).start()
                else:
                    hop_r(t, from_l.at[t - 1]).wait_recv()
                    merge(from_l, t - 1, t)
                    hop_r(t, from_l.at[t - 1]).start()

        @pl.when(L.z == NZ - 1 - s)
        def _():
            for t in range(0, NZ - 1 - s):
                if s == 0:
                    hop_l(t, acc.at[chip(t), full_cols]).start()
                else:
                    hop_l(t, from_r.at[t]).wait_recv()
                    merge(from_r, t, t)
                    hop_l(t, from_r.at[t]).start()

        def drain():
            @pl.when(L.z == s)
            def _():
                for t in range(NZ - 1, s, -1):
                    hop_r(t, from_l.at[t - 1]).wait_send()

            @pl.when(L.z == NZ - 1 - s)
            def _():
                for t in range(0, NZ - 1 - s):
                    hop_l(t, from_r.at[t]).wait_send()
        L.add(drain)

    fin_copy = lambda: L.copy(ifin, fin.at[1 - L.core], got, L.dp, L.sib)

    def s7():
        for z in range(NZ):
            @pl.when(L.z == z)
            def _(z=z):
                total = acc[chip(z), :].astype(jnp.float32)
                if z > 0:
                    hop_r(z, from_l.at[z - 1]).wait_recv()
                    total = total + from_l[z - 1].astype(jnp.float32)
                if z < NZ - 1:
                    hop_l(z, from_r.at[z]).wait_recv()
                    total = total + from_r[z].astype(jnp.float32)
                fin[...] = total.reshape(2, r, half)
        L.go(fin_copy)

    def s8():
        out[:, mine] = fin[L.core]
        fin_copy().wait_recv()
        out[:, other] = got[...]
    return [s0, s1, s2, s3] + [functools.partial(line, s) for s in range(3)] + [s7, s8]


def one_hot(slots, rows):
    row = lax.broadcasted_iota(jnp.int32, (rows, slots.shape[1]), 0)
    return jnp.where(slots == row, 1.0, 0.0).astype(jnp.bfloat16)


def head_lanes(width):
    row = lax.broadcasted_iota(jnp.int32, (2 * BLK, width), 0)
    lane = lax.rem(lax.broadcasted_iota(jnp.int32, (2 * BLK, width), 1), 128)
    return (row < BLK) == (lane < 64)


def dot(a, b, ca, cb):
    return lax.dot_general(a, b, (((ca,), (cb,)), ((), ())), preferred_element_type=jnp.float32)


def bdot(a, b, ca, cb):
    return lax.dot_general(a, b, (((ca,), (cb,)), ((0,), (0,))), preferred_element_type=jnp.float32)


BATCH = 8


SIZES = {"qkv": (24, 2560, (640, 640)), "out": (24, 768, (256, 128)), "up": (24, 3072, (768, 768)), "down": (96, 768, (128, 256))}
ALL = ("dp", "seq")
VM = pl.BlockSpec(memory_space=pltpu.VMEM)
BF = jnp.bfloat16
LIMIT = 60 * 2**20


def place_rows(route, perm, me):
    heads, n = route.shape[1], 2 * NZ
    size = route.shape[2] // n
    base = me * BLK
    head_row = jnp.concatenate([route[0, :, 0:size], jnp.full((16 - heads, size), -1, jnp.int32)], axis=0)
    mine = (head_row >= base) & (head_row < base + BLK)
    flags = jnp.where(mine, 1.0, 0.0).astype(jnp.bfloat16)
    before = []
    for c in range(0, size, 128):
        row = lax.broadcasted_iota(jnp.int32, (size, 128), 0)
        col = lax.broadcasted_iota(jnp.int32, (size, 128), 1) + c
        before.append(dot(flags, jnp.where(row < col, 1.0, 0.0).astype(jnp.bfloat16), 1, 0))
    slot = jnp.where(mine, jnp.concatenate(before, axis=1).astype(jnp.int32), -1)
    for h in range(heads):
        per = jnp.concatenate([route[0, h:h + 1, k * size:(k + 1) * size] for k in range(n)], axis=0)
        local = jnp.where((per >= base) & (per < base + BLK), per - base, 0).astype(jnp.float32).astype(jnp.bfloat16)
        pick = jnp.where(slot[h:h + 1, :] == lax.broadcasted_iota(jnp.int32, (BLK, size), 0), 1.0, 0.0).astype(jnp.bfloat16)
        perm[h // 2, :, pl.ds((h % 2) * BLK, BLK)] = dot(local, pick, 1, 1).astype(jnp.int32)


def front_pair(scale, qkv, width, perm, mixed, pool, head_ref, p, par):
    nblk = qkv.shape[0] // BLK
    share = BLK // nblk
    keep = head_lanes(384)
    cols = pl.ds(mult(par * 384, 128), 384)
    lane = lambda o: pl.ds(mult(par * 384 + o, 128), 128)
    col = lambda o: pl.ds(mult(p * 128 + o * width, 128), 128)
    half = nblk * BLK
    for k in range(nblk):
        here = pl.ds(k * BLK, BLK)
        packed = jnp.concatenate([qkv[here, col(0)], qkv[here, col(1)], qkv[here, col(2)]], axis=1)
        table = one_hot(perm[p, k:k + 1, :], BLK)
        moved = jnp.where(keep, dot(table, packed, 0, 0), 0.0).astype(jnp.bfloat16)
        for c in range(2 * nblk):
            pool[pl.ds(c * BLK + k * share, share), cols] = moved[c * share:(c + 1) * share]
    for h in range(2):
        rows = pl.ds(h * half, half)
        q, kk, v = [pool[rows, lane(o)].reshape(nblk, BLK, 128) for o in (0, 128, 256)]
        scores = bdot(q, kk, 2, 2) * scale
        e = jnp.exp(scores - jnp.max(scores, axis=-1, keepdims=True))
        probs = (e * (1.0 / jnp.sum(e, axis=-1, keepdims=True))).astype(jnp.bfloat16)
        pool[pl.ds(2 * half, half), pl.ds(mult((2 * par + h) * 128, 128), 128)] = probs.reshape(half, BLK)
        head_ref[rows, :] = bdot(probs, v, 2, 1).reshape(half, BLK).astype(jnp.bfloat16)
    for k in range(nblk):
        table = one_hot(perm[p, k:k + 1, :], BLK)
        back = jnp.concatenate([head_ref[pl.ds(c * BLK + k * share, share), :] for c in range(2 * nblk)], axis=0)
        mixed[pl.ds(k * BLK, BLK), col(0)] = dot(table, back, 1, 0).astype(jnp.bfloat16)


def loop(n, body, hooks=()):
    def one(i, _):
        body(i)
        for at, stage in hooks:
            pl.when(i == at)(stage)
        return 0
    lax.fori_loop(0, n, one, 0)


def moments(v):
    mean = jnp.mean(v, axis=-1, keepdims=True)
    centred = v - mean
    inv = lax.rsqrt(jnp.mean(centred * centred, axis=-1, keepdims=True) + epsilon)
    return centred * inv, inv


TB = 256
FB = 768


def front_kernel(scale, w_shard, out_shard, up_shard, down_shard, vec_shard, ub_shard, route, x_rows, up_rows,
                 x_home, w_home, slots, probs, d_proj, gx, g_up, g_out, sums, ubsum, out_rows, r_down,
                 w_out, w_up, w_down, act, gp, x, mixed, n1, s1, low, up, outb, dn, gd, head_ref, vec, ub, auxf,
                 bq, bo, bu, bd, qkv_shard, perm, d_res, *rest):
    red, (ss, rs, ls, cs) = rest[:N_SCRATCH], rest[N_SCRATCH:]
    rows_here, width = x.shape
    ff = w_up.shape[1]
    pairs = perm.shape[0]
    w = gp.at[pl.ds(0, width), pl.ds(0, qkv_shard.shape[1])]
    da = up
    L = Links(ss, rs)
    r = w_shard.shape[0]
    nv, step = vec_shard.shape[0], ub_shard.shape[1]
    qkv_shard[:, 0:3 * width] = w_shard[...]
    auxf[...] = jnp.zeros_like(auxf)
    auxf[0:nv, 0:r] = vec_shard[...].astype(jnp.float32)
    qkv_shard[:, 3 * width:3 * width + 128] = auxf[0:128, :].T[0:r, :].astype(jnp.bfloat16)
    auxf[0:nv, :] = jnp.zeros((nv, 128), jnp.float32)
    auxf[0:1, 0:step] = ub_shard[...].astype(jnp.float32)
    qkv_shard[:, 3 * width + 128:3 * width + 256] = auxf[0:r, :].astype(jnp.bfloat16)
    L.enter()
    Q = L.under("qkv", gather(L, qkv_shard, w, bq, *SIZES["qkv"][::2]))
    O = L.under("out", gather(L, out_shard, w_out, bo, *SIZES["out"][::2]))
    U = gather(L, up_shard, w_up, bu, *SIZES["up"][::2])
    D = L.under("down", gather(L, down_shard, w_down, bd, *SIZES["down"][::2]))
    x_begin, x_finish = spread(L, x_rows, x, ls.at[0])
    up_begin, up_finish = spread(L, up_rows, up, ls.at[1])
    out_begin, out_finish = spread(L, outb, out_rows, ls.at[2])
    R = reduce(L, gd, r_down, red, *SIZES["down"][::2])
    R = L.under("sum", R[:1]) + R[1:]
    plan = PLAN(Q, O, U, D, x_begin, up_begin, R)
    row = lambda i: vec[i:i + 1, :]

    def run(stages):
        for stage in stages:
            stage()

    run(plan["start"])
    sums[...] = jnp.zeros_like(sums)
    ubsum[...] = jnp.zeros_like(ubsum)
    place_rows(route, perm, L.sq)
    run(plan["placed"])
    vec[...] = w[:, 2304:2432].astype(jnp.float32).T[0:8, :]
    auxf[...] = w[:, 2432:2560].astype(jnp.float32)
    for i in range(ff // step):
        ub[:, i * step:(i + 1) * step] = auxf[i * r:i * r + 1, 0:step]
    w_flush = pltpu.make_async_copy(w, w_home, cs.at[0])
    w_flush.start()
    run(plan["weights"])
    x_finish()
    x_flush = pltpu.make_async_copy(x, x_home, cs.at[1])
    x_flush.start()

    def project(m):
        here = pl.ds(mult(m * TB, TB), TB)
        for j in range(3):
            c = pl.ds(j * width, width)
            r = dot(x[here, :], w[:, c], 1, 0)
            if j != 1:
                r = r + row(j // 2)
            act[here, c] = r.astype(jnp.bfloat16)

    loop(rows_here // TB, project, plan["project"])

    def kept(p, par):
        half = rows_here
        return [pltpu.make_async_copy(gd.at[pl.ds(0, 2 * half), pl.ds(mult(par * 384, 128), 384)], slots.at[p], cs.at[2 + 3 * par])] + [
            pltpu.make_async_copy(gd.at[pl.ds(2 * half, half), pl.ds(mult((2 * par + h) * 128, 128), 128)], probs.at[p, h],
                                  cs.at[3 + 3 * par + h]) for h in range(2)]

    def back_in(p, par):
        half = rows_here
        return [pltpu.make_async_copy(slots.at[p], w_down.at[pl.ds(0, 2 * half), pl.ds(mult(par * 384, 128), 384)], cs.at[2 + 3 * par])] + [
            pltpu.make_async_copy(probs.at[p, h], w_down.at[pl.ds(2 * half, half), pl.ds(mult((2 * par + h) * 128, 128), 128)],
                                  cs.at[3 + 3 * par + h]) for h in range(2)]

    def attend(p):
        par = lax.rem(p, 2)

        @pl.when(p >= 2)
        def _():
            for c in kept(p - 2, par):
                c.wait()
        front_pair(scale, act, width, perm, mixed, gd, head_ref, p, par)
        for c in kept(p, par):
            c.start()

    loop(pairs, attend, plan["attend"])
    w_flush.wait()
    L.drain(["qkv", "out"])

    def first_half(m):
        here = pl.ds(mult(m * TB, TB), TB)
        r1 = x[here, :].astype(jnp.float32) + dot(mixed[here, :], w_out[...], 1, 0) + row(2)
        norm, inv = moments(r1)
        n1[here, :] = norm
        s1[here, :] = inv
        lo = (norm * row(4) + row(5)).astype(jnp.bfloat16)
        low[here, :] = lo
        for f in range(0, ff, FB):
            c = pl.ds(f, FB)
            wide = dot(lo, w_up[:, c], 1, 0) + ub[:, c]
            cdf = 0.5 + 0.5 * lax.erf(wide * 0.7071067811865476)
            act[here, c] = (wide * cdf).astype(jnp.bfloat16)
            gp[here, c] = (cdf + wide * (0.3989422804014327 * jnp.exp(-0.5 * wide * wide))).astype(jnp.bfloat16)

    loop(rows_here // TB, first_half, plan["first"])
    run(plan["firsts"])
    up_finish()
    for p in range(pairs - 2, pairs):
        for c in kept(p, p % 2):
            c.wait()
    x_flush.wait()

    def second_half(m):
        here = pl.ds(mult(m * TB, TB), TB)
        first = n1[here, :] * row(4) + row(5)
        r2 = first + dot(act[here, :], w_down[...], 1, 0) + row(3)
        n2, s2 = moments(r2)
        outb[here, :] = (n2 * row(6) + row(7)).astype(jnp.bfloat16)
        g = up[here, :].astype(jnp.float32)
        sums[4:5, :] += jnp.sum(g * n2, axis=0, keepdims=True)
        sums[5:6, :] += jnp.sum(g, axis=0, keepdims=True)
        d = norm_back(g, n2, s2, row(6))
        d_res[here, :] = d
        lo = d.astype(jnp.bfloat16)
        dn[here, :] = lo
        sums[1:2, :] += jnp.sum(lo.astype(jnp.float32), axis=0, keepdims=True)

    loop(rows_here // TB, second_half)
    out_begin()

    def grad_down(i):
        c = pl.ds(mult(i * FB, FB), FB)
        gd[c, :] = dot(act[:, c], dn[...], 0, 0).astype(jnp.bfloat16)

    loop(ff // FB, grad_down)
    R[0]()

    def third(m):
        here = pl.ds(mult(m * TB, TB), TB)
        total = d_res[here, :]
        lo = dn[here, :]
        for f in range(0, ff, FB):
            c = pl.ds(f, FB)
            dw = (dot(lo, w_down[c, :], 1, 1) * gp[here, c].astype(jnp.float32)).astype(jnp.bfloat16)
            gp[here, c] = dw
            ubsum[0:1, c] += jnp.sum(dw.astype(jnp.float32), axis=0, keepdims=True)
            total = total + dot(dw, w_up[:, c], 1, 1)
        norm = n1[here, :]
        sums[2:3, :] += jnp.sum(total * norm, axis=0, keepdims=True)
        sums[3:4, :] += jnp.sum(total, axis=0, keepdims=True)
        d = norm_back(total, norm, s1[here, :], row(4))
        d_res[here, :] = d
        lo = d.astype(jnp.bfloat16)
        da[here, :] = lo
        sums[0:1, :] += jnp.sum(lo.astype(jnp.float32), axis=0, keepdims=True)
        x[here, :] = dot(lo, w_out[...], 1, 1).astype(jnp.bfloat16)

    loop(rows_here // TB, third, plan["third"])
    flush = []
    L.drain(["down"])
    for p in range(2):
        for c in back_in(p, p):
            c.start()

    def grad_up(i):
        c = pl.ds(mult(i * FB, FB), FB)
        act[pl.ds(0, width), c] = dot(low[...], gp[:, c], 0, 0).astype(jnp.bfloat16)

    loop(ff // FB, grad_up, plan["grad_up"])
    flush.append(pltpu.make_async_copy(act.at[pl.ds(0, width), :], g_up, cs.at[8]))
    flush[-1].start()
    w_out[...] = dot(mixed[...], da[...], 0, 0).astype(jnp.bfloat16)
    flush.append(pltpu.make_async_copy(w_out, g_out, cs.at[9]))
    flush[-1].start()
    run(plan["grads"])
    L.drain(["sum"])
    reload = [pltpu.make_async_copy(w_home.at[:, pl.ds(j * width, width)], gd.at[pl.ds(j * width, width), :], cs.at[10 + j])
              for j in range(3)]
    for c in reload:
        c.start()

    def back(p):
        par = lax.rem(p, 2)
        for c in back_in(p, par):
            c.wait()
        back_pair(scale, x, perm, w_down, head_ref, gp, sums, p, par)

        @pl.when(p < pairs - 2)
        def _():
            for c in back_in(p + 2, par):
                c.start()

    loop(pairs, back, plan["back"])
    flush.append(pltpu.make_async_copy(gp.at[:, pl.ds(0, 3 * width)], d_proj, cs.at[0]))
    flush[-1].start()
    for c in reload:
        c.wait()

    def grad_x(m):
        here = pl.ds(mult(m * TB, TB), TB)
        total = d_res[here, :]
        for j in range(3):
            total = total + dot(gp[here, pl.ds(j * width, width)], gd[pl.ds(j * width, width), :], 1, 1)
        dn[here, :] = total.astype(jnp.bfloat16)

    loop(rows_here // TB, grad_x)
    flush.append(pltpu.make_async_copy(dn, gx, cs.at[1]))
    flush[-1].start()
    run(plan["end"])
    out_finish()
    for f in flush:
        f.wait()
    L.drain()


def PLAN(Q, O, U, D, x_begin, up_begin, R):
    return {
        "start": [Q[0],O[0],U[0],D[0],Q[1],O[1],U[1],Q[2],O[2],U[2],Q[3],O[3],U[3],Q[4],x_begin,D[1],Q[5],O[4],U[4]],
        "placed": [Q[6],Q[7]],
        "weights": [O[5],U[5]],
        "project": [(0,D[2]),(3,O[6]),(3,U[6])],
        "attend": [(0,O[7]),(0,U[7]),(0,D[3]),(0,up_begin),(2,D[4])],
        "first": [(0,D[5]),(3,D[6])],
        "firsts": [D[7]],
        "third": [(0, R[1])],
        "grad_up": [],
        "grads": [R[2]],
        "back": [(1, R[3]), (1, R[4]), (3, R[5]), (4, R[6])],
        "end": [R[7], R[8]],
    }


def front_call(scale, pairs, w_qkv, w_out, w_up, w_down, vectors, up_bias, route, tokens, upstream):
    rows_here, width = tokens.shape
    ff = w_up.shape[1]
    r, cols, split = SIZES["down"]
    wq = SIZES["qkv"][1]
    count = 4 * N_GATHER + 3 * 7 + N_REDUCE
    f32 = lambda *s: jax.ShapeDtypeStruct(s, jnp.float32)
    bf = lambda *s: jax.ShapeDtypeStruct(s, BF)
    vbf = lambda *s: pltpu.VMEM(s, BF)
    vf = lambda *s: pltpu.VMEM(s, jnp.float32)
    hbm = pl.BlockSpec(memory_space=pl.ANY)
    return pl.pallas_call(
        functools.partial(front_kernel, scale),
        out_shape=[bf(rows_here, width), bf(width, wq), bf(pairs, 2 * rows_here, 384), bf(pairs, 2, rows_here, BLK),
                   bf(rows_here, 3 * width), bf(rows_here, width), bf(width, ff), bf(width, width), f32(8, width), f32(8, ff),
                   bf(rows_here, width), f32(r, cols)],
        in_specs=[VM] * 7 + [hbm] * 2,
        out_specs=[hbm] * 8 + [VM] * 2 + [hbm, VM],
        scratch_shapes=[vbf(width, width), vbf(width, ff), vbf(ff, width), vbf(rows_here, ff), vbf(rows_here, ff),
                        vbf(rows_here, width), vbf(rows_here, width), vf(rows_here, width), vf(rows_here, 1)]
        + [vbf(rows_here, width)] * 4
        + [vbf(ff, width), vbf(2 * rows_here, BLK), vf(8, width), vf(1, ff), vf(width, BLK)]
        + [vbf(SIZES[n][0], SIZES[n][1] // 2) for n in ("qkv", "out", "up", "down")]
        + [vbf(SIZES["qkv"][0], wq), pltpu.VMEM((pairs, 2 * NZ, 2 * BLK), jnp.int32), vf(rows_here, width)]
        + reduce_scratch(r, cols, split)
        + [pltpu.SemaphoreType.DMA((count,)), pltpu.SemaphoreType.DMA((count,)), pltpu.SemaphoreType.DMA((3, 1)),
           pltpu.SemaphoreType.DMA((13,))],
        compiler_params=pltpu.CompilerParams(collective_id=0, has_side_effects=True, vmem_limit_bytes=62 * 2**20),
    )(w_qkv, w_out, w_up, w_down, vectors, up_bias, route, tokens, upstream)


def back_pair(scale, dm, perm, pool, up_ref, gp, sums, p, par):
    nblk = dm.shape[0] // BLK
    share = BLK // nblk
    half = nblk * BLK
    width = dm.shape[1]
    keep = head_lanes(128)
    lane = lambda o: pl.ds(mult(par * 384 + o, 128), 128)
    col = lambda o: pl.ds(mult(p * 128 + o * width, 128), 128)
    for k in range(nblk):
        table = one_hot(perm[p, k:k + 1, :], BLK)
        moved = jnp.where(keep, dot(table, dm[pl.ds(k * BLK, BLK), col(0)], 0, 0), 0.0).astype(jnp.bfloat16)
        for c in range(2 * nblk):
            up_ref[pl.ds(c * BLK + k * share, share), :] = moved[c * share:(c + 1) * share]
    for h in range(2):
        rows = pl.ds(h * half, half)
        q, kk, v = [pool[rows, lane(o)].reshape(nblk, BLK, 128) for o in (0, 128, 256)]
        probs = pool[pl.ds(2 * half, half), pl.ds(mult((2 * par + h) * 128, 128), 128)].reshape(nblk, BLK, BLK)
        up = up_ref[rows, :].reshape(nblk, BLK, 128)
        dprobs = bdot(up, v, 2, 2)
        p32 = probs.astype(jnp.float32)
        pd = p32 * dprobs
        dscores = (pd - p32 * jnp.sum(pd, axis=-1, keepdims=True)).astype(jnp.bfloat16)
        parts = (bdot(dscores, kk, 2, 1) * scale, bdot(dscores, q, 1, 1) * scale, bdot(probs, up, 1, 1))
        for j, g in enumerate(parts):
            gp[:, pl.ds(3 * width + h * 384 + j * 128, 128)] = g.reshape(half, 128).astype(jnp.bfloat16)
    total = jnp.zeros((1, 384), jnp.float32)
    for k in range(nblk):
        table = one_hot(perm[p, k:k + 1, :], BLK)
        back = jnp.concatenate(
            [gp[pl.ds(c * BLK + k * share, share), pl.ds(3 * width + h * 384, 384)] for h in range(2) for c in range(nblk)], axis=0)
        moved = dot(table, back, 1, 0)
        total = total + jnp.sum(moved, axis=0, keepdims=True)
        for j in range(3):
            gp[pl.ds(k * BLK, BLK), col(j)] = moved[:, j * 128:(j + 1) * 128].astype(jnp.bfloat16)
    sums[6:7, col(0)] = total[:, 0:128]
    sums[7:8, col(0)] = total[:, 256:384]


PARTS = 4


def back_kernel(x_hbm, dp_hbm, gx_hbm, gup_hbm, gout_hbm, sums, ubsum, r_qkv, r_aux, r_up, r_out, gx_rows,
                x, dp, part, own_up, own_out, vsum, ubs, ra, *rest):
    red = [rest[N_SCRATCH * i:N_SCRATCH * (i + 1)] for i in range(3)]
    ss, rs, ls, cs = rest[3 * N_SCRATCH:]
    width = x.shape[1]
    L = Links(ss, rs)
    U = reduce(L, gup_hbm, r_up, red[0], *SIZES["up"][::2], own=own_up, sem=cs.at[0])
    O = reduce(L, gout_hbm, r_out, red[1], *SIZES["out"][::2], own=own_out, sem=cs.at[1])
    Q = reduce(L, part, ra, red[2], *SIZES["qkv"][::2])
    begin, finish = spread(L, gx_hbm, gx_rows, ls, PARTS)
    loads = [pltpu.make_async_copy(x_hbm, x, cs.at[2]), pltpu.make_async_copy(dp_hbm, dp, cs.at[3])]
    for c in loads:
        c.start()
    L.enter()
    G = [functools.partial(begin, i) for i in range(PARTS)]
    plan = BACK_PLAN(U, O, Q, G)
    for stage in plan[0]:
        stage()
    for c in loads:
        c.wait()
    for j in range(0, 3 * width, FB):
        part[:, j:j + FB] = dot(x[...], dp[:, j:j + FB], 0, 0).astype(jnp.bfloat16)
    ubs[...] = jnp.zeros_like(ubs)
    step = ubsum.shape[1] // ubs.shape[0]
    for i in range(ubs.shape[0]):
        ubs[i, 0:1, 0:step] = ubsum[0:1, i * step:(i + 1) * step]
    vsum[...] = jnp.zeros_like(vsum)
    vsum[0:2, :] = sums[6:8, :]
    vsum[2:8, :] = sums[0:6, :]
    part[:, 3 * width:3 * width + 128] = vsum[...].T.astype(jnp.bfloat16)
    part[:, 3 * width + 128:3 * width + 256] = ubs[...].reshape(width, 128).astype(jnp.bfloat16)
    for stage in plan[1]:
        stage()
    r_qkv[...] = ra[:, 0:3 * width]
    r_aux[...] = ra[:, 3 * width:3 * width + 256]
    finish()
    L.drain()


def BACK_PLAN(U, O, Q, G):
    return ([O[0], U[0], G[0]],
            [Q[0], O[1], U[1], G[1], Q[1], O[2], U[2], G[2], Q[2], O[3], U[3], O[4], U[4], Q[3], Q[4], G[3],
             O[5], U[5], Q[5], O[6], U[6], Q[6], O[7], U[7], Q[7], O[8], U[8], Q[8]])


def back_call(x, d_proj, gx, g_up, g_out, sums, ubsum):
    rows_here, width = x.shape
    count = 3 * N_REDUCE + 7 * PARTS
    hbm = pl.BlockSpec(memory_space=pl.ANY)
    vbf = lambda *s: pltpu.VMEM(s, BF)
    vf = lambda *s: pltpu.VMEM(s, jnp.float32)
    f32 = lambda *s: jax.ShapeDtypeStruct(s, jnp.float32)
    r, cu = SIZES["up"][:2]
    co, cq = SIZES["out"][1], SIZES["qkv"][1]
    return pl.pallas_call(
        back_kernel,
        out_shape=[f32(r, 3 * width), f32(r, 256), f32(r, cu), f32(r, co), jax.ShapeDtypeStruct((rows_here, width), BF)],
        in_specs=[hbm] * 5 + [VM] * 2, out_specs=[VM] * 4 + [hbm],
        scratch_shapes=[vbf(rows_here, width), vbf(rows_here, 3 * width), vbf(width, cq), vbf(32 * r, cu // 2),
                        vbf(32 * r, co // 2), vf(BLK, width), vf(32, r, BLK), vf(r, cq)]
        + reduce_scratch(*SIZES["up"]) + reduce_scratch(*SIZES["out"]) + reduce_scratch(*SIZES["qkv"])
        + [pltpu.SemaphoreType.DMA((count,)), pltpu.SemaphoreType.DMA((count,)), pltpu.SemaphoreType.DMA((PARTS,)),
           pltpu.SemaphoreType.DMA((4,))],
        compiler_params=pltpu.CompilerParams(collective_id=1, has_side_effects=True, vmem_limit_bytes=LIMIT),
    )(x, d_proj, gx, g_up, g_out, sums, ubsum)


def homes(tokens, w_qkv, w_out, w_up, w_down, vectors, up_bias, cluster_route, upstream):
    pairs = H // 2
    scale = (tokens.shape[1] // H) ** -0.5
    step = up_bias.shape[0]
    x, w, slots, probs, d_proj, gx, g_up, g_out, sums, ubsum, out_rows, r_down = front_call(
        scale, pairs, w_qkv, w_out, w_up, w_down, vectors, up_bias[None], cluster_route, tokens, upstream)
    r_qkv, r_aux, r_up, r_out, gx_rows = back_call(x, d_proj, gx, g_up, g_out, sums, ubsum)
    return (out_rows, gx_rows, r_qkv, r_out, r_up, r_down, r_aux[:, 0:8].T, r_aux[0, 128:128 + step])


def solution(mesh):
    small = dict(mesh.shape) == {"dp": 4, "seq": 2 * NZ}
    rows = P(ALL, None)
    return jax.shard_map(
        homes if small else shards, mesh=mesh,
        in_specs=(rows,) * 5 + (P(None, ALL), P(ALL), P("dp", None, None), rows),
        out_specs=(rows,) * 6 + (P(None, ALL), P(ALL)),
        check_vma=False,
    )
```

```python
import functools

import jax
import jax.numpy as jnp
from jax import lax
from jax.experimental import pallas as pl
from jax.experimental.pallas import tpu as pltpu
from jax.sharding import PartitionSpec as P

H = 12
CL = 128


epsilon = 1e-06


def normalize(resid, norm_gain, norm_shift):
    average = jnp.mean(resid, axis=-1, keepdims=True)
    centred = resid - average
    spread = jnp.mean(centred * centred, axis=-1, keepdims=True)
    scaled = lax.rsqrt(spread + epsilon)
    normed = centred * scaled
    return (normed * norm_gain + norm_shift, normed, scaled)


def norm_back(grad_output, normed, scaled, norm_gain):
    grad_norm = grad_output * norm_gain
    first_term = jnp.mean(grad_norm, axis=-1, keepdims=True)
    second_term = jnp.mean(grad_norm * normed, axis=-1, keepdims=True)
    return scaled * (grad_norm - first_term - normed * second_term)


def exact_gelu(value):
    return jax.nn.gelu(value, approximate=False)


def order_table(sending):
    heads, rows_here = sending.shape
    columns = jnp.arange(rows_here, dtype=jnp.int32)[None, None, :]
    return (sending[:, :, None] == columns).astype(jnp.bfloat16)


def to_slots(source_rows, table):
    moved = jnp.einsum("hrs,skhe->rkhe", table, source_rows, preferred_element_type=jnp.float32)
    return moved.astype(jnp.bfloat16)


def to_tokens(source_rows, table):
    moved = jnp.einsum("hrs,rkhe->skhe", table, source_rows, preferred_element_type=jnp.float32)
    return moved.astype(jnp.bfloat16)


def cluster_scores(query_c, key_c, scale_factor):
    return (
        jnp.einsum("cahe,cbhe->hcab", query_c, key_c, preferred_element_type=jnp.float32)
        * scale_factor
    )


def shards(tokens, w_qkv, w_out, w_up, w_down, vectors, up_bias, cluster_route, upstream):
    lane_count = lax.axis_size("seq")
    lane_index = lax.axis_index("seq")
    wide_qkv, wide_out, wide_up, wide_down, wide_vectors, wide_bias = (
        lax.all_gather(w_qkv, ("dp", "seq"), axis=0, tiled=True),
        lax.all_gather(w_out, ("dp", "seq"), axis=0, tiled=True),
        lax.all_gather(w_up, ("dp", "seq"), axis=0, tiled=True),
        lax.all_gather(w_down, ("dp", "seq"), axis=0, tiled=True),
        lax.all_gather(vectors, ("dp", "seq"), axis=1, tiled=True),
        lax.all_gather(up_bias, ("dp", "seq"), axis=0, tiled=True),
    )
    rows_here = tokens.shape[0]
    model_width = tokens.shape[1]
    head_size = model_width // H
    portion = rows_here // lane_count
    clusters = rows_here // CL
    scale_factor = head_size ** (-0.5)
    vector_rows = wide_vectors.astype(jnp.float32)
    route_rows = cluster_route[0]
    by_target = lax.dynamic_slice_in_dim(route_rows, lane_index * rows_here, rows_here, 1)
    sending = jnp.swapaxes(by_target.reshape(H, lane_count, portion), 1, 2).reshape(H, rows_here)
    table = order_table(sending)
    projected = jnp.dot(tokens, wide_qkv, preferred_element_type=jnp.float32)
    shifts = jnp.concatenate(
        [vector_rows[0], jnp.zeros((model_width,), jnp.float32), vector_rows[1]]
    )
    projected = (projected + shifts).astype(jnp.bfloat16).reshape(rows_here, 3, H, head_size)
    outgoing = to_slots(projected, table)
    arrived = lax.all_to_all(
        outgoing.reshape(portion, lane_count, 3 * model_width),
        "seq",
        split_axis=1,
        concat_axis=1,
        tiled=True,
    )
    slot_qkv = arrived.reshape(clusters, CL, 3, H, head_size)
    query_c = slot_qkv[:, :, 0]
    key_c = slot_qkv[:, :, 1]
    value_c = slot_qkv[:, :, 2]
    scores = cluster_scores(query_c, key_c, scale_factor)
    row_peak = jnp.max(scores, axis=-1, keepdims=True)
    exponent = jnp.exp(scores - row_peak)
    row_total = jnp.sum(exponent, axis=-1, keepdims=True)
    soft_weights = exponent / row_total
    log_total = row_peak + jnp.log(row_total)
    heads_slot = jnp.einsum(
        "hcab,cbhe->cahe",
        soft_weights.astype(jnp.bfloat16),
        value_c,
        preferred_element_type=jnp.float32,
    ).astype(jnp.bfloat16)
    returned = lax.all_to_all(
        heads_slot.reshape(portion, lane_count, model_width),
        "seq",
        split_axis=1,
        concat_axis=1,
        tiled=True,
    )
    mixed_heads = to_tokens(returned.reshape(rows_here, 1, H, head_size), table).reshape(
        rows_here, model_width
    )
    attention = jnp.dot(mixed_heads, wide_out, preferred_element_type=jnp.float32) + vector_rows[2]
    first_norm, first_normed, first_scaled = normalize(
        tokens.astype(jnp.float32) + attention, vector_rows[4], vector_rows[5]
    )
    first_low = first_norm.astype(jnp.bfloat16)
    widened = jnp.dot(first_low, wide_up, preferred_element_type=jnp.float32) + wide_bias.astype(
        jnp.float32
    )
    activated, gelu_pull = jax.vjp(exact_gelu, widened)
    activated_low = activated.astype(jnp.bfloat16)
    narrowed = (
        jnp.dot(activated_low, wide_down, preferred_element_type=jnp.float32) + vector_rows[3]
    )
    output, second_normed, second_scaled = normalize(
        first_norm + narrowed, vector_rows[6], vector_rows[7]
    )
    back_qkv, back_out, back_up, back_down = (
        lax.all_gather(w_qkv, ("dp", "seq"), axis=0, tiled=True),
        lax.all_gather(w_out, ("dp", "seq"), axis=0, tiled=True),
        lax.all_gather(w_up, ("dp", "seq"), axis=0, tiled=True),
        lax.all_gather(w_down, ("dp", "seq"), axis=0, tiled=True),
    )
    grad_output = upstream.astype(jnp.float32)
    grad_gain_two = jnp.sum(grad_output * second_normed, axis=0)
    grad_shift_two = jnp.sum(grad_output, axis=0)
    grad_second = norm_back(grad_output, second_normed, second_scaled, vector_rows[6])
    grad_narrow = grad_second.astype(jnp.bfloat16)
    grad_down_w = jnp.einsum(
        "tf,td->fd", activated_low, grad_narrow, preferred_element_type=jnp.float32
    )
    grad_down_bias = jnp.sum(grad_narrow.astype(jnp.float32), axis=0)
    grad_active = jnp.einsum(
        "td,fd->tf", grad_narrow, back_down, preferred_element_type=jnp.float32
    )
    grad_wide = gelu_pull(grad_active)[0].astype(jnp.bfloat16)
    grad_up_w = jnp.einsum("td,tf->df", first_low, grad_wide, preferred_element_type=jnp.float32)
    grad_lift_bias = jnp.sum(grad_wide.astype(jnp.float32), axis=0)
    grad_first = grad_second + jnp.einsum(
        "tf,df->td", grad_wide, back_up, preferred_element_type=jnp.float32
    )
    grad_gain_one = jnp.sum(grad_first * first_normed, axis=0)
    grad_shift_one = jnp.sum(grad_first, axis=0)
    grad_resid = norm_back(grad_first, first_normed, first_scaled, vector_rows[4])
    grad_attn = grad_resid.astype(jnp.bfloat16)
    grad_out_w = jnp.einsum("td,te->de", mixed_heads, grad_attn, preferred_element_type=jnp.float32)
    grad_out_bias = jnp.sum(grad_attn.astype(jnp.float32), axis=0)
    grad_mixed = jnp.einsum(
        "te,de->td", grad_attn, back_out, preferred_element_type=jnp.float32
    ).astype(jnp.bfloat16)
    grad_sending = to_slots(grad_mixed.reshape(rows_here, 1, H, head_size), table)
    grad_slot = lax.all_to_all(
        grad_sending.reshape(portion, lane_count, model_width),
        "seq",
        split_axis=1,
        concat_axis=1,
        tiled=True,
    )
    grad_slot = grad_slot.reshape(clusters, CL, H, head_size)
    scores = cluster_scores(query_c, key_c, scale_factor)
    soft_weights = jnp.exp(scores - log_total)
    grad_soft = jnp.einsum(
        "cahe,cbhe->hcab", grad_slot, value_c, preferred_element_type=jnp.float32
    )
    inner_sum = jnp.sum(soft_weights * grad_soft, axis=-1, keepdims=True)
    grad_scores = (soft_weights * (grad_soft - inner_sum)).astype(jnp.bfloat16)
    grad_query = (
        jnp.einsum("hcab,cbhe->cahe", grad_scores, key_c, preferred_element_type=jnp.float32)
        * scale_factor
    )
    grad_key = (
        jnp.einsum("hcab,cahe->cbhe", grad_scores, query_c, preferred_element_type=jnp.float32)
        * scale_factor
    )
    grad_value = jnp.einsum(
        "hcab,cahe->cbhe",
        soft_weights.astype(jnp.bfloat16),
        grad_slot,
        preferred_element_type=jnp.float32,
    )
    grad_slots = jnp.stack([grad_query, grad_key, grad_value], axis=2).astype(jnp.bfloat16)
    came_back = lax.all_to_all(
        grad_slots.reshape(portion, lane_count, 3 * model_width),
        "seq",
        split_axis=1,
        concat_axis=1,
        tiled=True,
    )
    grad_proj = to_tokens(came_back.reshape(rows_here, 3, H, head_size), table).reshape(
        rows_here, 3 * model_width
    )
    grad_qkv_w = jnp.einsum("td,tf->df", tokens, grad_proj, preferred_element_type=jnp.float32)
    bias_sums = jnp.sum(grad_proj.astype(jnp.float32), axis=0).reshape(3, model_width)
    grad_tokens = (
        jnp.einsum("tf,df->td", grad_proj, back_qkv, preferred_element_type=jnp.float32)
        + grad_resid
    ).astype(jnp.bfloat16)
    grad_vector_rows = jnp.stack(
        [
            bias_sums[0],
            bias_sums[2],
            grad_out_bias,
            grad_down_bias,
            grad_gain_one,
            grad_shift_one,
            grad_gain_two,
            grad_shift_two,
        ]
    )
    shares = (
        lax.psum_scatter(grad_qkv_w, ("dp", "seq"), scatter_dimension=0, tiled=True),
        lax.psum_scatter(grad_out_w, ("dp", "seq"), scatter_dimension=0, tiled=True),
        lax.psum_scatter(grad_up_w, ("dp", "seq"), scatter_dimension=0, tiled=True),
        lax.psum_scatter(grad_down_w, ("dp", "seq"), scatter_dimension=0, tiled=True),
        lax.psum_scatter(grad_vector_rows, ("dp", "seq"), scatter_dimension=1, tiled=True),
        lax.psum_scatter(grad_lift_bias, ("dp", "seq"), scatter_dimension=0, tiled=True),
    )
    return (
        output.astype(jnp.bfloat16),
        grad_tokens,
        shares[0],
        shares[1],
        shares[2],
        shares[3],
        shares[4],
        shares[5],
    )


MESH = pl.DeviceIdType.MESH
NZ = 4
BLK = 128

class Links:
    def __init__(self, send_sems, recv_sems):
        self.send_sems, self.recv_sems, self.count, self.drains, self.key = send_sems, recv_sems, 0, {}, None
        self.dp, self.sq = lax.axis_index("dp"), lax.axis_index("seq")
        self.x, self.y = lax.rem(self.dp, 2), self.dp // 2
        self.core, self.z = lax.rem(self.sq, 2), self.sq // 2
        self.sib = self.sq + 1 - 2 * self.core
        self.dp_x = self.dp + 1 - 2 * self.x
        self.dp_y = self.dp + 2 - 4 * self.y

    def peers(self):
        return jnp.where(self.core == 0, self.dp_x, self.dp_y), jnp.where(self.core == 0, self.dp_y, self.dp_x)

    def new(self):
        self.count += 1
        return self.count - 1

    def copy(self, i, src, dst, dp, sq):
        return pltpu.make_async_remote_copy(
            src_ref=src, dst_ref=dst, send_sem=self.send_sems.at[i], recv_sem=self.recv_sems.at[i],
            device_id=(dp, sq), device_id_type=MESH)

    def enter(self, near=True, line=True):
        barrier = pltpu.get_barrier_semaphore()
        n = 0
        if near:
            for dp in (self.dp_x, self.dp_y):
                pl.semaphore_signal(barrier, inc=1, device_id=(dp, self.sq), device_id_type=MESH)
                n += 1
        if line:
            for j in range(1, 2 * NZ):
                pl.semaphore_signal(barrier, inc=1, device_id=(self.dp, lax.rem(self.sq + j, 2 * NZ)), device_id_type=MESH)
                n += 1
        pl.semaphore_wait(barrier, n)

    def go(self, *makers):
        for make in makers:
            make().start()
            self.add(lambda make=make: make().wait_send())

    def drain(self, keys=None):
        for key in list(self.drains) if keys is None else keys:
            for d in self.drains.pop(key, []):
                d()

    def add(self, d):
        self.drains.setdefault(self.key, []).append(d)

    def under(self, key, stages):
        def run(stage):
            before, self.key = self.key, key
            stage()
            self.key = before
        return [functools.partial(run, stage) for stage in stages]


def mult(v, m):
    return pl.multiple_of(v, m)


def gather(L, shard, full, half_buf, r, split):
    half = full.shape[1] // 2
    a, b = split
    big = 2 * r
    mine = pl.ds(mult(L.core * half, 128), half)
    other = pl.ds(mult((1 - L.core) * half, 128), half)
    cols_a = pl.ds(mult(L.core * half, 128), a)
    cols_b = pl.ds(mult(L.core * half + a, 128), b)
    chip = lambda z: pl.ds(mult((L.dp * NZ + z) * big, 16), big)
    quarter = lambda dp, n=1: pl.ds(mult(dp * NZ * big, 16), n * NZ * big)
    i0 = L.new()
    fr = [None] + [L.new() for _ in range(3)]
    fl = [None] + [L.new() for _ in range(3)]
    a1, b1, a2, a3, b2, b3, c0, c1, c2 = [L.new() for _ in range(9)]
    fa, fb = L.peers()
    opposite = 3 - L.dp
    first = lambda: L.copy(i0, shard.at[:, other], half_buf, L.dp, L.sib)

    def right(d, z0):
        return L.copy(fr[d], full.at[chip(z0), mine], full.at[chip(z0), mine], L.dp, L.sq + 2)

    def left(d, z0):
        return L.copy(fl[d], full.at[chip(z0), mine], full.at[chip(z0), mine], L.dp, L.sq - 2)

    def send_line(d):
        @pl.when((L.z >= d - 1) & (L.z < NZ - 1))
        def _():
            right(d, L.z - d + 1).start()

        @pl.when((L.z <= NZ - d) & (L.z > 0))
        def _():
            left(d, L.z + d - 1).start()

    def drain_line(d):
        @pl.when((L.z >= d - 1) & (L.z < NZ - 1))
        def _():
            right(d, L.z - d + 1).wait_send()

        @pl.when((L.z <= NZ - d) & (L.z > 0))
        def _():
            left(d, L.z + d - 1).wait_send()

    def recv_line(d):
        @pl.when(L.z >= d)
        def _():
            right(d, L.z - d).wait_recv()

        @pl.when(L.z + d <= NZ - 1)
        def _():
            left(d, L.z + d).wait_recv()

    def same(i, rows, cols, dp, sq):
        ref = full.at[rows, cols]
        return L.copy(i, ref, ref, dp, sq)

    def s0():
        L.go(first)

    def s1():
        first().wait_recv()
        own, got = shard[:, mine], half_buf[...]

        @pl.when(L.core == 0)
        def _():
            full[chip(L.z), mine] = jnp.concatenate([own, got], axis=0)

        @pl.when(L.core == 1)
        def _():
            full[chip(L.z), mine] = jnp.concatenate([got, own], axis=0)
        send_line(1)
        L.add(functools.partial(drain_line, 1))

    def s2():
        recv_line(1)
        send_line(2)
        L.add(functools.partial(drain_line, 2))

    def s3():
        recv_line(2)
        send_line(3)
        L.add(functools.partial(drain_line, 3))

    def s4():
        recv_line(3)
        q = lambda: quarter(L.dp)
        L.go(lambda: same(a1, q(), cols_a, fa, L.sq), lambda: same(b1, q(), cols_b, fb, L.sq),
             lambda: same(c0, q(), mine, L.dp, L.sib))

    def s5():
        same(a1, quarter(fa), cols_a, fa, L.sq).wait_recv()
        L.go(lambda: same(a2, quarter(L.dp), cols_a, fb, L.sq), lambda: same(a3, quarter(fa), cols_a, fb, L.sq))
        same(b1, quarter(fb), cols_b, fb, L.sq).wait_recv()
        L.go(lambda: same(b2, quarter(L.dp), cols_b, fa, L.sq), lambda: same(b3, quarter(fb), cols_b, fa, L.sq))

    def s6():
        same(a2, quarter(fb), cols_a, fb, L.sq).wait_recv()
        same(b2, quarter(fa), cols_b, fa, L.sq).wait_recv()
        L.go(lambda: same(c1, quarter(L.dp_x), mine, L.dp, L.sib))
        same(a3, quarter(opposite), cols_a, fb, L.sq).wait_recv()
        same(b3, quarter(opposite), cols_b, fa, L.sq).wait_recv()
        L.go(lambda: same(c2, quarter(2 * (1 - L.y), 2), mine, L.dp, L.sib))

    def s7():
        same(c0, quarter(L.dp), other, L.dp, L.sib).wait_recv()
        same(c1, quarter(L.dp_x), other, L.dp, L.sib).wait_recv()
        same(c2, quarter(2 * (1 - L.y), 2), other, L.dp, L.sib).wait_recv()
    return [s0, s1, s2, s3, s4, s5, s6, s7]


def spread(L, src, dst, local_sem, parts=1):
    ids = [[L.new() for _ in range(2 * NZ - 1)] for _ in range(parts)]
    n = BLK // parts
    rows = lambda s, i: pl.ds(mult(s * BLK + i * n, n), n)

    def keep(i):
        return pltpu.make_async_copy(src.at[rows(L.sq, i)], dst.at[rows(L.sq, i)], local_sem.at[i])

    def move(i, j, to, frm):
        return L.copy(ids[i][j - 1], src.at[rows(to, i)], dst.at[rows(frm, i)], L.dp, to)

    def begin(i=0):
        keep(i).start()
        for j in range(1, 2 * NZ):
            L.go(lambda j=j: move(i, j, lax.rem(L.sq + j, 2 * NZ), L.sq))

    def finish():
        for i in range(parts):
            keep(i).wait()
            for j in range(1, 2 * NZ):
                move(i, j, L.sq, lax.rem(L.sq + 2 * NZ - j, 2 * NZ)).wait_recv()
    return begin, finish


def add_into(dst, rows0, cols, src, n):
    step = 48

    def one(i, _):
        here = pl.ds(mult(i * step, 16), step)
        there = pl.ds(mult(rows0 + i * step, 16), step)
        dst[there, cols] = (dst[there, cols].astype(jnp.float32) + src[here, :].astype(jnp.float32)).astype(jnp.bfloat16)
        return 0
    lax.fori_loop(0, n // step, one, 0)


def landing(r, c, split):
    half, (a, b), big = c // 2, split, 2 * r
    return [(32 * r, half), (4 * big, a), (4 * big, a), (4 * big, b), (4 * big, b), (4 * big, a), (4 * big, b)]


def line_scratch(r, c):
    half, big = c // 2, 2 * r
    return [pltpu.VMEM((3, big, half), jnp.bfloat16)] * 2 + [pltpu.VMEM((2, r, half), jnp.float32), pltpu.VMEM((r, half), jnp.float32)]


def reduce_scratch(r, c, split):
    return [pltpu.VMEM(shape, jnp.bfloat16) for shape in landing(r, c, split)] + line_scratch(r, c)


N_REDUCE = 15
N_GATHER = 16
N_SCRATCH = 11
N_LINE = 4


def reduce(L, part, out, scratch, r, split):
    acc, a10, a11, b10, b11, a2, b2, from_l, from_r, fin, got = scratch
    half = part.shape[1] // 2
    a, b = split
    big = 2 * r
    mine = pl.ds(mult(L.core * half, 128), half)
    other = pl.ds(mult((1 - L.core) * half, 128), half)
    ca, cb = pl.ds(0, a), pl.ds(a, b)
    quarter = lambda dp, n=1: pl.ds(mult(dp * NZ * big, 16), n * NZ * big)
    chip = lambda z: pl.ds(mult((L.dp * NZ + z) * big, 16), big)
    i0, ia0, ia1, ib0, ib1, ia2, ib2, ifin = [L.new() for _ in range(8)]
    fb, fa = L.peers()
    opposite = 3 - L.dp
    ir = [None] + [L.new() for _ in range(3)]
    il = [L.new() for _ in range(3)]
    q = lambda dp: dp * NZ * big

    core_copy = lambda: L.copy(i0, part.at[:, other], acc, L.dp, L.sib)
    def part_copy(i, dp, cols, to, peer):
        return L.copy(i, acc.at[quarter(dp), cols], to, peer, L.sq)

    a_copies = [lambda: part_copy(ia0, opposite, ca, a10, fa), lambda: part_copy(ia1, fa, ca, a11, fa)]
    b_copies = [lambda: part_copy(ib0, opposite, cb, b10, fb), lambda: part_copy(ib1, fb, cb, b11, fb)]
    a2_copy = lambda: part_copy(ia2, fb, ca, a2, fb)
    b2_copy = lambda: part_copy(ib2, fa, cb, b2, fa)
    def s0():
        L.go(core_copy)

    def s1():
        core_copy().wait_recv()
        step = 48

        def one(i, _):
            here = pl.ds(mult(i * step, 16), step)
            acc[here, :] = (acc[here, :].astype(jnp.float32) + part[here, mine].astype(jnp.float32)).astype(jnp.bfloat16)
            return 0
        lax.fori_loop(0, 32 * r // step, one, 0)
        L.go(a_copies[0], b_copies[0], a_copies[1], b_copies[1])

    def s2():
        a_copies[0]().wait_recv()
        add_into(acc, q(fb), ca, a10, 4 * big)
        L.go(a2_copy)
        b_copies[0]().wait_recv()
        add_into(acc, q(fa), cb, b10, 4 * big)
        L.go(b2_copy)
        a_copies[1]().wait_recv()
        add_into(acc, q(L.dp), ca, a11, 4 * big)
        b_copies[1]().wait_recv()
        add_into(acc, q(L.dp), cb, b11, 4 * big)

    def s3():
        a2_copy().wait_recv()
        add_into(acc, q(L.dp), ca, a2, 4 * big)
        b2_copy().wait_recv()
        add_into(acc, q(L.dp), cb, b2, 4 * big)

    full_cols = pl.ds(0, half)

    def hop_r(t, src):
        return L.copy(ir[t], src, from_l.at[t - 1], L.dp, L.sq + 2)

    def hop_l(t, src):
        return L.copy(il[t], src, from_r.at[t], L.dp, L.sq - 2)

    def merge(buf, k, t):
        buf[k] = (buf[k].astype(jnp.float32) + acc[chip(t), :].astype(jnp.float32)).astype(jnp.bfloat16)

    def line(s):
        @pl.when(L.z == s)
        def _():
            for t in range(NZ - 1, s, -1):
                if s == 0:
                    hop_r(t, acc.at[chip(t), full_cols]).start()
                else:
                    hop_r(t, from_l.at[t - 1]).wait_recv()
                    merge(from_l, t - 1, t)
                    hop_r(t, from_l.at[t - 1]).start()

        @pl.when(L.z == NZ - 1 - s)
        def _():
            for t in range(0, NZ - 1 - s):
                if s == 0:
                    hop_l(t, acc.at[chip(t), full_cols]).start()
                else:
                    hop_l(t, from_r.at[t]).wait_recv()
                    merge(from_r, t, t)
                    hop_l(t, from_r.at[t]).start()

        def drain():
            @pl.when(L.z == s)
            def _():
                for t in range(NZ - 1, s, -1):
                    hop_r(t, from_l.at[t - 1]).wait_send()

            @pl.when(L.z == NZ - 1 - s)
            def _():
                for t in range(0, NZ - 1 - s):
                    hop_l(t, from_r.at[t]).wait_send()
        L.add(drain)

    fin_copy = lambda: L.copy(ifin, fin.at[1 - L.core], got, L.dp, L.sib)

    def s7():
        for z in range(NZ):
            @pl.when(L.z == z)
            def _(z=z):
                total = acc[chip(z), :].astype(jnp.float32)
                if z > 0:
                    hop_r(z, from_l.at[z - 1]).wait_recv()
                    total = total + from_l[z - 1].astype(jnp.float32)
                if z < NZ - 1:
                    hop_l(z, from_r.at[z]).wait_recv()
                    total = total + from_r[z].astype(jnp.float32)
                fin[...] = total.reshape(2, r, half)
        L.go(fin_copy)

    def s8():
        out[:, mine] = fin[L.core]
        fin_copy().wait_recv()
        out[:, other] = got[...]
    return [s0, s1, s2, s3] + [functools.partial(line, s) for s in range(3)] + [s7, s8]


def one_hot(slots, rows):
    row = lax.broadcasted_iota(jnp.int32, (rows, slots.shape[1]), 0)
    return jnp.where(slots == row, 1.0, 0.0).astype(jnp.bfloat16)


def head_lanes(width):
    row = lax.broadcasted_iota(jnp.int32, (2 * BLK, width), 0)
    lane = lax.rem(lax.broadcasted_iota(jnp.int32, (2 * BLK, width), 1), 128)
    return (row < BLK) == (lane < 64)


def dot(a, b, ca, cb):
    return lax.dot_general(a, b, (((ca,), (cb,)), ((), ())), preferred_element_type=jnp.float32)


def bdot(a, b, ca, cb):
    return lax.dot_general(a, b, (((ca,), (cb,)), ((0,), (0,))), preferred_element_type=jnp.float32)


BATCH = 8


SIZES = {"qkv": (24, 2560, (640, 640)), "out": (24, 768, (256, 128)), "up": (24, 3072, (768, 768)), "down": (96, 768, (128, 256))}
ALL = ("dp", "seq")
VM = pl.BlockSpec(memory_space=pltpu.VMEM)
BF = jnp.bfloat16
LIMIT = 60 * 2**20


def place_rows(route, perm, me):
    heads, n = route.shape[1], 2 * NZ
    size = route.shape[2] // n
    base = me * BLK
    head_row = jnp.concatenate([route[0, :, 0:size], jnp.full((16 - heads, size), -1, jnp.int32)], axis=0)
    mine = (head_row >= base) & (head_row < base + BLK)
    flags = jnp.where(mine, 1.0, 0.0).astype(jnp.bfloat16)
    before = []
    for c in range(0, size, 128):
        row = lax.broadcasted_iota(jnp.int32, (size, 128), 0)
        col = lax.broadcasted_iota(jnp.int32, (size, 128), 1) + c
        before.append(dot(flags, jnp.where(row < col, 1.0, 0.0).astype(jnp.bfloat16), 1, 0))
    slot = jnp.where(mine, jnp.concatenate(before, axis=1).astype(jnp.int32), -1)
    for h in range(heads):
        per = jnp.concatenate([route[0, h:h + 1, k * size:(k + 1) * size] for k in range(n)], axis=0)
        local = jnp.where((per >= base) & (per < base + BLK), per - base, 0).astype(jnp.float32).astype(jnp.bfloat16)
        pick = jnp.where(slot[h:h + 1, :] == lax.broadcasted_iota(jnp.int32, (BLK, size), 0), 1.0, 0.0).astype(jnp.bfloat16)
        perm[h // 2, :, pl.ds((h % 2) * BLK, BLK)] = dot(local, pick, 1, 1).astype(jnp.int32)


def front_pair(scale, qkv, width, perm, mixed, pool, head_ref, p, par):
    nblk = qkv.shape[0] // BLK
    share = BLK // nblk
    keep = head_lanes(384)
    cols = pl.ds(mult(par * 384, 128), 384)
    lane = lambda o: pl.ds(mult(par * 384 + o, 128), 128)
    col = lambda o: pl.ds(mult(p * 128 + o * width, 128), 128)
    half = nblk * BLK
    for k in range(nblk):
        here = pl.ds(k * BLK, BLK)
        packed = jnp.concatenate([qkv[here, col(0)], qkv[here, col(1)], qkv[here, col(2)]], axis=1)
        table = one_hot(perm[p, k:k + 1, :], BLK)
        moved = jnp.where(keep, dot(table, packed, 0, 0), 0.0).astype(jnp.bfloat16)
        for c in range(2 * nblk):
            pool[pl.ds(c * BLK + k * share, share), cols] = moved[c * share:(c + 1) * share]
    for h in range(2):
        rows = pl.ds(h * half, half)
        q, kk, v = [pool[rows, lane(o)].reshape(nblk, BLK, 128) for o in (0, 128, 256)]
        scores = bdot(q, kk, 2, 2) * scale
        e = jnp.exp(scores - jnp.max(scores, axis=-1, keepdims=True))
        probs = (e * (1.0 / jnp.sum(e, axis=-1, keepdims=True))).astype(jnp.bfloat16)
        pool[pl.ds(2 * half, half), pl.ds(mult((2 * par + h) * 128, 128), 128)] = probs.reshape(half, BLK)
        head_ref[rows, :] = bdot(probs, v, 2, 1).reshape(half, BLK).astype(jnp.bfloat16)
    for k in range(nblk):
        table = one_hot(perm[p, k:k + 1, :], BLK)
        back = jnp.concatenate([head_ref[pl.ds(c * BLK + k * share, share), :] for c in range(2 * nblk)], axis=0)
        mixed[pl.ds(k * BLK, BLK), col(0)] = dot(table, back, 1, 0).astype(jnp.bfloat16)


def loop(n, body, hooks=()):
    def one(i, _):
        body(i)
        for at, stage in hooks:
            pl.when(i == at)(stage)
        return 0
    lax.fori_loop(0, n, one, 0)


def moments(v):
    mean = jnp.mean(v, axis=-1, keepdims=True)
    centred = v - mean
    inv = lax.rsqrt(jnp.mean(centred * centred, axis=-1, keepdims=True) + epsilon)
    return centred * inv, inv


TB = 256
FB = 768


def layer_kernel(scale, w_shard, out_shard, up_shard, down_shard, vec_shard, ub_shard, route, x_rows, up_rows,
                 x_home, w_home, slots, probs, out_rows, gx_rows, r_qkv, r_aux, r_out, r_up, r_down,
                 w_out, w_up, w_down, act, gp, x, mixed, n1, s1, low, up, outb, dn, gd, head_ref, vec, ub, auxf,
                 bq, bo, bu, bd, qkv_shard, perm, d_res, s2, sums, ubsum, ra, *rest):
    own = [rest[i:i + N_SCRATCH] for i in (0, N_SCRATCH)]
    late = rest[2 * N_SCRATCH:2 * N_SCRATCH + 3 + 2 * N_LINE]
    ss, rs, ls, cs = rest[2 * N_SCRATCH + 3 + 2 * N_LINE:]
    rows_here, width = x.shape
    ff = w_up.shape[1]
    pairs = perm.shape[0]
    w = gp.at[pl.ds(0, width), pl.ds(0, qkv_shard.shape[1])]
    da = up
    L = Links(ss, rs)
    r = w_shard.shape[0]
    nv, step = vec_shard.shape[0], ub_shard.shape[1]
    qkv_shard[:, 0:3 * width] = w_shard[...]
    auxf[...] = jnp.zeros_like(auxf)
    auxf[0:nv, 0:r] = vec_shard[...].astype(jnp.float32)
    qkv_shard[:, 3 * width:3 * width + 128] = auxf[0:128, :].T[0:r, :].astype(jnp.bfloat16)
    auxf[0:nv, :] = jnp.zeros((nv, 128), jnp.float32)
    auxf[0:1, 0:step] = ub_shard[...].astype(jnp.float32)
    qkv_shard[:, 3 * width + 128:3 * width + 256] = auxf[0:r, :].astype(jnp.bfloat16)
    L.enter()
    Q = L.under("qkv", gather(L, qkv_shard, w, bq, *SIZES["qkv"][::2]))
    O = L.under("out", gather(L, out_shard, w_out, bo, *SIZES["out"][::2]))
    U = L.under("up", gather(L, up_shard, w_up, bu, *SIZES["up"][::2]))
    D = L.under("down", gather(L, down_shard, w_down, bd, *SIZES["down"][::2]))
    x_begin, x_finish = spread(L, x_rows, x, ls.at[0])
    up_begin, up_finish = spread(L, up_rows, up, ls.at[1])
    out_begin, out_finish = spread(L, outb, out_rows, ls.at[2])
    gx_begin, gx_finish = spread(L, dn, gx_rows, ls.at[3], PARTS)
    g_up, part = act.at[pl.ds(0, width), :], act.at[pl.ds(0, width), pl.ds(0, SIZES["qkv"][1])]
    spare = [act.at[pl.ds(width, r * 8), pl.ds(i * width, width)] for i in range(4)]
    hq = SIZES["qkv"][1] // 2
    spare_q = [w_up.at[:, pl.ds(0, hq)]] + [w_up.at[pl.ds(i * r * 8, r * 8), pl.ds(hq + j * hq // 2, hq // 2)]
                                          for j in range(2) for i in range(3)]
    R = reduce(L, gd, r_down, own[0], *SIZES["down"][::2])
    R = L.under("sum", R[:1]) + R[1:]
    SO = reduce(L, w_out, r_out, own[1], *SIZES["out"][::2])
    SU = reduce(L, g_up, r_up, [late[0], *spare, *late[1:3 + N_LINE]], *SIZES["up"][::2])
    SU = L.under("sum_up", SU[:1]) + SU[1:]
    SQ = reduce(L, part, ra, [*spare_q, *late[3 + N_LINE:]], *SIZES["qkv"][::2])
    plan = PLAN(Q, O, U, D, x_begin, up_begin, R)
    plan.update(LATE(R, SO, SU, SQ, [functools.partial(gx_begin, i) for i in range(PARTS)]))
    row = lambda i: vec[i:i + 1, :]

    def run(stages):
        for stage in stages:
            stage()

    run(plan["start"])
    sums[...] = jnp.zeros_like(sums)
    ubsum[...] = jnp.zeros_like(ubsum)
    place_rows(route, perm, L.sq)
    run(plan["placed"])
    vec[...] = w[:, 2304:2432].astype(jnp.float32).T[0:8, :]
    auxf[...] = w[:, 2432:2560].astype(jnp.float32)
    for i in range(ff // step):
        ub[:, i * step:(i + 1) * step] = auxf[i * r:i * r + 1, 0:step]
    w_flush = pltpu.make_async_copy(w, w_home, cs.at[0])
    w_flush.start()
    run(plan["weights"])
    x_finish()
    x_flush = pltpu.make_async_copy(x, x_home, cs.at[1])
    x_flush.start()

    def project(m):
        here = pl.ds(mult(m * TB, TB), TB)
        for j in range(3):
            c = pl.ds(j * width, width)
            r = dot(x[here, :], w[:, c], 1, 0)
            if j != 1:
                r = r + row(j // 2)
            act[here, c] = r.astype(jnp.bfloat16)

    loop(rows_here // TB, project, plan["project"])

    def kept(p, par):
        half = rows_here
        return [pltpu.make_async_copy(gd.at[pl.ds(0, 2 * half), pl.ds(mult(par * 384, 128), 384)], slots.at[p], cs.at[2 + 3 * par])] + [
            pltpu.make_async_copy(gd.at[pl.ds(2 * half, half), pl.ds(mult((2 * par + h) * 128, 128), 128)], probs.at[p, h],
                                  cs.at[3 + 3 * par + h]) for h in range(2)]

    def back_in(p, par):
        half = rows_here
        return [pltpu.make_async_copy(slots.at[p], w_down.at[pl.ds(0, 2 * half), pl.ds(mult(par * 384, 128), 384)], cs.at[2 + 3 * par])] + [
            pltpu.make_async_copy(probs.at[p, h], w_down.at[pl.ds(2 * half, half), pl.ds(mult((2 * par + h) * 128, 128), 128)],
                                  cs.at[3 + 3 * par + h]) for h in range(2)]

    def attend(p):
        par = lax.rem(p, 2)

        @pl.when(p >= 2)
        def _():
            for c in kept(p - 2, par):
                c.wait()
        front_pair(scale, act, width, perm, mixed, gd, head_ref, p, par)
        for c in kept(p, par):
            c.start()

    loop(pairs, attend, plan["attend"])
    w_flush.wait()
    L.drain(["qkv", "out"])

    def first_half(m):
        here = pl.ds(mult(m * TB, TB), TB)
        r1 = x[here, :].astype(jnp.float32) + dot(mixed[here, :], w_out[...], 1, 0) + row(2)
        norm, inv = moments(r1)
        n1[here, :] = norm
        s1[here, :] = inv
        lo = (norm * row(4) + row(5)).astype(jnp.bfloat16)
        low[here, :] = lo
        for f in range(0, ff, FB):
            c = pl.ds(f, FB)
            wide = dot(lo, w_up[:, c], 1, 0) + ub[:, c]
            cdf = 0.5 + 0.5 * lax.erf(wide * 0.7071067811865476)
            act[here, c] = (wide * cdf).astype(jnp.bfloat16)
            gp[here, c] = (cdf + wide * (0.3989422804014327 * jnp.exp(-0.5 * wide * wide))).astype(jnp.bfloat16)

    loop(rows_here // TB, first_half, plan["first"])
    run(plan["firsts"])
    for p in range(pairs - 2, pairs):
        for c in kept(p, p % 2):
            c.wait()
    x_flush.wait()

    def second(m):
        here = pl.ds(mult(m * TB, TB), TB)
        first = n1[here, :] * row(4) + row(5)
        r2 = first + dot(act[here, :], w_down[...], 1, 0) + row(3)
        n2, inv = moments(r2)
        outb[here, :] = (n2 * row(6) + row(7)).astype(jnp.bfloat16)
        d_res[here, :] = n2
        s2[here, :] = inv

    loop(rows_here // TB, second)
    out_begin()
    up_finish()

    def second_back(m):
        here = pl.ds(mult(m * TB, TB), TB)
        n2 = d_res[here, :]
        g = up[here, :].astype(jnp.float32)
        sums[4:5, :] += jnp.sum(g * n2, axis=0, keepdims=True)
        sums[5:6, :] += jnp.sum(g, axis=0, keepdims=True)
        d = norm_back(g, n2, s2[here, :], row(6))
        d_res[here, :] = d
        lo = d.astype(jnp.bfloat16)
        dn[here, :] = lo
        sums[1:2, :] += jnp.sum(lo.astype(jnp.float32), axis=0, keepdims=True)

    loop(rows_here // TB, second_back)

    def grad_down(i):
        c = pl.ds(mult(i * FB, FB), FB)
        gd[c, :] = dot(act[:, c], dn[...], 0, 0).astype(jnp.bfloat16)

    loop(ff // FB, grad_down)
    R[0]()

    def third(m):
        here = pl.ds(mult(m * TB, TB), TB)
        total = d_res[here, :]
        lo = dn[here, :]
        for f in range(0, ff, FB):
            c = pl.ds(f, FB)
            dw = (dot(lo, w_down[c, :], 1, 1) * gp[here, c].astype(jnp.float32)).astype(jnp.bfloat16)
            gp[here, c] = dw
            ubsum[0:1, c] += jnp.sum(dw.astype(jnp.float32), axis=0, keepdims=True)
            total = total + dot(dw, w_up[:, c], 1, 1)
        norm = n1[here, :]
        sums[2:3, :] += jnp.sum(total * norm, axis=0, keepdims=True)
        sums[3:4, :] += jnp.sum(total, axis=0, keepdims=True)
        d = norm_back(total, norm, s1[here, :], row(4))
        d_res[here, :] = d
        lo = d.astype(jnp.bfloat16)
        da[here, :] = lo
        sums[0:1, :] += jnp.sum(lo.astype(jnp.float32), axis=0, keepdims=True)
        x[here, :] = dot(lo, w_out[...], 1, 1).astype(jnp.bfloat16)

    loop(rows_here // TB, third, plan["third"])
    L.drain(["down"])
    for p in range(2):
        for c in back_in(p, p):
            c.start()

    def grad_up(i):
        c = pl.ds(mult(i * FB, FB), FB)
        act[pl.ds(0, width), c] = dot(low[...], gp[:, c], 0, 0).astype(jnp.bfloat16)

    loop(ff // FB, grad_up, plan["grad_up"])
    L.drain(["up"])
    run(plan["up_ready"])
    w_out[...] = dot(mixed[...], da[...], 0, 0).astype(jnp.bfloat16)
    run(plan["out_ready"])
    L.drain(["sum"])
    reload = [pltpu.make_async_copy(w_home.at[:, pl.ds(j * width, width)], gd.at[pl.ds(j * width, width), :], cs.at[10 + j])
              for j in range(3)]
    for c in reload:
        c.start()

    def back(p):
        par = lax.rem(p, 2)
        for c in back_in(p, par):
            c.wait()
        back_pair(scale, x, perm, w_down, head_ref, gp, sums, p, par)

        @pl.when(p < pairs - 2)
        def _():
            for c in back_in(p + 2, par):
                c.start()

    loop(pairs, back, plan["back"])
    x_again = pltpu.make_async_copy(x_home, x, cs.at[0])
    x_again.start()
    for c in reload:
        c.wait()

    def grad_x(m):
        here = pl.ds(mult(m * TB, TB), TB)
        total = d_res[here, :]
        for j in range(3):
            total = total + dot(gp[here, pl.ds(j * width, width)], gd[pl.ds(j * width, width), :], 1, 1)
        dn[here, :] = total.astype(jnp.bfloat16)

    loop(rows_here // TB, grad_x)
    run(plan["x_ready"])
    x_again.wait()
    L.drain(["sum_up"])

    def grad_qkv(i):
        c = pl.ds(mult(i * FB, FB), FB)
        part[:, c] = dot(x[...], gp[:, c], 0, 0).astype(jnp.bfloat16)

    loop(3 * width // FB, grad_qkv)
    d_res[0:BLK, :] = jnp.zeros((BLK, width), jnp.float32)
    d_res[0:2, :] = sums[6:8, :]
    d_res[2:8, :] = sums[0:6, :]
    part[:, 3 * width:3 * width + 128] = d_res[0:BLK, :].T.astype(jnp.bfloat16)
    auxf[...] = jnp.zeros_like(auxf)
    for i in range(ff // step):
        auxf[i * r:i * r + 1, 0:step] = ubsum[0:1, i * step:(i + 1) * step]
    part[:, 3 * width + 128:3 * width + 256] = auxf[...].astype(jnp.bfloat16)
    run(plan["end"])
    r_qkv[...] = ra[:, 0:3 * width]
    r_aux[...] = ra[:, 3 * width:3 * width + 256]
    out_finish()
    gx_finish()
    L.drain()


def PLAN(Q, O, U, D, x_begin, up_begin, R):
    return {
        "start": [Q[0],O[0],U[0],D[0],Q[1],O[1],U[1],Q[2],O[2],U[2],Q[3],O[3],U[3],Q[4],x_begin,D[1],Q[5],O[4],U[4]],
        "placed": [Q[6],Q[7]],
        "weights": [O[5],U[5]],
        "project": [(1,D[2])],
        "attend": [(0,D[3]),(0,up_begin),(0,O[6]),(0,U[6]),(2,O[7]),(2,U[7]),(3,D[4])],
        "first": [(0,D[5]),(3,D[6])],
        "firsts": [D[7]],
    }


def LATE(R, O, U, Q, G):
    return {
        "third": [(0, R[1])],
        "grad_up": [],
        "up_ready": [U[0]],
        "out_ready": [O[0], R[2]],
        "back": [(0, U[1]), (1, R[3]), (1, R[4]), (2, O[1]), (3, R[5]), (4, R[6]), (5, R[7])],
        "x_ready": [G[0], G[1], U[2], O[2]],
        "end": [Q[0], R[8], U[3], U[4], G[2], Q[1], O[3], O[4], U[5], G[3], Q[2], U[6], O[5], Q[3], Q[4], O[6], Q[5], U[7], O[7],
                Q[6], Q[7], U[8], O[8], Q[8]],
    }


PARTS = 4


def layer_call(scale, pairs, w_qkv, w_out, w_up, w_down, vectors, up_bias, route, tokens, upstream):
    rows_here, width = tokens.shape
    ff = w_up.shape[1]
    r, cols, split = SIZES["down"]
    wq = SIZES["qkv"][1]
    count = 4 * (N_GATHER + N_REDUCE) + 7 * (3 + PARTS)
    f32 = lambda *s: jax.ShapeDtypeStruct(s, jnp.float32)
    bf = lambda *s: jax.ShapeDtypeStruct(s, BF)
    vbf = lambda *s: pltpu.VMEM(s, BF)
    vf = lambda *s: pltpu.VMEM(s, jnp.float32)
    hbm = pl.BlockSpec(memory_space=pl.ANY)
    ru = landing(*SIZES["up"])
    rq = SIZES["qkv"][0]
    return pl.pallas_call(
        functools.partial(layer_kernel, scale),
        out_shape=[bf(rows_here, width), bf(width, wq), bf(pairs, 2 * rows_here, 384), bf(pairs, 2, rows_here, BLK),
                   bf(rows_here, width), bf(rows_here, width), f32(rq, 3 * width), f32(rq, 256), f32(*SIZES["out"][:2]),
                   f32(*SIZES["up"][:2]), f32(r, cols)],
        in_specs=[VM] * 7 + [hbm] * 2,
        out_specs=[hbm] * 6 + [VM] * 5,
        scratch_shapes=[vbf(width, width), vbf(width, ff), vbf(ff, width), vbf(rows_here, ff), vbf(rows_here, ff),
                        vbf(rows_here, width), vbf(rows_here, width), vf(rows_here, width), vf(rows_here, 1)]
        + [vbf(rows_here, width)] * 4
        + [vbf(ff, width), vbf(2 * rows_here, BLK), vf(8, width), vf(1, ff), vf(width, BLK)]
        + [vbf(SIZES[n][0], SIZES[n][1] // 2) for n in ("qkv", "out", "up", "down")]
        + [vbf(rq, wq), pltpu.VMEM((pairs, 2 * NZ, 2 * BLK), jnp.int32), vf(rows_here, width), vf(rows_here, 1), vf(8, width),
           vf(8, ff), vf(rq, wq)]
        + reduce_scratch(r, cols, split) + reduce_scratch(*SIZES["out"])
        + [vbf(*ru[0]), vbf(*ru[5]), vbf(*ru[6])] + line_scratch(*SIZES["up"][:2]) + line_scratch(rq, wq)
        + [pltpu.SemaphoreType.DMA((count,)), pltpu.SemaphoreType.DMA((count,)), pltpu.SemaphoreType.DMA((4, PARTS)),
           pltpu.SemaphoreType.DMA((13,))],
        compiler_params=pltpu.CompilerParams(collective_id=0, has_side_effects=True, vmem_limit_bytes=62 * 2**20),
    )(w_qkv, w_out, w_up, w_down, vectors, up_bias, route, tokens, upstream)


def back_pair(scale, dm, perm, pool, up_ref, gp, sums, p, par):
    nblk = dm.shape[0] // BLK
    share = BLK // nblk
    half = nblk * BLK
    width = dm.shape[1]
    keep = head_lanes(128)
    lane = lambda o: pl.ds(mult(par * 384 + o, 128), 128)
    col = lambda o: pl.ds(mult(p * 128 + o * width, 128), 128)
    for k in range(nblk):
        table = one_hot(perm[p, k:k + 1, :], BLK)
        moved = jnp.where(keep, dot(table, dm[pl.ds(k * BLK, BLK), col(0)], 0, 0), 0.0).astype(jnp.bfloat16)
        for c in range(2 * nblk):
            up_ref[pl.ds(c * BLK + k * share, share), :] = moved[c * share:(c + 1) * share]
    for h in range(2):
        rows = pl.ds(h * half, half)
        q, kk, v = [pool[rows, lane(o)].reshape(nblk, BLK, 128) for o in (0, 128, 256)]
        probs = pool[pl.ds(2 * half, half), pl.ds(mult((2 * par + h) * 128, 128), 128)].reshape(nblk, BLK, BLK)
        up = up_ref[rows, :].reshape(nblk, BLK, 128)
        dprobs = bdot(up, v, 2, 2)
        p32 = probs.astype(jnp.float32)
        pd = p32 * dprobs
        dscores = (pd - p32 * jnp.sum(pd, axis=-1, keepdims=True)).astype(jnp.bfloat16)
        parts = (bdot(dscores, kk, 2, 1) * scale, bdot(dscores, q, 1, 1) * scale, bdot(probs, up, 1, 1))
        for j, g in enumerate(parts):
            gp[:, pl.ds(3 * width + h * 384 + j * 128, 128)] = g.reshape(half, 128).astype(jnp.bfloat16)
    total = jnp.zeros((1, 384), jnp.float32)
    for k in range(nblk):
        table = one_hot(perm[p, k:k + 1, :], BLK)
        back = jnp.concatenate(
            [gp[pl.ds(c * BLK + k * share, share), pl.ds(3 * width + h * 384, 384)] for h in range(2) for c in range(nblk)], axis=0)
        moved = dot(table, back, 1, 0)
        total = total + jnp.sum(moved, axis=0, keepdims=True)
        for j in range(3):
            gp[pl.ds(k * BLK, BLK), col(j)] = moved[:, j * 128:(j + 1) * 128].astype(jnp.bfloat16)
    sums[6:7, col(0)] = total[:, 0:128]
    sums[7:8, col(0)] = total[:, 256:384]


def homes(tokens, w_qkv, w_out, w_up, w_down, vectors, up_bias, cluster_route, upstream):
    pairs = H // 2
    scale = (tokens.shape[1] // H) ** -0.5
    step = up_bias.shape[0]
    out_rows, gx_rows, r_qkv, r_aux, r_out, r_up, r_down = layer_call(
        scale, pairs, w_qkv, w_out, w_up, w_down, vectors, up_bias[None], cluster_route, tokens, upstream)[4:]
    return (out_rows, gx_rows, r_qkv, r_out, r_up, r_down, r_aux[:, 0:8].T, r_aux[0, 128:128 + step])


def solution(mesh):
    small = dict(mesh.shape) == {"dp": 4, "seq": 2 * NZ}
    rows = P(ALL, None)
    return jax.shard_map(
        homes if small else shards, mesh=mesh,
        in_specs=(rows,) * 5 + (P(None, ALL), P(ALL), P("dp", None, None), rows),
        out_specs=(rows,) * 6 + (P(None, ALL), P(ALL)),
        check_vma=False,
    )
```

```python
import functools

import jax
import jax.numpy as jnp
from jax import lax
from jax.experimental import pallas as pl
from jax.experimental.pallas import tpu as pltpu
from jax.sharding import PartitionSpec as P

H = 12
CL = 128


epsilon = 1e-06


def normalize(resid, norm_gain, norm_shift):
    average = jnp.mean(resid, axis=-1, keepdims=True)
    centred = resid - average
    spread = jnp.mean(centred * centred, axis=-1, keepdims=True)
    scaled = lax.rsqrt(spread + epsilon)
    normed = centred * scaled
    return (normed * norm_gain + norm_shift, normed, scaled)


def norm_back(grad_output, normed, scaled, norm_gain):
    grad_norm = grad_output * norm_gain
    first_term = jnp.mean(grad_norm, axis=-1, keepdims=True)
    second_term = jnp.mean(grad_norm * normed, axis=-1, keepdims=True)
    return scaled * (grad_norm - first_term - normed * second_term)


def exact_gelu(value):
    return jax.nn.gelu(value, approximate=False)


def order_table(sending):
    heads, rows_here = sending.shape
    columns = jnp.arange(rows_here, dtype=jnp.int32)[None, None, :]
    return (sending[:, :, None] == columns).astype(jnp.bfloat16)


def to_slots(source_rows, table):
    moved = jnp.einsum("hrs,skhe->rkhe", table, source_rows, preferred_element_type=jnp.float32)
    return moved.astype(jnp.bfloat16)


def to_tokens(source_rows, table):
    moved = jnp.einsum("hrs,rkhe->skhe", table, source_rows, preferred_element_type=jnp.float32)
    return moved.astype(jnp.bfloat16)


def cluster_scores(query_c, key_c, scale_factor):
    return (
        jnp.einsum("cahe,cbhe->hcab", query_c, key_c, preferred_element_type=jnp.float32)
        * scale_factor
    )


def shards(tokens, w_qkv, w_out, w_up, w_down, vectors, up_bias, cluster_route, upstream):
    lane_count = lax.axis_size("seq")
    lane_index = lax.axis_index("seq")
    wide_qkv, wide_out, wide_up, wide_down, wide_vectors, wide_bias = (
        lax.all_gather(w_qkv, ("dp", "seq"), axis=0, tiled=True),
        lax.all_gather(w_out, ("dp", "seq"), axis=0, tiled=True),
        lax.all_gather(w_up, ("dp", "seq"), axis=0, tiled=True),
        lax.all_gather(w_down, ("dp", "seq"), axis=0, tiled=True),
        lax.all_gather(vectors, ("dp", "seq"), axis=1, tiled=True),
        lax.all_gather(up_bias, ("dp", "seq"), axis=0, tiled=True),
    )
    rows_here = tokens.shape[0]
    model_width = tokens.shape[1]
    head_size = model_width // H
    portion = rows_here // lane_count
    clusters = rows_here // CL
    scale_factor = head_size ** (-0.5)
    vector_rows = wide_vectors.astype(jnp.float32)
    route_rows = cluster_route[0]
    by_target = lax.dynamic_slice_in_dim(route_rows, lane_index * rows_here, rows_here, 1)
    sending = jnp.swapaxes(by_target.reshape(H, lane_count, portion), 1, 2).reshape(H, rows_here)
    table = order_table(sending)
    projected = jnp.dot(tokens, wide_qkv, preferred_element_type=jnp.float32)
    shifts = jnp.concatenate(
        [vector_rows[0], jnp.zeros((model_width,), jnp.float32), vector_rows[1]]
    )
    projected = (projected + shifts).astype(jnp.bfloat16).reshape(rows_here, 3, H, head_size)
    outgoing = to_slots(projected, table)
    arrived = lax.all_to_all(
        outgoing.reshape(portion, lane_count, 3 * model_width),
        "seq",
        split_axis=1,
        concat_axis=1,
        tiled=True,
    )
    slot_qkv = arrived.reshape(clusters, CL, 3, H, head_size)
    query_c = slot_qkv[:, :, 0]
    key_c = slot_qkv[:, :, 1]
    value_c = slot_qkv[:, :, 2]
    scores = cluster_scores(query_c, key_c, scale_factor)
    row_peak = jnp.max(scores, axis=-1, keepdims=True)
    exponent = jnp.exp(scores - row_peak)
    row_total = jnp.sum(exponent, axis=-1, keepdims=True)
    soft_weights = exponent / row_total
    log_total = row_peak + jnp.log(row_total)
    heads_slot = jnp.einsum(
        "hcab,cbhe->cahe",
        soft_weights.astype(jnp.bfloat16),
        value_c,
        preferred_element_type=jnp.float32,
    ).astype(jnp.bfloat16)
    returned = lax.all_to_all(
        heads_slot.reshape(portion, lane_count, model_width),
        "seq",
        split_axis=1,
        concat_axis=1,
        tiled=True,
    )
    mixed_heads = to_tokens(returned.reshape(rows_here, 1, H, head_size), table).reshape(
        rows_here, model_width
    )
    attention = jnp.dot(mixed_heads, wide_out, preferred_element_type=jnp.float32) + vector_rows[2]
    first_norm, first_normed, first_scaled = normalize(
        tokens.astype(jnp.float32) + attention, vector_rows[4], vector_rows[5]
    )
    first_low = first_norm.astype(jnp.bfloat16)
    widened = jnp.dot(first_low, wide_up, preferred_element_type=jnp.float32) + wide_bias.astype(
        jnp.float32
    )
    activated, gelu_pull = jax.vjp(exact_gelu, widened)
    activated_low = activated.astype(jnp.bfloat16)
    narrowed = (
        jnp.dot(activated_low, wide_down, preferred_element_type=jnp.float32) + vector_rows[3]
    )
    output, second_normed, second_scaled = normalize(
        first_norm + narrowed, vector_rows[6], vector_rows[7]
    )
    back_qkv, back_out, back_up, back_down = (
        lax.all_gather(w_qkv, ("dp", "seq"), axis=0, tiled=True),
        lax.all_gather(w_out, ("dp", "seq"), axis=0, tiled=True),
        lax.all_gather(w_up, ("dp", "seq"), axis=0, tiled=True),
        lax.all_gather(w_down, ("dp", "seq"), axis=0, tiled=True),
    )
    grad_output = upstream.astype(jnp.float32)
    grad_gain_two = jnp.sum(grad_output * second_normed, axis=0)
    grad_shift_two = jnp.sum(grad_output, axis=0)
    grad_second = norm_back(grad_output, second_normed, second_scaled, vector_rows[6])
    grad_narrow = grad_second.astype(jnp.bfloat16)
    grad_down_w = jnp.einsum(
        "tf,td->fd", activated_low, grad_narrow, preferred_element_type=jnp.float32
    )
    grad_down_bias = jnp.sum(grad_narrow.astype(jnp.float32), axis=0)
    grad_active = jnp.einsum(
        "td,fd->tf", grad_narrow, back_down, preferred_element_type=jnp.float32
    )
    grad_wide = gelu_pull(grad_active)[0].astype(jnp.bfloat16)
    grad_up_w = jnp.einsum("td,tf->df", first_low, grad_wide, preferred_element_type=jnp.float32)
    grad_lift_bias = jnp.sum(grad_wide.astype(jnp.float32), axis=0)
    grad_first = grad_second + jnp.einsum(
        "tf,df->td", grad_wide, back_up, preferred_element_type=jnp.float32
    )
    grad_gain_one = jnp.sum(grad_first * first_normed, axis=0)
    grad_shift_one = jnp.sum(grad_first, axis=0)
    grad_resid = norm_back(grad_first, first_normed, first_scaled, vector_rows[4])
    grad_attn = grad_resid.astype(jnp.bfloat16)
    grad_out_w = jnp.einsum("td,te->de", mixed_heads, grad_attn, preferred_element_type=jnp.float32)
    grad_out_bias = jnp.sum(grad_attn.astype(jnp.float32), axis=0)
    grad_mixed = jnp.einsum(
        "te,de->td", grad_attn, back_out, preferred_element_type=jnp.float32
    ).astype(jnp.bfloat16)
    grad_sending = to_slots(grad_mixed.reshape(rows_here, 1, H, head_size), table)
    grad_slot = lax.all_to_all(
        grad_sending.reshape(portion, lane_count, model_width),
        "seq",
        split_axis=1,
        concat_axis=1,
        tiled=True,
    )
    grad_slot = grad_slot.reshape(clusters, CL, H, head_size)
    scores = cluster_scores(query_c, key_c, scale_factor)
    soft_weights = jnp.exp(scores - log_total)
    grad_soft = jnp.einsum(
        "cahe,cbhe->hcab", grad_slot, value_c, preferred_element_type=jnp.float32
    )
    inner_sum = jnp.sum(soft_weights * grad_soft, axis=-1, keepdims=True)
    grad_scores = (soft_weights * (grad_soft - inner_sum)).astype(jnp.bfloat16)
    grad_query = (
        jnp.einsum("hcab,cbhe->cahe", grad_scores, key_c, preferred_element_type=jnp.float32)
        * scale_factor
    )
    grad_key = (
        jnp.einsum("hcab,cahe->cbhe", grad_scores, query_c, preferred_element_type=jnp.float32)
        * scale_factor
    )
    grad_value = jnp.einsum(
        "hcab,cahe->cbhe",
        soft_weights.astype(jnp.bfloat16),
        grad_slot,
        preferred_element_type=jnp.float32,
    )
    grad_slots = jnp.stack([grad_query, grad_key, grad_value], axis=2).astype(jnp.bfloat16)
    came_back = lax.all_to_all(
        grad_slots.reshape(portion, lane_count, 3 * model_width),
        "seq",
        split_axis=1,
        concat_axis=1,
        tiled=True,
    )
    grad_proj = to_tokens(came_back.reshape(rows_here, 3, H, head_size), table).reshape(
        rows_here, 3 * model_width
    )
    grad_qkv_w = jnp.einsum("td,tf->df", tokens, grad_proj, preferred_element_type=jnp.float32)
    bias_sums = jnp.sum(grad_proj.astype(jnp.float32), axis=0).reshape(3, model_width)
    grad_tokens = (
        jnp.einsum("tf,df->td", grad_proj, back_qkv, preferred_element_type=jnp.float32)
        + grad_resid
    ).astype(jnp.bfloat16)
    grad_vector_rows = jnp.stack(
        [
            bias_sums[0],
            bias_sums[2],
            grad_out_bias,
            grad_down_bias,
            grad_gain_one,
            grad_shift_one,
            grad_gain_two,
            grad_shift_two,
        ]
    )
    shares = (
        lax.psum_scatter(grad_qkv_w, ("dp", "seq"), scatter_dimension=0, tiled=True),
        lax.psum_scatter(grad_out_w, ("dp", "seq"), scatter_dimension=0, tiled=True),
        lax.psum_scatter(grad_up_w, ("dp", "seq"), scatter_dimension=0, tiled=True),
        lax.psum_scatter(grad_down_w, ("dp", "seq"), scatter_dimension=0, tiled=True),
        lax.psum_scatter(grad_vector_rows, ("dp", "seq"), scatter_dimension=1, tiled=True),
        lax.psum_scatter(grad_lift_bias, ("dp", "seq"), scatter_dimension=0, tiled=True),
    )
    return (
        output.astype(jnp.bfloat16),
        grad_tokens,
        shares[0],
        shares[1],
        shares[2],
        shares[3],
        shares[4],
        shares[5],
    )


MESH = pl.DeviceIdType.MESH
NZ = 4
BLK = 128

class Links:
    def __init__(self, send_sems, recv_sems):
        self.send_sems, self.recv_sems, self.count, self.drains, self.key = send_sems, recv_sems, 0, {}, None
        self.dp, self.sq = lax.axis_index("dp"), lax.axis_index("seq")
        self.x, self.y = lax.rem(self.dp, 2), self.dp // 2
        self.core, self.z = lax.rem(self.sq, 2), self.sq // 2
        self.sib = self.sq + 1 - 2 * self.core
        self.dp_x = self.dp + 1 - 2 * self.x
        self.dp_y = self.dp + 2 - 4 * self.y

    def peers(self):
        return jnp.where(self.core == 0, self.dp_x, self.dp_y), jnp.where(self.core == 0, self.dp_y, self.dp_x)

    def new(self):
        self.count += 1
        return self.count - 1

    def copy(self, i, src, dst, dp, sq):
        return pltpu.make_async_remote_copy(
            src_ref=src, dst_ref=dst, send_sem=self.send_sems.at[i], recv_sem=self.recv_sems.at[i],
            device_id=(dp, sq), device_id_type=MESH)

    def enter(self, near=True, line=True):
        barrier = pltpu.get_barrier_semaphore()
        n = 0
        if near:
            for dp in (self.dp_x, self.dp_y):
                pl.semaphore_signal(barrier, inc=1, device_id=(dp, self.sq), device_id_type=MESH)
                n += 1
        if line:
            for j in range(1, 2 * NZ):
                pl.semaphore_signal(barrier, inc=1, device_id=(self.dp, lax.rem(self.sq + j, 2 * NZ)), device_id_type=MESH)
                n += 1
        pl.semaphore_wait(barrier, n)

    def go(self, *makers):
        for make in makers:
            make().start()
            self.add(lambda make=make: make().wait_send())

    def drain(self, keys=None):
        for key in list(self.drains) if keys is None else keys:
            for d in self.drains.pop(key, []):
                d()

    def add(self, d):
        self.drains.setdefault(self.key, []).append(d)

    def under(self, key, stages):
        def run(stage):
            before, self.key = self.key, key
            stage()
            self.key = before
        return [functools.partial(run, stage) for stage in stages]


def mult(v, m):
    return pl.multiple_of(v, m)


def gather(L, shard, full, half_buf, r, split):
    half = full.shape[1] // 2
    a, b = split
    big = 2 * r
    mine = pl.ds(mult(L.core * half, 128), half)
    other = pl.ds(mult((1 - L.core) * half, 128), half)
    cols_a = pl.ds(mult(L.core * half, 128), a)
    cols_b = pl.ds(mult(L.core * half + a, 128), b)
    chip = lambda z: pl.ds(mult((L.dp * NZ + z) * big, 16), big)
    quarter = lambda dp, n=1: pl.ds(mult(dp * NZ * big, 16), n * NZ * big)
    i0 = L.new()
    fr = [None] + [L.new() for _ in range(3)]
    fl = [None] + [L.new() for _ in range(3)]
    a1, b1, a2, a3, b2, b3, c0, c1, c2 = [L.new() for _ in range(9)]
    fa, fb = L.peers()
    opposite = 3 - L.dp
    first = lambda: L.copy(i0, shard.at[:, other], half_buf, L.dp, L.sib)

    def right(d, z0):
        return L.copy(fr[d], full.at[chip(z0), mine], full.at[chip(z0), mine], L.dp, L.sq + 2)

    def left(d, z0):
        return L.copy(fl[d], full.at[chip(z0), mine], full.at[chip(z0), mine], L.dp, L.sq - 2)

    def send_line(d):
        @pl.when((L.z >= d - 1) & (L.z < NZ - 1))
        def _():
            right(d, L.z - d + 1).start()

        @pl.when((L.z <= NZ - d) & (L.z > 0))
        def _():
            left(d, L.z + d - 1).start()

    def drain_line(d):
        @pl.when((L.z >= d - 1) & (L.z < NZ - 1))
        def _():
            right(d, L.z - d + 1).wait_send()

        @pl.when((L.z <= NZ - d) & (L.z > 0))
        def _():
            left(d, L.z + d - 1).wait_send()

    def recv_line(d):
        @pl.when(L.z >= d)
        def _():
            right(d, L.z - d).wait_recv()

        @pl.when(L.z + d <= NZ - 1)
        def _():
            left(d, L.z + d).wait_recv()

    def same(i, rows, cols, dp, sq):
        ref = full.at[rows, cols]
        return L.copy(i, ref, ref, dp, sq)

    def s0():
        L.go(first)

    def s1():
        first().wait_recv()
        own, got = shard[:, mine], half_buf[...]

        @pl.when(L.core == 0)
        def _():
            full[chip(L.z), mine] = jnp.concatenate([own, got], axis=0)

        @pl.when(L.core == 1)
        def _():
            full[chip(L.z), mine] = jnp.concatenate([got, own], axis=0)
        send_line(1)
        L.add(functools.partial(drain_line, 1))

    def s2():
        recv_line(1)
        send_line(2)
        L.add(functools.partial(drain_line, 2))

    def s3():
        recv_line(2)
        send_line(3)
        L.add(functools.partial(drain_line, 3))

    def s4():
        recv_line(3)
        q = lambda: quarter(L.dp)
        L.go(lambda: same(a1, q(), cols_a, fa, L.sq), lambda: same(b1, q(), cols_b, fb, L.sq),
             lambda: same(c0, q(), mine, L.dp, L.sib))

    def s5():
        same(a1, quarter(fa), cols_a, fa, L.sq).wait_recv()
        L.go(lambda: same(a2, quarter(L.dp), cols_a, fb, L.sq), lambda: same(a3, quarter(fa), cols_a, fb, L.sq))
        same(b1, quarter(fb), cols_b, fb, L.sq).wait_recv()
        L.go(lambda: same(b2, quarter(L.dp), cols_b, fa, L.sq), lambda: same(b3, quarter(fb), cols_b, fa, L.sq))

    def s6():
        same(a2, quarter(fb), cols_a, fb, L.sq).wait_recv()
        same(b2, quarter(fa), cols_b, fa, L.sq).wait_recv()
        L.go(lambda: same(c1, quarter(L.dp_x), mine, L.dp, L.sib))
        same(a3, quarter(opposite), cols_a, fb, L.sq).wait_recv()
        same(b3, quarter(opposite), cols_b, fa, L.sq).wait_recv()
        L.go(lambda: same(c2, quarter(2 * (1 - L.y), 2), mine, L.dp, L.sib))

    def s7():
        same(c0, quarter(L.dp), other, L.dp, L.sib).wait_recv()
        same(c1, quarter(L.dp_x), other, L.dp, L.sib).wait_recv()
        same(c2, quarter(2 * (1 - L.y), 2), other, L.dp, L.sib).wait_recv()
    return [s0, s1, s2, s3, s4, s5, s6, s7]


def spread(L, src, dst, local_sem, parts=1):
    ids = [[L.new() for _ in range(2 * NZ - 1)] for _ in range(parts)]
    n = BLK // parts
    rows = lambda s, i: pl.ds(mult(s * BLK + i * n, n), n)

    def keep(i):
        return pltpu.make_async_copy(src.at[rows(L.sq, i)], dst.at[rows(L.sq, i)], local_sem.at[i])

    def move(i, j, to, frm):
        return L.copy(ids[i][j - 1], src.at[rows(to, i)], dst.at[rows(frm, i)], L.dp, to)

    def begin(i=0):
        keep(i).start()
        for j in range(1, 2 * NZ):
            L.go(lambda j=j: move(i, j, lax.rem(L.sq + j, 2 * NZ), L.sq))

    def finish():
        for i in range(parts):
            keep(i).wait()
            for j in range(1, 2 * NZ):
                move(i, j, L.sq, lax.rem(L.sq + 2 * NZ - j, 2 * NZ)).wait_recv()
    return begin, finish


def add_into(dst, rows0, cols, src, n):
    step = 192

    def one(i, _):
        here = pl.ds(mult(i * step, 16), step)
        there = pl.ds(mult(rows0 + i * step, 16), step)
        dst[there, cols] = dst[there, cols] + src[here, :]
        return 0
    lax.fori_loop(0, n // step, one, 0)


def landing(r, c, split):
    half, (a, b), big = c // 2, split, 2 * r
    return [(32 * r, half), (4 * big, a), (4 * big, a), (4 * big, b), (4 * big, b), (4 * big, a), (4 * big, b)]


def line_scratch(r, c):
    half, big = c // 2, 2 * r
    return [pltpu.VMEM((3, big, half), jnp.bfloat16)] * 2 + [pltpu.VMEM((2, r, half), jnp.float32), pltpu.VMEM((r, half), jnp.float32)]


def reduce_scratch(r, c, split):
    return [pltpu.VMEM(shape, jnp.bfloat16) for shape in landing(r, c, split)] + line_scratch(r, c)


N_REDUCE = 15
N_GATHER = 16
N_SCRATCH = 11
N_LINE = 4


def reduce(L, part, out, scratch, r, split):
    acc, a10, a11, b10, b11, a2, b2, from_l, from_r, fin, got = scratch
    half = part.shape[1] // 2
    a, b = split
    big = 2 * r
    mine = pl.ds(mult(L.core * half, 128), half)
    other = pl.ds(mult((1 - L.core) * half, 128), half)
    ca, cb = pl.ds(0, a), pl.ds(a, b)
    quarter = lambda dp, n=1: pl.ds(mult(dp * NZ * big, 16), n * NZ * big)
    chip = lambda z: pl.ds(mult((L.dp * NZ + z) * big, 16), big)
    i0, ia0, ia1, ib0, ib1, ia2, ib2, ifin = [L.new() for _ in range(8)]
    fb, fa = L.peers()
    opposite = 3 - L.dp
    ir = [None] + [L.new() for _ in range(3)]
    il = [L.new() for _ in range(3)]
    q = lambda dp: dp * NZ * big

    core_copy = lambda: L.copy(i0, part.at[:, other], acc, L.dp, L.sib)
    def part_copy(i, dp, cols, to, peer):
        return L.copy(i, acc.at[quarter(dp), cols], to, peer, L.sq)

    a_copies = [lambda: part_copy(ia0, opposite, ca, a10, fa), lambda: part_copy(ia1, fa, ca, a11, fa)]
    b_copies = [lambda: part_copy(ib0, opposite, cb, b10, fb), lambda: part_copy(ib1, fb, cb, b11, fb)]
    a2_copy = lambda: part_copy(ia2, fb, ca, a2, fb)
    b2_copy = lambda: part_copy(ib2, fa, cb, b2, fa)
    def s0():
        L.go(core_copy)

    def s1():
        core_copy().wait_recv()
        step = 192

        def one(i, _):
            here = pl.ds(mult(i * step, 16), step)
            acc[here, :] = acc[here, :] + part[here, mine]
            return 0
        lax.fori_loop(0, 32 * r // step, one, 0)
        L.go(a_copies[0], b_copies[0], a_copies[1], b_copies[1])

    def s2():
        a_copies[0]().wait_recv()
        add_into(acc, q(fb), ca, a10, 4 * big)
        L.go(a2_copy)
        b_copies[0]().wait_recv()
        add_into(acc, q(fa), cb, b10, 4 * big)
        L.go(b2_copy)
        a_copies[1]().wait_recv()
        add_into(acc, q(L.dp), ca, a11, 4 * big)
        b_copies[1]().wait_recv()
        add_into(acc, q(L.dp), cb, b11, 4 * big)

    def s3():
        a2_copy().wait_recv()
        add_into(acc, q(L.dp), ca, a2, 4 * big)
        b2_copy().wait_recv()
        add_into(acc, q(L.dp), cb, b2, 4 * big)

    full_cols = pl.ds(0, half)

    def hop_r(t, src):
        return L.copy(ir[t], src, from_l.at[t - 1], L.dp, L.sq + 2)

    def hop_l(t, src):
        return L.copy(il[t], src, from_r.at[t], L.dp, L.sq - 2)

    def merge(buf, k, t):
        buf[k] = (buf[k].astype(jnp.float32) + acc[chip(t), :].astype(jnp.float32)).astype(jnp.bfloat16)

    def line(s):
        @pl.when(L.z == s)
        def _():
            for t in range(NZ - 1, s, -1):
                if s == 0:
                    hop_r(t, acc.at[chip(t), full_cols]).start()
                else:
                    hop_r(t, from_l.at[t - 1]).wait_recv()
                    merge(from_l, t - 1, t)
                    hop_r(t, from_l.at[t - 1]).start()

        @pl.when(L.z == NZ - 1 - s)
        def _():
            for t in range(0, NZ - 1 - s):
                if s == 0:
                    hop_l(t, acc.at[chip(t), full_cols]).start()
                else:
                    hop_l(t, from_r.at[t]).wait_recv()
                    merge(from_r, t, t)
                    hop_l(t, from_r.at[t]).start()

        def drain():
            @pl.when(L.z == s)
            def _():
                for t in range(NZ - 1, s, -1):
                    hop_r(t, from_l.at[t - 1]).wait_send()

            @pl.when(L.z == NZ - 1 - s)
            def _():
                for t in range(0, NZ - 1 - s):
                    hop_l(t, from_r.at[t]).wait_send()
        L.add(drain)

    fin_copy = lambda: L.copy(ifin, fin.at[1 - L.core], got, L.dp, L.sib)

    def s7():
        for z in range(NZ):
            @pl.when(L.z == z)
            def _(z=z):
                total = acc[chip(z), :].astype(jnp.float32)
                if z > 0:
                    hop_r(z, from_l.at[z - 1]).wait_recv()
                    total = total + from_l[z - 1].astype(jnp.float32)
                if z < NZ - 1:
                    hop_l(z, from_r.at[z]).wait_recv()
                    total = total + from_r[z].astype(jnp.float32)
                fin[...] = total.reshape(2, r, half)
        L.go(fin_copy)

    def s8():
        out[:, mine] = fin[L.core]
        fin_copy().wait_recv()
        out[:, other] = got[...]
    return [s0, s1, s2, s3] + [functools.partial(line, s) for s in range(3)] + [s7, s8]


def one_hot(slots, rows):
    row = lax.broadcasted_iota(jnp.int32, (rows, slots.shape[1]), 0)
    return jnp.where(slots == row, 1.0, 0.0).astype(jnp.bfloat16)


def head_lanes(width):
    row = lax.broadcasted_iota(jnp.int32, (2 * BLK, width), 0)
    lane = lax.rem(lax.broadcasted_iota(jnp.int32, (2 * BLK, width), 1), 128)
    return (row < BLK) == (lane < 64)


def dot(a, b, ca, cb):
    return lax.dot_general(a, b, (((ca,), (cb,)), ((), ())), preferred_element_type=jnp.float32)


def bdot(a, b, ca, cb):
    return lax.dot_general(a, b, (((ca,), (cb,)), ((0,), (0,))), preferred_element_type=jnp.float32)


BATCH = 8


SIZES = {"qkv": (24, 2560, (640, 640)), "out": (24, 768, (256, 128)), "up": (24, 3072, (768, 768)), "down": (96, 768, (128, 256)),
         "qk": (24, 1536, (384, 384)), "v": (24, 1024, (256, 256))}
ALL = ("dp", "seq")
VM = pl.BlockSpec(memory_space=pltpu.VMEM)
BF = jnp.bfloat16
LIMIT = 60 * 2**20


def place_rows(route, perm, me):
    heads, n = 2 * perm.shape[0], 2 * NZ
    size = route.shape[0] * BLK // (heads * n)
    chunks = size // BLK
    base = me * BLK
    pers = [jnp.concatenate([route[pl.ds((h * n) * chunks + c, n, stride=chunks), :] for c in range(chunks)], axis=1)
            for h in range(heads)]
    head_row = jnp.concatenate([per[0:1] for per in pers] + [jnp.full((16 - heads, size), -1, jnp.int32)], axis=0)
    mine = (head_row >= base) & (head_row < base + BLK)
    flags = jnp.where(mine, 1.0, 0.0).astype(jnp.bfloat16)
    before = []
    for c in range(0, size, 128):
        row = lax.broadcasted_iota(jnp.int32, (size, 128), 0)
        col = lax.broadcasted_iota(jnp.int32, (size, 128), 1) + c
        before.append(dot(flags, jnp.where(row < col, 1.0, 0.0).astype(jnp.bfloat16), 1, 0))
    slot = jnp.where(mine, jnp.concatenate(before, axis=1).astype(jnp.int32), -1)
    for h in range(heads):
        per = pers[h]
        local = jnp.where((per >= base) & (per < base + BLK), per - base, 0).astype(jnp.float32).astype(jnp.bfloat16)
        pick = jnp.where(slot[h:h + 1, :] == lax.broadcasted_iota(jnp.int32, (BLK, size), 0), 1.0, 0.0).astype(jnp.bfloat16)
        perm[h // 2, :, pl.ds((h % 2) * BLK, BLK)] = dot(local, pick, 1, 1).astype(jnp.int32)


def front_pair(scale, qkv, width, perm, mixed, pool, head_ref, p, par):
    nblk = qkv.shape[0] // BLK
    share = BLK // nblk
    keep = head_lanes(384)
    cols = pl.ds(mult(par * 384, 128), 384)
    lane = lambda o: pl.ds(mult(par * 384 + o, 128), 128)
    col = lambda o: pl.ds(mult(p * 128 + o * width, 128), 128)
    half = nblk * BLK
    for k in range(nblk):
        here = pl.ds(k * BLK, BLK)
        packed = jnp.concatenate([qkv[here, col(0)], qkv[here, col(1)], qkv[here, col(2)]], axis=1)
        table = one_hot(perm[p, k:k + 1, :], BLK)
        moved = jnp.where(keep, dot(table, packed, 0, 0), 0.0).astype(jnp.bfloat16)
        for c in range(2 * nblk):
            pool[pl.ds(c * BLK + k * share, share), cols] = moved[c * share:(c + 1) * share]
    for h in range(2):
        rows = pl.ds(h * half, half)
        q, kk, v = [pool[rows, lane(o)].reshape(nblk, BLK, 128) for o in (0, 128, 256)]
        scores = bdot(q, kk, 2, 2) * scale
        e = jnp.exp(scores - jnp.max(scores, axis=-1, keepdims=True))
        probs = (e * (1.0 / jnp.sum(e, axis=-1, keepdims=True))).astype(jnp.bfloat16)
        pool[pl.ds(2 * half, half), pl.ds(mult((2 * par + h) * 128, 128), 128)] = probs.reshape(half, BLK)
        head_ref[rows, :] = bdot(probs, v, 2, 1).reshape(half, BLK).astype(jnp.bfloat16)
    for k in range(nblk):
        table = one_hot(perm[p, k:k + 1, :], BLK)
        back = jnp.concatenate([head_ref[pl.ds(c * BLK + k * share, share), :] for c in range(2 * nblk)], axis=0)
        mixed[pl.ds(k * BLK, BLK), col(0)] = dot(table, back, 1, 0).astype(jnp.bfloat16)


def loop(n, body, hooks=()):
    def one(i, _):
        body(i)
        for at, stage in hooks:
            pl.when(i == at)(stage)
        return 0
    lax.fori_loop(0, n, one, 0)


def moments(v):
    mean = jnp.mean(v, axis=-1, keepdims=True)
    centred = v - mean
    inv = lax.rsqrt(jnp.mean(centred * centred, axis=-1, keepdims=True) + epsilon)
    return centred * inv, inv


TB = 256
FB = 768


def layer_kernel(scale, w_shard, out_shard, up_shard, down_shard, vec_shard, ub_shard, route, x_rows, up_rows,
                 x_home, w_home, slots, probs, out_rows, gx_rows, r_qkv, r_aux, r_out, r_up, r_down,
                 w_out, w_up, w_down, act, gp, x, mixed, n1, s1, low, up, outb, dn, gd, head_ref, vec, ub, auxf,
                 bq, bo, bu, bd, qkv_shard, perm, d_res, s2, sums, ubsum, ra, rb, *rest):
    own = [rest[i:i + N_SCRATCH] for i in (0, N_SCRATCH)]
    late = rest[2 * N_SCRATCH:2 * N_SCRATCH + 3 + 3 * N_LINE]
    ss, rs, ls, cs = rest[2 * N_SCRATCH + 3 + 3 * N_LINE:]
    rows_here, width = x.shape
    ff = w_up.shape[1]
    pairs = perm.shape[0]
    w = gp.at[pl.ds(0, width), pl.ds(0, qkv_shard.shape[1])]
    da = up
    L = Links(ss, rs)
    r = w_shard.shape[0]
    nv, step = vec_shard.shape[0], ub_shard.shape[1]
    qkv_shard[:, 0:3 * width] = w_shard[...]
    auxf[...] = jnp.zeros_like(auxf)
    auxf[0:nv, 0:r] = vec_shard[...].astype(jnp.float32)
    qkv_shard[:, 3 * width:3 * width + 128] = auxf[0:128, :].T[0:r, :].astype(jnp.bfloat16)
    auxf[0:nv, :] = jnp.zeros((nv, 128), jnp.float32)
    auxf[0:1, 0:step] = ub_shard[...].astype(jnp.float32)
    qkv_shard[:, 3 * width + 128:3 * width + 256] = auxf[0:r, :].astype(jnp.bfloat16)
    L.enter()
    Q = L.under("qkv", gather(L, qkv_shard, w, bq, *SIZES["qkv"][::2]))
    O = L.under("out", gather(L, out_shard, w_out, bo, *SIZES["out"][::2]))
    U = L.under("up", gather(L, up_shard, w_up, bu, *SIZES["up"][::2]))
    D = L.under("down", gather(L, down_shard, w_down, bd, *SIZES["down"][::2]))
    x_begin, x_finish = spread(L, x_rows, x, ls.at[0])
    up_begin, up_finish = spread(L, up_rows, up, ls.at[1])
    out_begin, out_finish = spread(L, outb, out_rows, ls.at[2])
    gx_begin, gx_finish = spread(L, dn, gx_rows, ls.at[3], PARTS)
    g_up, part = act.at[pl.ds(0, width), :], act.at[pl.ds(0, width), pl.ds(0, SIZES["qkv"][1])]
    spare = [act.at[pl.ds(width, r * 8), pl.ds(i * width, width)] for i in range(4)]
    n_qk, n_v = SIZES["qk"][1], SIZES["v"][1]

    def in_w_up(at, size, pieces):
        q = size // 4
        return [w_up.at[:, pl.ds(at, size // 2)]] + [w_up.at[pl.ds(i * r * 8, r * 8), pl.ds(pieces + j * q, q)]
                                                    for j in range(2) for i in range(3)]
    spare_qk = in_w_up(0, n_qk, (n_qk + n_v) // 2)
    spare_v = in_w_up(n_qk // 2, n_v, (n_qk + n_v) // 2 + n_qk // 2)
    R = reduce(L, gd, r_down, own[0], *SIZES["down"][::2])
    R = L.under("sum", R[:1]) + R[1:]
    SO = reduce(L, w_out, r_out, own[1], *SIZES["out"][::2])
    SU = reduce(L, g_up, r_up, [late[0], *spare, *late[1:3 + N_LINE]], *SIZES["up"][::2])
    SU = L.under("sum_up", SU[:1]) + SU[1:]
    lines = late[3 + N_LINE:]
    SK = reduce(L, act.at[pl.ds(0, width), pl.ds(0, n_qk)], ra, [*spare_qk, *lines[:N_LINE]], *SIZES["qk"][::2])
    SV = reduce(L, act.at[pl.ds(0, width), pl.ds(n_qk, n_v)], rb, [*spare_v, *lines[N_LINE:]], *SIZES["v"][::2])
    plan = PLAN(Q, O, U, D, x_begin, up_begin, R)
    plan.update(LATE(R, SO, SU, SK, SV, [functools.partial(gx_begin, i) for i in range(PARTS)]))
    row = lambda i: vec[i:i + 1, :]

    def run(stages):
        for stage in stages:
            stage()

    run(plan["start"])
    sums[...] = jnp.zeros_like(sums)
    ubsum[...] = jnp.zeros_like(ubsum)
    place_rows(route, perm, L.sq)
    run(plan["placed"])
    vec[...] = w[:, 2304:2432].astype(jnp.float32).T[0:8, :]
    auxf[...] = w[:, 2432:2560].astype(jnp.float32)
    for i in range(ff // step):
        ub[:, i * step:(i + 1) * step] = auxf[i * r:i * r + 1, 0:step]
    w_flush = pltpu.make_async_copy(w, w_home, cs.at[0])
    w_flush.start()
    run(plan["weights"])
    x_finish()
    x_flush = pltpu.make_async_copy(x, x_home, cs.at[1])
    x_flush.start()

    def project(m):
        here = pl.ds(mult(m * TB, TB), TB)
        for j in range(3):
            c = pl.ds(j * width, width)
            r = dot(x[here, :], w[:, c], 1, 0)
            if j != 1:
                r = r + row(j // 2)
            act[here, c] = r.astype(jnp.bfloat16)

    loop(rows_here // TB, project, plan["project"])

    def kept(p, par):
        half = rows_here
        return [pltpu.make_async_copy(gd.at[pl.ds(0, 2 * half), pl.ds(mult(par * 384, 128), 384)], slots.at[p], cs.at[2 + 3 * par])] + [
            pltpu.make_async_copy(gd.at[pl.ds(2 * half, half), pl.ds(mult((2 * par + h) * 128, 128), 128)], probs.at[p, h],
                                  cs.at[3 + 3 * par + h]) for h in range(2)]

    def back_in(p, par):
        half = rows_here
        return [pltpu.make_async_copy(slots.at[p], w_down.at[pl.ds(0, 2 * half), pl.ds(mult(par * 384, 128), 384)], cs.at[2 + 3 * par])] + [
            pltpu.make_async_copy(probs.at[p, h], w_down.at[pl.ds(2 * half, half), pl.ds(mult((2 * par + h) * 128, 128), 128)],
                                  cs.at[3 + 3 * par + h]) for h in range(2)]

    def attend(p):
        par = lax.rem(p, 2)

        @pl.when(p >= 2)
        def _():
            for c in kept(p - 2, par):
                c.wait()
        front_pair(scale, act, width, perm, mixed, gd, head_ref, p, par)
        for c in kept(p, par):
            c.start()

    loop(pairs, attend, plan["attend"])
    w_flush.wait()
    L.drain(["qkv", "out"])

    def first_half(m):
        here = pl.ds(mult(m * TB, TB), TB)
        r1 = x[here, :].astype(jnp.float32) + dot(mixed[here, :], w_out[...], 1, 0) + row(2)
        norm, inv = moments(r1)
        n1[here, :] = norm
        s1[here, :] = inv
        lo = (norm * row(4) + row(5)).astype(jnp.bfloat16)
        low[here, :] = lo
        for f in range(0, ff, FB):
            c = pl.ds(f, FB)
            wide = dot(lo, w_up[:, c], 1, 0) + ub[:, c]
            cdf = 0.5 + 0.5 * lax.erf(wide * 0.7071067811865476)
            act[here, c] = (wide * cdf).astype(jnp.bfloat16)
            gp[here, c] = (cdf + wide * (0.3989422804014327 * jnp.exp(-0.5 * wide * wide))).astype(jnp.bfloat16)

    loop(rows_here // TB, first_half, plan["first"])
    run(plan["firsts"])
    for p in range(pairs - 2, pairs):
        for c in kept(p, p % 2):
            c.wait()
    x_flush.wait()

    def second(m):
        here = pl.ds(mult(m * TB, TB), TB)
        first = n1[here, :] * row(4) + row(5)
        r2 = first + dot(act[here, :], w_down[...], 1, 0) + row(3)
        n2, inv = moments(r2)
        outb[here, :] = (n2 * row(6) + row(7)).astype(jnp.bfloat16)
        d_res[here, :] = n2
        s2[here, :] = inv

    loop(rows_here // TB, second)
    out_begin()
    up_finish()

    def second_back(m):
        here = pl.ds(mult(m * TB, TB), TB)
        n2 = d_res[here, :]
        g = up[here, :].astype(jnp.float32)
        sums[4:5, :] += jnp.sum(g * n2, axis=0, keepdims=True)
        sums[5:6, :] += jnp.sum(g, axis=0, keepdims=True)
        d = norm_back(g, n2, s2[here, :], row(6))
        d_res[here, :] = d
        lo = d.astype(jnp.bfloat16)
        dn[here, :] = lo
        sums[1:2, :] += jnp.sum(lo.astype(jnp.float32), axis=0, keepdims=True)

    loop(rows_here // TB, second_back)

    def grad_down(i):
        c = pl.ds(mult(i * FB, FB), FB)
        gd[c, :] = dot(act[:, c], dn[...], 0, 0).astype(jnp.bfloat16)

    loop(ff // FB, grad_down)
    R[0]()

    def third(m):
        here = pl.ds(mult(m * TB, TB), TB)
        total = d_res[here, :]
        lo = dn[here, :]
        for f in range(0, ff, FB):
            c = pl.ds(f, FB)
            dw = (dot(lo, w_down[c, :], 1, 1) * gp[here, c].astype(jnp.float32)).astype(jnp.bfloat16)
            gp[here, c] = dw
            ubsum[0:1, c] += jnp.sum(dw.astype(jnp.float32), axis=0, keepdims=True)
            total = total + dot(dw, w_up[:, c], 1, 1)
        norm = n1[here, :]
        sums[2:3, :] += jnp.sum(total * norm, axis=0, keepdims=True)
        sums[3:4, :] += jnp.sum(total, axis=0, keepdims=True)
        d = norm_back(total, norm, s1[here, :], row(4))
        d_res[here, :] = d
        lo = d.astype(jnp.bfloat16)
        da[here, :] = lo
        sums[0:1, :] += jnp.sum(lo.astype(jnp.float32), axis=0, keepdims=True)
        x[here, :] = dot(lo, w_out[...], 1, 1).astype(jnp.bfloat16)

    loop(rows_here // TB, third, plan["third"])
    L.drain(["down"])
    for p in range(2):
        for c in back_in(p, p):
            c.start()

    def grad_up(i):
        c = pl.ds(mult(i * FB, FB), FB)
        act[pl.ds(0, width), c] = dot(low[...], gp[:, c], 0, 0).astype(jnp.bfloat16)

    loop(ff // FB, grad_up, plan["grad_up"])
    L.drain(["up"])
    run(plan["up_ready"])
    w_out[...] = dot(mixed[...], da[...], 0, 0).astype(jnp.bfloat16)
    run(plan["out_ready"])
    L.drain(["sum"])
    reload = [pltpu.make_async_copy(w_home.at[:, pl.ds(j * width, width)], gd.at[pl.ds(j * width, width), :], cs.at[10 + j])
              for j in range(3)]
    for c in reload:
        c.start()

    def back(p):
        par = lax.rem(p, 2)
        for c in back_in(p, par):
            c.wait()
        back_pair(scale, x, perm, w_down, head_ref, gp, sums, p, par)

        @pl.when(p < pairs - 2)
        def _():
            for c in back_in(p + 2, par):
                c.start()

    loop(pairs, back, plan["back"])
    x_again = pltpu.make_async_copy(x_home, x, cs.at[0])
    x_again.start()
    for c in reload:
        c.wait()

    def grad_x(m):
        here = pl.ds(mult(m * TB, TB), TB)
        total = d_res[here, :]
        for j in range(3):
            total = total + dot(gp[here, pl.ds(j * width, width)], gd[pl.ds(j * width, width), :], 1, 1)
        dn[here, :] = total.astype(jnp.bfloat16)

    loop(rows_here // TB, grad_x)
    run(plan["x_ready"])
    x_again.wait()
    L.drain(["sum_up"])

    def grad_qkv(i):
        c = pl.ds(mult(i * FB, FB), FB)
        part[:, c] = dot(x[...], gp[:, c], 0, 0).astype(jnp.bfloat16)

    loop(3 * width // FB, grad_qkv, plan["qkv"])
    d_res[0:BLK, :] = jnp.zeros((BLK, width), jnp.float32)
    d_res[0:2, :] = sums[6:8, :]
    d_res[2:8, :] = sums[0:6, :]
    part[:, 3 * width:3 * width + 128] = d_res[0:BLK, :].T.astype(jnp.bfloat16)
    auxf[...] = jnp.zeros_like(auxf)
    for i in range(ff // step):
        auxf[i * r:i * r + 1, 0:step] = ubsum[0:1, i * step:(i + 1) * step]
    part[:, 3 * width + 128:3 * width + 256] = auxf[...].astype(jnp.bfloat16)
    run(plan["end"])
    r_qkv[:, 0:n_qk] = ra[...]
    r_qkv[:, n_qk:3 * width] = rb[:, 0:3 * width - n_qk]
    r_aux[...] = rb[:, 3 * width - n_qk:n_v]
    out_finish()
    gx_finish()
    L.drain()


def PLAN(Q, O, U, D, x_begin, up_begin, R):
    return {
        "start": [Q[0],O[0],U[0],D[0],Q[1],O[1],U[1],Q[2],O[2],U[2],Q[3],O[3],U[3],Q[4],x_begin,D[1],Q[5],O[4],U[4]],
        "placed": [Q[6],Q[7]],
        "weights": [O[5],U[5]],
        "project": [(1,D[2])],
        "attend": [(0,D[3]),(0,up_begin),(0,O[6]),(0,U[6]),(2,O[7]),(2,U[7]),(3,D[4])],
        "first": [(0,D[5]),(3,D[6])],
        "firsts": [D[7]],
    }


def LATE(R, O, U, K, V, G):
    return {
        "third": [(0, R[1])],
        "grad_up": [],
        "up_ready": [R[2], U[0]],
        "out_ready": [O[0]],
        "back": [(0, U[1]), (1, R[3]), (1, R[4]), (2, O[1]), (3, R[5]), (4, R[6]), (5, R[7])],
        "x_ready": [G[0], G[1], U[2], O[2]],
        "qkv": [(1, K[0])],
        "end": [V[0], R[8], U[3], U[4], G[2], K[1], V[1], O[3], O[4], U[5], G[3], K[2], V[2], U[6], O[5], K[3], K[4], O[6],
                V[3], V[4], K[5], U[7], O[7], V[5], K[6], V[6], K[7], V[7], U[8], O[8], K[8], V[8]],
    }


PARTS = 4


def layer_call(scale, pairs, w_qkv, w_out, w_up, w_down, vectors, up_bias, route, tokens, upstream):
    rows_here, width = tokens.shape
    ff = w_up.shape[1]
    r, cols, split = SIZES["down"]
    wq = SIZES["qkv"][1]
    count = 4 * N_GATHER + 5 * N_REDUCE + 7 * (3 + PARTS)
    f32 = lambda *s: jax.ShapeDtypeStruct(s, jnp.float32)
    bf = lambda *s: jax.ShapeDtypeStruct(s, BF)
    vbf = lambda *s: pltpu.VMEM(s, BF)
    vf = lambda *s: pltpu.VMEM(s, jnp.float32)
    hbm = pl.BlockSpec(memory_space=pl.ANY)
    ru = landing(*SIZES["up"])
    rq = SIZES["qkv"][0]
    return pl.pallas_call(
        functools.partial(layer_kernel, scale),
        out_shape=[bf(rows_here, width), bf(width, wq), bf(pairs, 2 * rows_here, 384), bf(pairs, 2, rows_here, BLK),
                   bf(rows_here, width), bf(rows_here, width), f32(rq, 3 * width), f32(rq, 256), f32(*SIZES["out"][:2]),
                   f32(*SIZES["up"][:2]), f32(r, cols)],
        in_specs=[VM] * 7 + [hbm] * 2,
        out_specs=[hbm] * 6 + [VM] * 5,
        scratch_shapes=[vbf(width, width), vbf(width, ff), vbf(ff, width), vbf(rows_here, ff), vbf(rows_here, ff),
                        vbf(rows_here, width), vbf(rows_here, width), vf(rows_here, width), vf(rows_here, 1)]
        + [vbf(rows_here, width)] * 4
        + [vbf(ff, width), vbf(2 * rows_here, BLK), vf(8, width), vf(1, ff), vf(width, BLK)]
        + [vbf(SIZES[n][0], SIZES[n][1] // 2) for n in ("qkv", "out", "up", "down")]
        + [vbf(rq, wq), pltpu.VMEM((pairs, 2 * NZ, 2 * BLK), jnp.int32), vf(rows_here, width), vf(rows_here, 1), vf(8, width),
           vf(8, ff), vf(rq, SIZES["qk"][1]), vf(rq, SIZES["v"][1])]
        + reduce_scratch(r, cols, split) + reduce_scratch(*SIZES["out"])
        + [vbf(*ru[0]), vbf(*ru[5]), vbf(*ru[6])] + line_scratch(*SIZES["up"][:2])
        + line_scratch(*SIZES["qk"][:2]) + line_scratch(*SIZES["v"][:2])
        + [pltpu.SemaphoreType.DMA((count,)), pltpu.SemaphoreType.DMA((count,)), pltpu.SemaphoreType.DMA((4, PARTS)),
           pltpu.SemaphoreType.DMA((13,))],
        compiler_params=pltpu.CompilerParams(collective_id=0, has_side_effects=True, vmem_limit_bytes=62 * 2**20),
    )(w_qkv, w_out, w_up, w_down, vectors, up_bias, route, tokens, upstream)


def back_pair(scale, dm, perm, pool, up_ref, gp, sums, p, par):
    nblk = dm.shape[0] // BLK
    share = BLK // nblk
    half = nblk * BLK
    width = dm.shape[1]
    keep = head_lanes(128)
    lane = lambda o: pl.ds(mult(par * 384 + o, 128), 128)
    col = lambda o: pl.ds(mult(p * 128 + o * width, 128), 128)
    for k in range(nblk):
        table = one_hot(perm[p, k:k + 1, :], BLK)
        moved = jnp.where(keep, dot(table, dm[pl.ds(k * BLK, BLK), col(0)], 0, 0), 0.0).astype(jnp.bfloat16)
        for c in range(2 * nblk):
            up_ref[pl.ds(c * BLK + k * share, share), :] = moved[c * share:(c + 1) * share]
    for h in range(2):
        rows = pl.ds(h * half, half)
        q, kk, v = [pool[rows, lane(o)].reshape(nblk, BLK, 128) for o in (0, 128, 256)]
        probs = pool[pl.ds(2 * half, half), pl.ds(mult((2 * par + h) * 128, 128), 128)].reshape(nblk, BLK, BLK)
        up = up_ref[rows, :].reshape(nblk, BLK, 128)
        dprobs = bdot(up, v, 2, 2)
        p32 = probs.astype(jnp.float32)
        pd = p32 * dprobs
        dscores = (pd - p32 * jnp.sum(pd, axis=-1, keepdims=True)).astype(jnp.bfloat16)
        parts = (bdot(dscores, kk, 2, 1) * scale, bdot(dscores, q, 1, 1) * scale, bdot(probs, up, 1, 1))
        for j, g in enumerate(parts):
            gp[:, pl.ds(3 * width + h * 384 + j * 128, 128)] = g.reshape(half, 128).astype(jnp.bfloat16)
    total = jnp.zeros((1, 384), jnp.float32)
    for k in range(nblk):
        table = one_hot(perm[p, k:k + 1, :], BLK)
        back = jnp.concatenate(
            [gp[pl.ds(c * BLK + k * share, share), pl.ds(3 * width + h * 384, 384)] for h in range(2) for c in range(nblk)], axis=0)
        moved = dot(table, back, 1, 0)
        total = total + jnp.sum(moved, axis=0, keepdims=True)
        for j in range(3):
            gp[pl.ds(k * BLK, BLK), col(j)] = moved[:, j * 128:(j + 1) * 128].astype(jnp.bfloat16)
    sums[6:7, col(0)] = total[:, 0:128]
    sums[7:8, col(0)] = total[:, 256:384]


def settle_kernel(n, *refs):
    ins, aux, outs, (gv, gb), bufs, sem = refs[:n], refs[n], refs[n + 1:2 * n + 1], refs[2 * n + 1:2 * n + 3], refs[2 * n + 3:-1], refs[-1]
    loads = [pltpu.make_async_copy(a, b, sem.at[0, i]) for i, (a, b) in enumerate(zip(ins, bufs))]
    stores = [pltpu.make_async_copy(a, b, sem.at[1, i]) for i, (a, b) in enumerate(zip(bufs, outs))]
    for c in loads:
        c.start()
    gv[...] = aux[:, 0:128].T[0:gv.shape[0], :]
    gb[...] = aux[0:1, 128:128 + gb.shape[1]]
    for c, d in zip(loads, stores):
        c.wait()
        d.start()
    for d in stores:
        d.wait()


def settle(arrays, aux, n_vec, n_bias):
    hbm = pl.BlockSpec(memory_space=pl.ANY)
    like = lambda a: jax.ShapeDtypeStruct(a.shape, a.dtype)
    f32 = lambda *s: jax.ShapeDtypeStruct(s, jnp.float32)
    return pl.pallas_call(
        functools.partial(settle_kernel, len(arrays)), out_shape=[like(a) for a in arrays] + [f32(n_vec, aux.shape[0]), f32(1, n_bias)],
        in_specs=[hbm] * len(arrays) + [VM], out_specs=[hbm] * len(arrays) + [VM] * 2,
        scratch_shapes=[pltpu.VMEM(a.shape, a.dtype) for a in arrays] + [pltpu.SemaphoreType.DMA((2, len(arrays)))],
        compiler_params=pltpu.CompilerParams(vmem_limit_bytes=LIMIT),
    )(*arrays, aux)


def homes(tokens, w_qkv, w_out, w_up, w_down, vectors, up_bias, cluster_route, upstream):
    pairs = H // 2
    scale = (tokens.shape[1] // H) ** -0.5
    step = up_bias.shape[0]
    out_rows, gx_rows, r_qkv, r_aux, r_out, r_up, r_down = layer_call(
        scale, pairs, w_qkv, w_out, w_up, w_down, vectors, up_bias[None], cluster_route.reshape(-1, BLK), tokens, upstream)[4:]
    gx, out, g_qkv, g_up, g_down, g_out, g_vec, g_bias = settle(
        [gx_rows, out_rows, r_qkv, r_up, r_down, r_out], r_aux, vectors.shape[0], step)
    return out, gx, g_qkv, g_out, g_up, g_down, g_vec, g_bias[0]


def solution(mesh):
    small = dict(mesh.shape) == {"dp": 4, "seq": 2 * NZ}
    rows = P(ALL, None)
    return jax.shard_map(
        homes if small else shards, mesh=mesh,
        in_specs=(rows,) * 5 + (P(None, ALL), P(ALL), P("dp", None, None), rows),
        out_specs=(rows,) * 6 + (P(None, ALL), P(ALL)),
        check_vma=False,
    )
```

```python
import functools

import jax
import jax.numpy as jnp
from jax import lax
from jax.experimental import pallas as pl
from jax.experimental.pallas import tpu as pltpu
from jax.sharding import PartitionSpec as P

H = 12
CL = 128


epsilon = 1e-06


def normalize(resid, norm_gain, norm_shift):
    average = jnp.mean(resid, axis=-1, keepdims=True)
    centred = resid - average
    spread = jnp.mean(centred * centred, axis=-1, keepdims=True)
    scaled = lax.rsqrt(spread + epsilon)
    normed = centred * scaled
    return (normed * norm_gain + norm_shift, normed, scaled)


def norm_back(grad_output, normed, scaled, norm_gain):
    grad_norm = grad_output * norm_gain
    first_term = jnp.mean(grad_norm, axis=-1, keepdims=True)
    second_term = jnp.mean(grad_norm * normed, axis=-1, keepdims=True)
    return scaled * (grad_norm - first_term - normed * second_term)


def exact_gelu(value):
    return jax.nn.gelu(value, approximate=False)


def order_table(sending):
    heads, rows_here = sending.shape
    columns = jnp.arange(rows_here, dtype=jnp.int32)[None, None, :]
    return (sending[:, :, None] == columns).astype(jnp.bfloat16)


def to_slots(source_rows, table):
    moved = jnp.einsum("hrs,skhe->rkhe", table, source_rows, preferred_element_type=jnp.float32)
    return moved.astype(jnp.bfloat16)


def to_tokens(source_rows, table):
    moved = jnp.einsum("hrs,rkhe->skhe", table, source_rows, preferred_element_type=jnp.float32)
    return moved.astype(jnp.bfloat16)


def cluster_scores(query_c, key_c, scale_factor):
    return (
        jnp.einsum("cahe,cbhe->hcab", query_c, key_c, preferred_element_type=jnp.float32)
        * scale_factor
    )


def shards(tokens, w_qkv, w_out, w_up, w_down, vectors, up_bias, cluster_route, upstream):
    lane_count = lax.axis_size("seq")
    lane_index = lax.axis_index("seq")
    wide_qkv, wide_out, wide_up, wide_down, wide_vectors, wide_bias = (
        lax.all_gather(w_qkv, ("dp", "seq"), axis=0, tiled=True),
        lax.all_gather(w_out, ("dp", "seq"), axis=0, tiled=True),
        lax.all_gather(w_up, ("dp", "seq"), axis=0, tiled=True),
        lax.all_gather(w_down, ("dp", "seq"), axis=0, tiled=True),
        lax.all_gather(vectors, ("dp", "seq"), axis=1, tiled=True),
        lax.all_gather(up_bias, ("dp", "seq"), axis=0, tiled=True),
    )
    rows_here = tokens.shape[0]
    model_width = tokens.shape[1]
    head_size = model_width // H
    portion = rows_here // lane_count
    clusters = rows_here // CL
    scale_factor = head_size ** (-0.5)
    vector_rows = wide_vectors.astype(jnp.float32)
    route_rows = cluster_route[0]
    by_target = lax.dynamic_slice_in_dim(route_rows, lane_index * rows_here, rows_here, 1)
    sending = jnp.swapaxes(by_target.reshape(H, lane_count, portion), 1, 2).reshape(H, rows_here)
    table = order_table(sending)
    projected = jnp.dot(tokens, wide_qkv, preferred_element_type=jnp.float32)
    shifts = jnp.concatenate(
        [vector_rows[0], jnp.zeros((model_width,), jnp.float32), vector_rows[1]]
    )
    projected = (projected + shifts).astype(jnp.bfloat16).reshape(rows_here, 3, H, head_size)
    outgoing = to_slots(projected, table)
    arrived = lax.all_to_all(
        outgoing.reshape(portion, lane_count, 3 * model_width),
        "seq",
        split_axis=1,
        concat_axis=1,
        tiled=True,
    )
    slot_qkv = arrived.reshape(clusters, CL, 3, H, head_size)
    query_c = slot_qkv[:, :, 0]
    key_c = slot_qkv[:, :, 1]
    value_c = slot_qkv[:, :, 2]
    scores = cluster_scores(query_c, key_c, scale_factor)
    row_peak = jnp.max(scores, axis=-1, keepdims=True)
    exponent = jnp.exp(scores - row_peak)
    row_total = jnp.sum(exponent, axis=-1, keepdims=True)
    soft_weights = exponent / row_total
    log_total = row_peak + jnp.log(row_total)
    heads_slot = jnp.einsum(
        "hcab,cbhe->cahe",
        soft_weights.astype(jnp.bfloat16),
        value_c,
        preferred_element_type=jnp.float32,
    ).astype(jnp.bfloat16)
    returned = lax.all_to_all(
        heads_slot.reshape(portion, lane_count, model_width),
        "seq",
        split_axis=1,
        concat_axis=1,
        tiled=True,
    )
    mixed_heads = to_tokens(returned.reshape(rows_here, 1, H, head_size), table).reshape(
        rows_here, model_width
    )
    attention = jnp.dot(mixed_heads, wide_out, preferred_element_type=jnp.float32) + vector_rows[2]
    first_norm, first_normed, first_scaled = normalize(
        tokens.astype(jnp.float32) + attention, vector_rows[4], vector_rows[5]
    )
    first_low = first_norm.astype(jnp.bfloat16)
    widened = jnp.dot(first_low, wide_up, preferred_element_type=jnp.float32) + wide_bias.astype(
        jnp.float32
    )
    activated, gelu_pull = jax.vjp(exact_gelu, widened)
    activated_low = activated.astype(jnp.bfloat16)
    narrowed = (
        jnp.dot(activated_low, wide_down, preferred_element_type=jnp.float32) + vector_rows[3]
    )
    output, second_normed, second_scaled = normalize(
        first_norm + narrowed, vector_rows[6], vector_rows[7]
    )
    back_qkv, back_out, back_up, back_down = (
        lax.all_gather(w_qkv, ("dp", "seq"), axis=0, tiled=True),
        lax.all_gather(w_out, ("dp", "seq"), axis=0, tiled=True),
        lax.all_gather(w_up, ("dp", "seq"), axis=0, tiled=True),
        lax.all_gather(w_down, ("dp", "seq"), axis=0, tiled=True),
    )
    grad_output = upstream.astype(jnp.float32)
    grad_gain_two = jnp.sum(grad_output * second_normed, axis=0)
    grad_shift_two = jnp.sum(grad_output, axis=0)
    grad_second = norm_back(grad_output, second_normed, second_scaled, vector_rows[6])
    grad_narrow = grad_second.astype(jnp.bfloat16)
    grad_down_w = jnp.einsum(
        "tf,td->fd", activated_low, grad_narrow, preferred_element_type=jnp.float32
    )
    grad_down_bias = jnp.sum(grad_narrow.astype(jnp.float32), axis=0)
    grad_active = jnp.einsum(
        "td,fd->tf", grad_narrow, back_down, preferred_element_type=jnp.float32
    )
    grad_wide = gelu_pull(grad_active)[0].astype(jnp.bfloat16)
    grad_up_w = jnp.einsum("td,tf->df", first_low, grad_wide, preferred_element_type=jnp.float32)
    grad_lift_bias = jnp.sum(grad_wide.astype(jnp.float32), axis=0)
    grad_first = grad_second + jnp.einsum(
        "tf,df->td", grad_wide, back_up, preferred_element_type=jnp.float32
    )
    grad_gain_one = jnp.sum(grad_first * first_normed, axis=0)
    grad_shift_one = jnp.sum(grad_first, axis=0)
    grad_resid = norm_back(grad_first, first_normed, first_scaled, vector_rows[4])
    grad_attn = grad_resid.astype(jnp.bfloat16)
    grad_out_w = jnp.einsum("td,te->de", mixed_heads, grad_attn, preferred_element_type=jnp.float32)
    grad_out_bias = jnp.sum(grad_attn.astype(jnp.float32), axis=0)
    grad_mixed = jnp.einsum(
        "te,de->td", grad_attn, back_out, preferred_element_type=jnp.float32
    ).astype(jnp.bfloat16)
    grad_sending = to_slots(grad_mixed.reshape(rows_here, 1, H, head_size), table)
    grad_slot = lax.all_to_all(
        grad_sending.reshape(portion, lane_count, model_width),
        "seq",
        split_axis=1,
        concat_axis=1,
        tiled=True,
    )
    grad_slot = grad_slot.reshape(clusters, CL, H, head_size)
    scores = cluster_scores(query_c, key_c, scale_factor)
    soft_weights = jnp.exp(scores - log_total)
    grad_soft = jnp.einsum(
        "cahe,cbhe->hcab", grad_slot, value_c, preferred_element_type=jnp.float32
    )
    inner_sum = jnp.sum(soft_weights * grad_soft, axis=-1, keepdims=True)
    grad_scores = (soft_weights * (grad_soft - inner_sum)).astype(jnp.bfloat16)
    grad_query = (
        jnp.einsum("hcab,cbhe->cahe", grad_scores, key_c, preferred_element_type=jnp.float32)
        * scale_factor
    )
    grad_key = (
        jnp.einsum("hcab,cahe->cbhe", grad_scores, query_c, preferred_element_type=jnp.float32)
        * scale_factor
    )
    grad_value = jnp.einsum(
        "hcab,cahe->cbhe",
        soft_weights.astype(jnp.bfloat16),
        grad_slot,
        preferred_element_type=jnp.float32,
    )
    grad_slots = jnp.stack([grad_query, grad_key, grad_value], axis=2).astype(jnp.bfloat16)
    came_back = lax.all_to_all(
        grad_slots.reshape(portion, lane_count, 3 * model_width),
        "seq",
        split_axis=1,
        concat_axis=1,
        tiled=True,
    )
    grad_proj = to_tokens(came_back.reshape(rows_here, 3, H, head_size), table).reshape(
        rows_here, 3 * model_width
    )
    grad_qkv_w = jnp.einsum("td,tf->df", tokens, grad_proj, preferred_element_type=jnp.float32)
    bias_sums = jnp.sum(grad_proj.astype(jnp.float32), axis=0).reshape(3, model_width)
    grad_tokens = (
        jnp.einsum("tf,df->td", grad_proj, back_qkv, preferred_element_type=jnp.float32)
        + grad_resid
    ).astype(jnp.bfloat16)
    grad_vector_rows = jnp.stack(
        [
            bias_sums[0],
            bias_sums[2],
            grad_out_bias,
            grad_down_bias,
            grad_gain_one,
            grad_shift_one,
            grad_gain_two,
            grad_shift_two,
        ]
    )
    shares = (
        lax.psum_scatter(grad_qkv_w, ("dp", "seq"), scatter_dimension=0, tiled=True),
        lax.psum_scatter(grad_out_w, ("dp", "seq"), scatter_dimension=0, tiled=True),
        lax.psum_scatter(grad_up_w, ("dp", "seq"), scatter_dimension=0, tiled=True),
        lax.psum_scatter(grad_down_w, ("dp", "seq"), scatter_dimension=0, tiled=True),
        lax.psum_scatter(grad_vector_rows, ("dp", "seq"), scatter_dimension=1, tiled=True),
        lax.psum_scatter(grad_lift_bias, ("dp", "seq"), scatter_dimension=0, tiled=True),
    )
    return (
        output.astype(jnp.bfloat16),
        grad_tokens,
        shares[0],
        shares[1],
        shares[2],
        shares[3],
        shares[4],
        shares[5],
    )


MESH = pl.DeviceIdType.MESH
NZ = 4
BLK = 128

class Links:
    def __init__(self, send_sems, recv_sems):
        self.send_sems, self.recv_sems, self.count, self.drains, self.key = send_sems, recv_sems, 0, {}, None
        self.dp, self.sq = lax.axis_index("dp"), lax.axis_index("seq")
        self.x, self.y = lax.rem(self.dp, 2), self.dp // 2
        self.core, self.z = lax.rem(self.sq, 2), self.sq // 2
        self.sib = self.sq + 1 - 2 * self.core
        self.dp_x = self.dp + 1 - 2 * self.x
        self.dp_y = self.dp + 2 - 4 * self.y

    def peers(self):
        return jnp.where(self.core == 0, self.dp_x, self.dp_y), jnp.where(self.core == 0, self.dp_y, self.dp_x)

    def new(self):
        self.count += 1
        return self.count - 1

    def copy(self, i, src, dst, dp, sq):
        return pltpu.make_async_remote_copy(
            src_ref=src, dst_ref=dst, send_sem=self.send_sems.at[i], recv_sem=self.recv_sems.at[i],
            device_id=(dp, sq), device_id_type=MESH)

    def enter(self, near=True, line=True):
        barrier = pltpu.get_barrier_semaphore()
        n = 0
        if near:
            for dp in (self.dp_x, self.dp_y):
                pl.semaphore_signal(barrier, inc=1, device_id=(dp, self.sq), device_id_type=MESH)
                n += 1
        if line:
            for j in range(1, 2 * NZ):
                pl.semaphore_signal(barrier, inc=1, device_id=(self.dp, lax.rem(self.sq + j, 2 * NZ)), device_id_type=MESH)
                n += 1
        pl.semaphore_wait(barrier, n)

    def go(self, *makers):
        for make in makers:
            make().start()
            self.add(lambda make=make: make().wait_send())

    def drain(self, keys=None):
        for key in list(self.drains) if keys is None else keys:
            for d in self.drains.pop(key, []):
                d()

    def add(self, d):
        self.drains.setdefault(self.key, []).append(d)

    def under(self, key, stages):
        def run(stage):
            before, self.key = self.key, key
            stage()
            self.key = before
        return [functools.partial(run, stage) for stage in stages]


def mult(v, m):
    return pl.multiple_of(v, m)


def gather(L, shard, full, half_buf, r, split):
    half = full.shape[1] // 2
    a, b = split
    big = 2 * r
    mine = pl.ds(mult(L.core * half, 128), half)
    other = pl.ds(mult((1 - L.core) * half, 128), half)
    cols_a = pl.ds(mult(L.core * half, 128), a)
    cols_b = pl.ds(mult(L.core * half + a, 128), b)
    chip = lambda z: pl.ds(mult((L.dp * NZ + z) * big, 16), big)
    quarter = lambda dp, n=1: pl.ds(mult(dp * NZ * big, 16), n * NZ * big)
    i0 = L.new()
    fr = [None] + [L.new() for _ in range(3)]
    fl = [None] + [L.new() for _ in range(3)]
    a1, b1, a2, a3, b2, b3, c0, c1, c2 = [L.new() for _ in range(9)]
    fa, fb = L.peers()
    opposite = 3 - L.dp
    first = lambda: L.copy(i0, shard.at[:, other], half_buf, L.dp, L.sib)

    def right(d, z0):
        return L.copy(fr[d], full.at[chip(z0), mine], full.at[chip(z0), mine], L.dp, L.sq + 2)

    def left(d, z0):
        return L.copy(fl[d], full.at[chip(z0), mine], full.at[chip(z0), mine], L.dp, L.sq - 2)

    def send_line(d):
        @pl.when((L.z >= d - 1) & (L.z < NZ - 1))
        def _():
            right(d, L.z - d + 1).start()

        @pl.when((L.z <= NZ - d) & (L.z > 0))
        def _():
            left(d, L.z + d - 1).start()

    def drain_line(d):
        @pl.when((L.z >= d - 1) & (L.z < NZ - 1))
        def _():
            right(d, L.z - d + 1).wait_send()

        @pl.when((L.z <= NZ - d) & (L.z > 0))
        def _():
            left(d, L.z + d - 1).wait_send()

    def recv_line(d):
        @pl.when(L.z >= d)
        def _():
            right(d, L.z - d).wait_recv()

        @pl.when(L.z + d <= NZ - 1)
        def _():
            left(d, L.z + d).wait_recv()

    def same(i, rows, cols, dp, sq):
        ref = full.at[rows, cols]
        return L.copy(i, ref, ref, dp, sq)

    def s0():
        L.go(first)

    def s1():
        first().wait_recv()
        own, got = shard[:, mine], half_buf[...]

        @pl.when(L.core == 0)
        def _():
            full[chip(L.z), mine] = jnp.concatenate([own, got], axis=0)

        @pl.when(L.core == 1)
        def _():
            full[chip(L.z), mine] = jnp.concatenate([got, own], axis=0)
        send_line(1)
        L.add(functools.partial(drain_line, 1))

    def s2():
        recv_line(1)
        send_line(2)
        L.add(functools.partial(drain_line, 2))

    def s3():
        recv_line(2)
        send_line(3)
        L.add(functools.partial(drain_line, 3))

    def s4():
        recv_line(3)
        q = lambda: quarter(L.dp)
        L.go(lambda: same(a1, q(), cols_a, fa, L.sq), lambda: same(b1, q(), cols_b, fb, L.sq),
             lambda: same(c0, q(), mine, L.dp, L.sib))

    def s5():
        same(a1, quarter(fa), cols_a, fa, L.sq).wait_recv()
        L.go(lambda: same(a2, quarter(L.dp), cols_a, fb, L.sq), lambda: same(a3, quarter(fa), cols_a, fb, L.sq))
        same(b1, quarter(fb), cols_b, fb, L.sq).wait_recv()
        L.go(lambda: same(b2, quarter(L.dp), cols_b, fa, L.sq), lambda: same(b3, quarter(fb), cols_b, fa, L.sq))

    def s6():
        same(a2, quarter(fb), cols_a, fb, L.sq).wait_recv()
        same(b2, quarter(fa), cols_b, fa, L.sq).wait_recv()
        L.go(lambda: same(c1, quarter(L.dp_x), mine, L.dp, L.sib))
        same(a3, quarter(opposite), cols_a, fb, L.sq).wait_recv()
        same(b3, quarter(opposite), cols_b, fa, L.sq).wait_recv()
        L.go(lambda: same(c2, quarter(2 * (1 - L.y), 2), mine, L.dp, L.sib))

    def s7():
        same(c0, quarter(L.dp), other, L.dp, L.sib).wait_recv()
        same(c1, quarter(L.dp_x), other, L.dp, L.sib).wait_recv()
        same(c2, quarter(2 * (1 - L.y), 2), other, L.dp, L.sib).wait_recv()
    return [s0, s1, s2, s3, s4, s5, s6, s7]


def spread(L, src, dst, local_sem, parts=1):
    ids = [[L.new() for _ in range(2 * NZ - 1)] for _ in range(parts)]
    n = BLK // parts
    rows = lambda s, i: pl.ds(mult(s * BLK + i * n, n), n)

    def keep(i):
        return pltpu.make_async_copy(src.at[rows(L.sq, i)], dst.at[rows(L.sq, i)], local_sem.at[i])

    def move(i, j, to, frm):
        return L.copy(ids[i][j - 1], src.at[rows(to, i)], dst.at[rows(frm, i)], L.dp, to)

    def begin(i=0):
        keep(i).start()
        for j in (1, 7, 2, 6, 3, 5, 4):
            L.go(lambda j=j: move(i, j, lax.rem(L.sq + j, 2 * NZ), L.sq))

    def finish():
        for i in range(parts):
            keep(i).wait()
            for j in range(1, 2 * NZ):
                move(i, j, L.sq, lax.rem(L.sq + 2 * NZ - j, 2 * NZ)).wait_recv()
    return begin, finish


def add_into(dst, rows0, cols, src, n):
    step = 192

    def one(i, _):
        here = pl.ds(mult(i * step, 16), step)
        there = pl.ds(mult(rows0 + i * step, 16), step)
        dst[there, cols] = dst[there, cols] + src[here, :]
        return 0
    lax.fori_loop(0, n // step, one, 0)


def landing(r, c, split):
    half, (a, b), big = c // 2, split, 2 * r
    return [(32 * r, half), (4 * big, a), (4 * big, a), (4 * big, b), (4 * big, b), (4 * big, a), (4 * big, b)]


def line_scratch(r, c):
    half, big = c // 2, 2 * r
    return [pltpu.VMEM((3, big, half), jnp.bfloat16)] * 2 + [pltpu.VMEM((2, r, half), jnp.float32), pltpu.VMEM((r, half), jnp.float32)]


def reduce_scratch(r, c, split):
    return [pltpu.VMEM(shape, jnp.bfloat16) for shape in landing(r, c, split)] + line_scratch(r, c)


N_REDUCE = 15
N_GATHER = 16
N_SCRATCH = 11
N_LINE = 4


def reduce(L, part, out, scratch, r, split):
    acc, a10, a11, b10, b11, a2, b2, from_l, from_r, fin, got = scratch
    half = part.shape[1] // 2
    a, b = split
    big = 2 * r
    mine = pl.ds(mult(L.core * half, 128), half)
    other = pl.ds(mult((1 - L.core) * half, 128), half)
    ca, cb = pl.ds(0, a), pl.ds(a, b)
    quarter = lambda dp, n=1: pl.ds(mult(dp * NZ * big, 16), n * NZ * big)
    chip = lambda z: pl.ds(mult((L.dp * NZ + z) * big, 16), big)
    i0, ia0, ia1, ib0, ib1, ia2, ib2, ifin = [L.new() for _ in range(8)]
    fb, fa = L.peers()
    opposite = 3 - L.dp
    ir = [None] + [L.new() for _ in range(3)]
    il = [L.new() for _ in range(3)]
    q = lambda dp: dp * NZ * big

    core_copy = lambda: L.copy(i0, part.at[:, other], acc, L.dp, L.sib)
    def part_copy(i, dp, cols, to, peer):
        return L.copy(i, acc.at[quarter(dp), cols], to, peer, L.sq)

    a_copies = [lambda: part_copy(ia0, opposite, ca, a10, fa), lambda: part_copy(ia1, fa, ca, a11, fa)]
    b_copies = [lambda: part_copy(ib0, opposite, cb, b10, fb), lambda: part_copy(ib1, fb, cb, b11, fb)]
    a2_copy = lambda: part_copy(ia2, fb, ca, a2, fb)
    b2_copy = lambda: part_copy(ib2, fa, cb, b2, fa)
    def s0():
        L.go(core_copy)

    def s1():
        core_copy().wait_recv()
        step = 192

        def one(i, _):
            here = pl.ds(mult(i * step, 16), step)
            acc[here, :] = acc[here, :] + part[here, mine]
            return 0
        lax.fori_loop(0, 32 * r // step, one, 0)
        L.go(a_copies[0], b_copies[0], a_copies[1], b_copies[1])

    def s2():
        a_copies[0]().wait_recv()
        add_into(acc, q(fb), ca, a10, 4 * big)
        L.go(a2_copy)
        b_copies[0]().wait_recv()
        add_into(acc, q(fa), cb, b10, 4 * big)
        L.go(b2_copy)
        a_copies[1]().wait_recv()
        add_into(acc, q(L.dp), ca, a11, 4 * big)
        b_copies[1]().wait_recv()
        add_into(acc, q(L.dp), cb, b11, 4 * big)

    def s3():
        a2_copy().wait_recv()
        add_into(acc, q(L.dp), ca, a2, 4 * big)
        b2_copy().wait_recv()
        add_into(acc, q(L.dp), cb, b2, 4 * big)

    full_cols = pl.ds(0, half)

    def hop_r(t, src):
        return L.copy(ir[t], src, from_l.at[t - 1], L.dp, L.sq + 2)

    def hop_l(t, src):
        return L.copy(il[t], src, from_r.at[t], L.dp, L.sq - 2)

    def merge(buf, k, t):
        buf[k] = (buf[k].astype(jnp.float32) + acc[chip(t), :].astype(jnp.float32)).astype(jnp.bfloat16)

    def line(s):
        @pl.when(L.z == s)
        def _():
            for t in range(NZ - 1, s, -1):
                if s == 0:
                    hop_r(t, acc.at[chip(t), full_cols]).start()
                else:
                    hop_r(t, from_l.at[t - 1]).wait_recv()
                    merge(from_l, t - 1, t)
                    hop_r(t, from_l.at[t - 1]).start()

        @pl.when(L.z == NZ - 1 - s)
        def _():
            for t in range(0, NZ - 1 - s):
                if s == 0:
                    hop_l(t, acc.at[chip(t), full_cols]).start()
                else:
                    hop_l(t, from_r.at[t]).wait_recv()
                    merge(from_r, t, t)
                    hop_l(t, from_r.at[t]).start()

        def drain():
            @pl.when(L.z == s)
            def _():
                for t in range(NZ - 1, s, -1):
                    hop_r(t, from_l.at[t - 1]).wait_send()

            @pl.when(L.z == NZ - 1 - s)
            def _():
                for t in range(0, NZ - 1 - s):
                    hop_l(t, from_r.at[t]).wait_send()
        L.add(drain)

    fin_copy = lambda: L.copy(ifin, fin.at[1 - L.core], got, L.dp, L.sib)

    def s7():
        for z in range(NZ):
            @pl.when(L.z == z)
            def _(z=z):
                total = acc[chip(z), :].astype(jnp.float32)
                if z > 0:
                    hop_r(z, from_l.at[z - 1]).wait_recv()
                    total = total + from_l[z - 1].astype(jnp.float32)
                if z < NZ - 1:
                    hop_l(z, from_r.at[z]).wait_recv()
                    total = total + from_r[z].astype(jnp.float32)
                fin[...] = total.reshape(2, r, half)
        L.go(fin_copy)

    def s8():
        out[:, mine] = fin[L.core]
        fin_copy().wait_recv()
        out[:, other] = got[...]
    return [s0, s1, s2, s3] + [functools.partial(line, s) for s in range(3)] + [s7, s8]


def one_hot(slots, rows):
    row = lax.broadcasted_iota(jnp.int32, (rows, slots.shape[1]), 0)
    return jnp.where(slots == row, 1.0, 0.0).astype(jnp.bfloat16)


def head_lanes(width):
    row = lax.broadcasted_iota(jnp.int32, (2 * BLK, width), 0)
    lane = lax.rem(lax.broadcasted_iota(jnp.int32, (2 * BLK, width), 1), 128)
    return (row < BLK) == (lane < 64)


def dot(a, b, ca, cb):
    return lax.dot_general(a, b, (((ca,), (cb,)), ((), ())), preferred_element_type=jnp.float32)


def bdot(a, b, ca, cb):
    return lax.dot_general(a, b, (((ca,), (cb,)), ((0,), (0,))), preferred_element_type=jnp.float32)


BATCH = 8


SIZES = {"qkv": (24, 2560, (640, 640)), "out": (24, 768, (256, 128)), "up": (24, 3072, (768, 768)), "down": (96, 768, (128, 256)),
         "qk": (24, 1536, (384, 384)), "v": (24, 1024, (256, 256))}
ALL = ("dp", "seq")
VM = pl.BlockSpec(memory_space=pltpu.VMEM)
BF = jnp.bfloat16
LIMIT = 60 * 2**20


def place_rows(route, perm, me):
    heads, n = 2 * perm.shape[0], 2 * NZ
    size = route.shape[0] * BLK // (heads * n)
    chunks = size // BLK
    base = me * BLK
    pers = [jnp.concatenate([route[pl.ds((h * n) * chunks + c, n, stride=chunks), :] for c in range(chunks)], axis=1)
            for h in range(heads)]
    head_row = jnp.concatenate([per[0:1] for per in pers] + [jnp.full((16 - heads, size), -1, jnp.int32)], axis=0)
    mine = (head_row >= base) & (head_row < base + BLK)
    flags = jnp.where(mine, 1.0, 0.0).astype(jnp.bfloat16)
    before = []
    for c in range(0, size, 128):
        row = lax.broadcasted_iota(jnp.int32, (size, 128), 0)
        col = lax.broadcasted_iota(jnp.int32, (size, 128), 1) + c
        before.append(dot(flags, jnp.where(row < col, 1.0, 0.0).astype(jnp.bfloat16), 1, 0))
    slot = jnp.where(mine, jnp.concatenate(before, axis=1).astype(jnp.int32), -1)
    for h in range(heads):
        per = pers[h]
        local = jnp.where((per >= base) & (per < base + BLK), per - base, 0).astype(jnp.float32).astype(jnp.bfloat16)
        pick = jnp.where(slot[h:h + 1, :] == lax.broadcasted_iota(jnp.int32, (BLK, size), 0), 1.0, 0.0).astype(jnp.bfloat16)
        perm[h // 2, :, pl.ds((h % 2) * BLK, BLK)] = dot(local, pick, 1, 1).astype(jnp.int32)


def front_pair(scale, qkv, width, perm, mixed, pool, head_ref, p, par):
    nblk = qkv.shape[0] // BLK
    share = BLK // nblk
    keep = head_lanes(384)
    cols = pl.ds(mult(par * 384, 128), 384)
    lane = lambda o: pl.ds(mult(par * 384 + o, 128), 128)
    col = lambda o: pl.ds(mult(p * 128 + o * width, 128), 128)
    half = nblk * BLK
    for k in range(nblk):
        here = pl.ds(k * BLK, BLK)
        packed = jnp.concatenate([qkv[here, col(0)], qkv[here, col(1)], qkv[here, col(2)]], axis=1)
        table = one_hot(perm[p, k:k + 1, :], BLK)
        moved = jnp.where(keep, dot(table, packed, 0, 0), 0.0).astype(jnp.bfloat16)
        for c in range(2 * nblk):
            pool[pl.ds(c * BLK + k * share, share), cols] = moved[c * share:(c + 1) * share]
    for h in range(2):
        rows = pl.ds(h * half, half)
        q, kk, v = [pool[rows, lane(o)].reshape(nblk, BLK, 128) for o in (0, 128, 256)]
        scores = bdot(q, kk, 2, 2) * scale
        e = jnp.exp(scores - jnp.max(scores, axis=-1, keepdims=True))
        probs = (e * (1.0 / jnp.sum(e, axis=-1, keepdims=True))).astype(jnp.bfloat16)
        pool[pl.ds(2 * half, half), pl.ds(mult((2 * par + h) * 128, 128), 128)] = probs.reshape(half, BLK)
        head_ref[rows, :] = bdot(probs, v, 2, 1).reshape(half, BLK).astype(jnp.bfloat16)
    for k in range(nblk):
        table = one_hot(perm[p, k:k + 1, :], BLK)
        back = jnp.concatenate([head_ref[pl.ds(c * BLK + k * share, share), :] for c in range(2 * nblk)], axis=0)
        mixed[pl.ds(k * BLK, BLK), col(0)] = dot(table, back, 1, 0).astype(jnp.bfloat16)


def loop(n, body, hooks=()):
    def one(i, _):
        body(i)
        for at, stage in hooks:
            pl.when(i == at)(stage)
        return 0
    lax.fori_loop(0, n, one, 0)


def moments(v):
    mean = jnp.mean(v, axis=-1, keepdims=True)
    centred = v - mean
    inv = lax.rsqrt(jnp.mean(centred * centred, axis=-1, keepdims=True) + epsilon)
    return centred * inv, inv


TB = 256
FB = 768


def layer_kernel(scale, w_shard, out_shard, up_shard, down_shard, vec_shard, ub_shard, route, x_rows, up_rows,
                 x_home, w_home, slots, probs, out_rows, gx_rows, r_qkv, r_aux, r_out, r_up, r_down,
                 w_out, w_up, w_down, act, gp, x, mixed, n1, s1, low, up, outb, dn, gd, head_ref, vec, ub, auxf,
                 bq, bo, bu, bd, qkv_shard, perm, d_res, s2, sums, ubsum, ra, rb, *rest):
    own = [rest[i:i + N_SCRATCH] for i in (0, N_SCRATCH)]
    late = rest[2 * N_SCRATCH:2 * N_SCRATCH + 3 + 3 * N_LINE]
    ss, rs, ls, cs = rest[2 * N_SCRATCH + 3 + 3 * N_LINE:]
    rows_here, width = x.shape
    ff = w_up.shape[1]
    pairs = perm.shape[0]
    w = gp.at[pl.ds(0, width), pl.ds(0, qkv_shard.shape[1])]
    da = up
    L = Links(ss, rs)
    r = w_shard.shape[0]
    nv, step = vec_shard.shape[0], ub_shard.shape[1]
    qkv_shard[:, 0:3 * width] = w_shard[...]
    auxf[...] = jnp.zeros_like(auxf)
    auxf[0:nv, 0:r] = vec_shard[...].astype(jnp.float32)
    qkv_shard[:, 3 * width:3 * width + 128] = auxf[0:128, :].T[0:r, :].astype(jnp.bfloat16)
    auxf[0:nv, :] = jnp.zeros((nv, 128), jnp.float32)
    auxf[0:1, 0:step] = ub_shard[...].astype(jnp.float32)
    qkv_shard[:, 3 * width + 128:3 * width + 256] = auxf[0:r, :].astype(jnp.bfloat16)
    L.enter()
    Q = L.under("qkv", gather(L, qkv_shard, w, bq, *SIZES["qkv"][::2]))
    O = L.under("out", gather(L, out_shard, w_out, bo, *SIZES["out"][::2]))
    U = L.under("up", gather(L, up_shard, w_up, bu, *SIZES["up"][::2]))
    D = L.under("down", gather(L, down_shard, w_down, bd, *SIZES["down"][::2]))
    x_begin, x_finish = spread(L, x_rows, x, ls.at[0])
    up_begin, up_finish = spread(L, up_rows, up, ls.at[1])
    out_begin, out_finish = spread(L, outb, out_rows, ls.at[2])
    gx_begin, gx_finish = spread(L, dn, gx_rows, ls.at[3], PARTS)
    g_up, part = act.at[pl.ds(0, width), :], act.at[pl.ds(0, width), pl.ds(0, SIZES["qkv"][1])]
    spare = [act.at[pl.ds(width, r * 8), pl.ds(i * width, width)] for i in range(4)]
    n_qk, n_v = SIZES["qk"][1], SIZES["v"][1]

    def in_w_up(at, size, pieces):
        q = size // 4
        return [w_up.at[:, pl.ds(at, size // 2)]] + [w_up.at[pl.ds(i * r * 8, r * 8), pl.ds(pieces + j * q, q)]
                                                    for j in range(2) for i in range(3)]
    spare_qk = in_w_up(0, n_qk, (n_qk + n_v) // 2)
    spare_v = in_w_up(n_qk // 2, n_v, (n_qk + n_v) // 2 + n_qk // 2)
    R = reduce(L, gd, r_down, own[0], *SIZES["down"][::2])
    R = L.under("sum", R[:1]) + R[1:]
    SO = reduce(L, w_out, r_out, own[1], *SIZES["out"][::2])
    SU = reduce(L, g_up, r_up, [late[0], *spare, *late[1:3 + N_LINE]], *SIZES["up"][::2])
    SU = L.under("sum_up", SU[:1]) + SU[1:]
    lines = late[3 + N_LINE:]
    SK = reduce(L, act.at[pl.ds(0, width), pl.ds(0, n_qk)], ra, [*spare_qk, *lines[:N_LINE]], *SIZES["qk"][::2])
    SV = reduce(L, act.at[pl.ds(0, width), pl.ds(n_qk, n_v)], rb, [*spare_v, *lines[N_LINE:]], *SIZES["v"][::2])
    plan = PLAN(Q, O, U, D, x_begin, up_begin, R)
    plan.update(LATE(R, SO, SU, SK, SV, [functools.partial(gx_begin, i) for i in range(PARTS)]))
    row = lambda i: vec[i:i + 1, :]

    def run(stages):
        for stage in stages:
            stage()

    run(plan["start"])
    sums[...] = jnp.zeros_like(sums)
    ubsum[...] = jnp.zeros_like(ubsum)
    place_rows(route, perm, L.sq)
    run(plan["placed"])
    vec[...] = w[:, 2304:2432].astype(jnp.float32).T[0:8, :]
    auxf[...] = w[:, 2432:2560].astype(jnp.float32)
    for i in range(ff // step):
        ub[:, i * step:(i + 1) * step] = auxf[i * r:i * r + 1, 0:step]
    w_flush = pltpu.make_async_copy(w, w_home, cs.at[0])
    w_flush.start()
    run(plan["weights"])
    x_finish()
    x_flush = pltpu.make_async_copy(x, x_home, cs.at[1])
    x_flush.start()

    def project(m):
        here = pl.ds(mult(m * TB, TB), TB)
        for j in range(3):
            c = pl.ds(j * width, width)
            r = dot(x[here, :], w[:, c], 1, 0)
            if j != 1:
                r = r + row(j // 2)
            act[here, c] = r.astype(jnp.bfloat16)

    loop(rows_here // TB, project, plan["project"])

    def kept(p, par):
        half = rows_here
        return [pltpu.make_async_copy(gd.at[pl.ds(0, 2 * half), pl.ds(mult(par * 384, 128), 384)], slots.at[p], cs.at[2 + 3 * par])] + [
            pltpu.make_async_copy(gd.at[pl.ds(2 * half, half), pl.ds(mult((2 * par + h) * 128, 128), 128)], probs.at[p, h],
                                  cs.at[3 + 3 * par + h]) for h in range(2)]

    def back_in(p, par):
        half = rows_here
        return [pltpu.make_async_copy(slots.at[p], w_down.at[pl.ds(0, 2 * half), pl.ds(mult(par * 384, 128), 384)], cs.at[2 + 3 * par])] + [
            pltpu.make_async_copy(probs.at[p, h], w_down.at[pl.ds(2 * half, half), pl.ds(mult((2 * par + h) * 128, 128), 128)],
                                  cs.at[3 + 3 * par + h]) for h in range(2)]

    def attend(p):
        par = lax.rem(p, 2)

        @pl.when(p >= 2)
        def _():
            for c in kept(p - 2, par):
                c.wait()
        front_pair(scale, act, width, perm, mixed, gd, head_ref, p, par)
        for c in kept(p, par):
            c.start()

    loop(pairs, attend, plan["attend"])
    w_flush.wait()
    L.drain(["qkv", "out"])

    def first_half(m):
        here = pl.ds(mult(m * TB, TB), TB)
        r1 = x[here, :].astype(jnp.float32) + dot(mixed[here, :], w_out[...], 1, 0) + row(2)
        norm, inv = moments(r1)
        n1[here, :] = norm
        s1[here, :] = inv
        lo = (norm * row(4) + row(5)).astype(jnp.bfloat16)
        low[here, :] = lo
        for f in range(0, ff, FB):
            c = pl.ds(f, FB)
            wide = dot(lo, w_up[:, c], 1, 0) + ub[:, c]
            cdf = 0.5 + 0.5 * lax.erf(wide * 0.7071067811865476)
            act[here, c] = (wide * cdf).astype(jnp.bfloat16)
            gp[here, c] = (cdf + wide * (0.3989422804014327 * jnp.exp(-0.5 * wide * wide))).astype(jnp.bfloat16)

    loop(rows_here // TB, first_half, plan["first"])
    run(plan["firsts"])
    for p in range(pairs - 2, pairs):
        for c in kept(p, p % 2):
            c.wait()
    x_flush.wait()

    def second(m):
        here = pl.ds(mult(m * TB, TB), TB)
        first = n1[here, :] * row(4) + row(5)
        r2 = first + dot(act[here, :], w_down[...], 1, 0) + row(3)
        n2, inv = moments(r2)
        outb[here, :] = (n2 * row(6) + row(7)).astype(jnp.bfloat16)
        d_res[here, :] = n2
        s2[here, :] = inv

    loop(rows_here // TB, second)
    out_begin()
    up_finish()

    def second_back(m):
        here = pl.ds(mult(m * TB, TB), TB)
        n2 = d_res[here, :]
        g = up[here, :].astype(jnp.float32)
        sums[4:5, :] += jnp.sum(g * n2, axis=0, keepdims=True)
        sums[5:6, :] += jnp.sum(g, axis=0, keepdims=True)
        d = norm_back(g, n2, s2[here, :], row(6))
        d_res[here, :] = d
        lo = d.astype(jnp.bfloat16)
        dn[here, :] = lo
        sums[1:2, :] += jnp.sum(lo.astype(jnp.float32), axis=0, keepdims=True)

    loop(rows_here // TB, second_back)

    def grad_down(i):
        c = pl.ds(mult(i * FB, FB), FB)
        gd[c, :] = dot(act[:, c], dn[...], 0, 0).astype(jnp.bfloat16)

    loop(ff // FB, grad_down)
    R[0]()

    def third(m):
        here = pl.ds(mult(m * TB, TB), TB)
        total = d_res[here, :]
        lo = dn[here, :]
        for f in range(0, ff, FB):
            c = pl.ds(f, FB)
            dw = (dot(lo, w_down[c, :], 1, 1) * gp[here, c].astype(jnp.float32)).astype(jnp.bfloat16)
            gp[here, c] = dw
            ubsum[0:1, c] += jnp.sum(dw.astype(jnp.float32), axis=0, keepdims=True)
            total = total + dot(dw, w_up[:, c], 1, 1)
        norm = n1[here, :]
        sums[2:3, :] += jnp.sum(total * norm, axis=0, keepdims=True)
        sums[3:4, :] += jnp.sum(total, axis=0, keepdims=True)
        d = norm_back(total, norm, s1[here, :], row(4))
        d_res[here, :] = d
        lo = d.astype(jnp.bfloat16)
        da[here, :] = lo
        sums[0:1, :] += jnp.sum(lo.astype(jnp.float32), axis=0, keepdims=True)
        x[here, :] = dot(lo, w_out[...], 1, 1).astype(jnp.bfloat16)

    loop(rows_here // TB, third, plan["third"])
    L.drain(["down"])
    for p in range(2):
        for c in back_in(p, p):
            c.start()

    def grad_up(i):
        c = pl.ds(mult(i * FB, FB), FB)
        act[pl.ds(0, width), c] = dot(low[...], gp[:, c], 0, 0).astype(jnp.bfloat16)

    loop(ff // FB, grad_up, plan["grad_up"])
    L.drain(["up"])
    run(plan["up_ready"])
    w_out[...] = dot(mixed[...], da[...], 0, 0).astype(jnp.bfloat16)
    run(plan["out_ready"])
    L.drain(["sum"])
    reload = [pltpu.make_async_copy(w_home.at[:, pl.ds(j * width, width)], gd.at[pl.ds(j * width, width), :], cs.at[10 + j])
              for j in range(3)]
    for c in reload:
        c.start()

    def back(p):
        par = lax.rem(p, 2)
        for c in back_in(p, par):
            c.wait()
        back_pair(scale, x, perm, w_down, head_ref, gp, sums, p, par)

        @pl.when(p < pairs - 2)
        def _():
            for c in back_in(p + 2, par):
                c.start()

    loop(pairs, back, plan["back"])
    x_again = pltpu.make_async_copy(x_home, x, cs.at[0])
    x_again.start()
    for c in reload:
        c.wait()

    def grad_x(m):
        here = pl.ds(mult(m * TB, TB), TB)
        total = d_res[here, :]
        for j in range(3):
            total = total + dot(gp[here, pl.ds(j * width, width)], gd[pl.ds(j * width, width), :], 1, 1)
        dn[here, :] = total.astype(jnp.bfloat16)

    loop(rows_here // TB, grad_x)
    run(plan["x_ready"])
    x_again.wait()
    L.drain(["sum_up"])

    def grad_qkv(i):
        c = pl.ds(mult(i * FB, FB), FB)
        part[:, c] = dot(x[...], gp[:, c], 0, 0).astype(jnp.bfloat16)

    loop(3 * width // FB, grad_qkv, plan["qkv"])
    d_res[0:BLK, :] = jnp.zeros((BLK, width), jnp.float32)
    d_res[0:2, :] = sums[6:8, :]
    d_res[2:8, :] = sums[0:6, :]
    part[:, 3 * width:3 * width + 128] = d_res[0:BLK, :].T.astype(jnp.bfloat16)
    auxf[...] = jnp.zeros_like(auxf)
    for i in range(ff // step):
        auxf[i * r:i * r + 1, 0:step] = ubsum[0:1, i * step:(i + 1) * step]
    part[:, 3 * width + 128:3 * width + 256] = auxf[...].astype(jnp.bfloat16)
    run(plan["end"])
    r_qkv[:, 0:n_qk] = ra[...]
    r_qkv[:, n_qk:3 * width] = rb[:, 0:3 * width - n_qk]
    r_aux[...] = rb[:, 3 * width - n_qk:n_v]
    out_finish()
    gx_finish()
    L.drain()


def PLAN(Q, O, U, D, x_begin, up_begin, R):
    return {
        "start": [Q[0],O[0],U[0],D[0],Q[1],O[1],U[1],Q[2],O[2],U[2],Q[3],O[3],U[3],Q[4],x_begin,D[1],Q[5],O[4],U[4]],
        "placed": [Q[6],Q[7]],
        "weights": [O[5],U[5]],
        "project": [(1,D[2])],
        "attend": [(0,D[3]),(0,up_begin),(1,O[6]),(1,U[6]),(3,O[7]),(3,U[7]),(3,D[4])],
        "first": [(0,D[5]),(3,D[6])],
        "firsts": [D[7]],
    }


def LATE(R, O, U, K, V, G):
    return {
        "third": [(0, R[1])],
        "grad_up": [],
        "up_ready": [R[2], U[0]],
        "out_ready": [O[0]],
        "back": [(0, U[1]), (1, R[3]), (1, R[4]), (2, O[1]), (3, R[5]), (4, R[6]), (5, R[7])],
        "x_ready": [G[0], G[1], U[2], O[2]],
        "qkv": [(1, K[0])],
        "end": [V[0], R[8], U[3], U[4], G[2], K[1], V[1], O[3], O[4], U[5], G[3], K[2], V[2], U[6], O[5], K[3], K[4], O[6],
                V[3], V[4], K[5], U[7], O[7], V[5], K[6], V[6], K[7], V[7], U[8], O[8], K[8], V[8]],
    }


PARTS = 4


def layer_call(scale, pairs, w_qkv, w_out, w_up, w_down, vectors, up_bias, route, tokens, upstream):
    rows_here, width = tokens.shape
    ff = w_up.shape[1]
    r, cols, split = SIZES["down"]
    wq = SIZES["qkv"][1]
    count = 4 * N_GATHER + 5 * N_REDUCE + 7 * (3 + PARTS)
    f32 = lambda *s: jax.ShapeDtypeStruct(s, jnp.float32)
    bf = lambda *s: jax.ShapeDtypeStruct(s, BF)
    vbf = lambda *s: pltpu.VMEM(s, BF)
    vf = lambda *s: pltpu.VMEM(s, jnp.float32)
    hbm = pl.BlockSpec(memory_space=pl.ANY)
    ru = landing(*SIZES["up"])
    rq = SIZES["qkv"][0]
    return pl.pallas_call(
        functools.partial(layer_kernel, scale),
        out_shape=[bf(rows_here, width), bf(width, wq), bf(pairs, 2 * rows_here, 384), bf(pairs, 2, rows_here, BLK),
                   bf(rows_here, width), bf(rows_here, width), f32(rq, 3 * width), f32(rq, 256), f32(*SIZES["out"][:2]),
                   f32(*SIZES["up"][:2]), f32(r, cols)],
        in_specs=[VM] * 7 + [hbm] * 2,
        out_specs=[hbm] * 6 + [VM] * 5,
        scratch_shapes=[vbf(width, width), vbf(width, ff), vbf(ff, width), vbf(rows_here, ff), vbf(rows_here, ff),
                        vbf(rows_here, width), vbf(rows_here, width), vf(rows_here, width), vf(rows_here, 1)]
        + [vbf(rows_here, width)] * 4
        + [vbf(ff, width), vbf(2 * rows_here, BLK), vf(8, width), vf(1, ff), vf(width, BLK)]
        + [vbf(SIZES[n][0], SIZES[n][1] // 2) for n in ("qkv", "out", "up", "down")]
        + [vbf(rq, wq), pltpu.VMEM((pairs, 2 * NZ, 2 * BLK), jnp.int32), vf(rows_here, width), vf(rows_here, 1), vf(8, width),
           vf(8, ff), vf(rq, SIZES["qk"][1]), vf(rq, SIZES["v"][1])]
        + reduce_scratch(r, cols, split) + reduce_scratch(*SIZES["out"])
        + [vbf(*ru[0]), vbf(*ru[5]), vbf(*ru[6])] + line_scratch(*SIZES["up"][:2])
        + line_scratch(*SIZES["qk"][:2]) + line_scratch(*SIZES["v"][:2])
        + [pltpu.SemaphoreType.DMA((count,)), pltpu.SemaphoreType.DMA((count,)), pltpu.SemaphoreType.DMA((4, PARTS)),
           pltpu.SemaphoreType.DMA((13,))],
        compiler_params=pltpu.CompilerParams(collective_id=0, has_side_effects=True, vmem_limit_bytes=62 * 2**20),
    )(w_qkv, w_out, w_up, w_down, vectors, up_bias, route, tokens, upstream)


def back_pair(scale, dm, perm, pool, up_ref, gp, sums, p, par):
    nblk = dm.shape[0] // BLK
    share = BLK // nblk
    half = nblk * BLK
    width = dm.shape[1]
    keep = head_lanes(128)
    lane = lambda o: pl.ds(mult(par * 384 + o, 128), 128)
    col = lambda o: pl.ds(mult(p * 128 + o * width, 128), 128)
    for k in range(nblk):
        table = one_hot(perm[p, k:k + 1, :], BLK)
        moved = jnp.where(keep, dot(table, dm[pl.ds(k * BLK, BLK), col(0)], 0, 0), 0.0).astype(jnp.bfloat16)
        for c in range(2 * nblk):
            up_ref[pl.ds(c * BLK + k * share, share), :] = moved[c * share:(c + 1) * share]
    for h in range(2):
        rows = pl.ds(h * half, half)
        q, kk, v = [pool[rows, lane(o)].reshape(nblk, BLK, 128) for o in (0, 128, 256)]
        probs = pool[pl.ds(2 * half, half), pl.ds(mult((2 * par + h) * 128, 128), 128)].reshape(nblk, BLK, BLK)
        up = up_ref[rows, :].reshape(nblk, BLK, 128)
        dprobs = bdot(up, v, 2, 2)
        p32 = probs.astype(jnp.float32)
        pd = p32 * dprobs
        dscores = (pd - p32 * jnp.sum(pd, axis=-1, keepdims=True)).astype(jnp.bfloat16)
        parts = (bdot(dscores, kk, 2, 1) * scale, bdot(dscores, q, 1, 1) * scale, bdot(probs, up, 1, 1))
        for j, g in enumerate(parts):
            gp[:, pl.ds(3 * width + h * 384 + j * 128, 128)] = g.reshape(half, 128).astype(jnp.bfloat16)
    total = jnp.zeros((1, 384), jnp.float32)
    for k in range(nblk):
        table = one_hot(perm[p, k:k + 1, :], BLK)
        back = jnp.concatenate(
            [gp[pl.ds(c * BLK + k * share, share), pl.ds(3 * width + h * 384, 384)] for h in range(2) for c in range(nblk)], axis=0)
        moved = dot(table, back, 1, 0)
        total = total + jnp.sum(moved, axis=0, keepdims=True)
        for j in range(3):
            gp[pl.ds(k * BLK, BLK), col(j)] = moved[:, j * 128:(j + 1) * 128].astype(jnp.bfloat16)
    sums[6:7, col(0)] = total[:, 0:128]
    sums[7:8, col(0)] = total[:, 256:384]


def settle_kernel(n, *refs):
    ins, aux, outs, (gv, gb), bufs, sem = refs[:n], refs[n], refs[n + 1:2 * n + 1], refs[2 * n + 1:2 * n + 3], refs[2 * n + 3:-1], refs[-1]
    loads = [pltpu.make_async_copy(a, b, sem.at[0, i]) for i, (a, b) in enumerate(zip(ins, bufs))]
    stores = [pltpu.make_async_copy(a, b, sem.at[1, i]) for i, (a, b) in enumerate(zip(bufs, outs))]
    for c in loads:
        c.start()
    gv[...] = aux[:, 0:128].T[0:gv.shape[0], :]
    gb[...] = aux[0:1, 128:128 + gb.shape[1]]
    for c, d in zip(loads, stores):
        c.wait()
        d.start()
    for d in stores:
        d.wait()


def settle(arrays, aux, n_vec, n_bias):
    hbm = pl.BlockSpec(memory_space=pl.ANY)
    like = lambda a: jax.ShapeDtypeStruct(a.shape, a.dtype)
    f32 = lambda *s: jax.ShapeDtypeStruct(s, jnp.float32)
    return pl.pallas_call(
        functools.partial(settle_kernel, len(arrays)), out_shape=[like(a) for a in arrays] + [f32(n_vec, aux.shape[0]), f32(1, n_bias)],
        in_specs=[hbm] * len(arrays) + [VM], out_specs=[hbm] * len(arrays) + [VM] * 2,
        scratch_shapes=[pltpu.VMEM(a.shape, a.dtype) for a in arrays] + [pltpu.SemaphoreType.DMA((2, len(arrays)))],
        compiler_params=pltpu.CompilerParams(vmem_limit_bytes=LIMIT),
    )(*arrays, aux)


def homes(tokens, w_qkv, w_out, w_up, w_down, vectors, up_bias, cluster_route, upstream):
    pairs = H // 2
    scale = (tokens.shape[1] // H) ** -0.5
    step = up_bias.shape[0]
    out_rows, gx_rows, r_qkv, r_aux, r_out, r_up, r_down = layer_call(
        scale, pairs, w_qkv, w_out, w_up, w_down, vectors, up_bias[None], cluster_route.reshape(-1, BLK), tokens, upstream)[4:]
    gx, out, g_qkv, g_up, g_down, g_out, g_vec, g_bias = settle(
        [gx_rows, out_rows, r_qkv, r_up, r_down, r_out], r_aux, vectors.shape[0], step)
    return out, gx, g_qkv, g_out, g_up, g_down, g_vec, g_bias[0]


def solution(mesh):
    small = dict(mesh.shape) == {"dp": 4, "seq": 2 * NZ}
    rows = P(ALL, None)
    return jax.shard_map(
        homes if small else shards, mesh=mesh,
        in_specs=(rows,) * 5 + (P(None, ALL), P(ALL), P("dp", None, None), rows),
        out_specs=(rows,) * 6 + (P(None, ALL), P(ALL)),
        check_vma=False,
    )
```
